512 devices in a mesh: depth: 8 (over x, z_lo), row: 8 (over y), col: 8 (over z_hi, core).
Axes of the slice: x: 4, y: 8, z: 8 (z_hi: 4, z_lo: 2; z = z_hi * 2 + z_lo), core: 2. Of those that a mesh axis runs over, the one named last changes fastest.
Arguments:
- half_slabs: bfloat16 [2, 4000, 8192], P(None, 'depth', ('row', 'col')), may hold values from -6 to 6
- virtuals: bfloat16 [4000, 3456], P('col', 'depth'), may hold values from -0.015625 to 0.015625
- occupied_energy: float32 [2], replicated, may hold values from -2 to -0.3
- virtual_energy: float32 [3456], P('depth'), may hold values from 0.1 to 3
- frequency: float32 [1], replicated, may hold values from 0.2 to 2
Outputs:
- gram_block: float32 [8192, 8192], P('row', 'col')
The draws below stay inside these ranges and needn't reach their ends.
All inputs are finite; a program needn't handle non-finite values.
Results may differ from the reference program's by a relative error of at most 0.003.
Values may be sent and summed in bfloat16 or wider, within the bound.
A program may use at most 64 MiB of HBM per device.

```python
import math
import jax
import jax.numpy as jnp

NBAS = 4000
NVIR = 3456
NAUX = 8192
OCC = 2


def block_levels(key, extent, shards, least, largest):
    loudness, own = 1.0, jax.random.fold_in(key, 6)
    for axis_at, blocks in shards:
        heights = jnp.exp(jax.random.uniform(jax.random.fold_in(own, axis_at), (blocks,), jnp.float32, least / len(shards), largest / len(shards)))
        loudness = loudness * jnp.repeat(heights, extent[axis_at] // blocks).reshape([-1 if axis == axis_at else 1 for axis in range(len(extent))])
    return loudness


def bell_draw(own_key, dims, spread, limit, shards=(), held_as=jnp.bfloat16):
    loudness = block_levels(own_key, dims, shards, -0.22, 0.18) if shards else 1.0
    values = jax.random.normal(own_key, dims, jnp.float32) * spread * loudness
    return jnp.minimum(jnp.maximum(values, -limit), limit).astype(held_as)


def setup_inputs(seed: int = 0) -> dict:
    key_of = jax.random.split(jax.random.key(seed), 6)
    return {
        "half_slabs": bell_draw(key_of[0], (OCC, NBAS, NAUX), 1.0, 6.0, ((1, 8), (2, 64))),
        "virtuals": bell_draw(key_of[1], (NBAS, NVIR), (NBAS * 32) ** -0.5, 0.015625, ((0, 8), (1, 8))),
        "occupied_energy": jnp.clip(jax.random.uniform(key_of[2], (OCC,), jnp.float32, -2.0, -0.3), -2.0, -0.3),
        "virtual_energy": jnp.clip(0.1 + 2.9 * jax.random.uniform(key_of[3], (NVIR,), jnp.float32) ** block_levels(key_of[3], (NVIR,), ((0, 8),), -0.2, 0.2), 0.1, 3.0),
        "frequency": jnp.clip(jnp.exp(jax.random.uniform(key_of[4], (1,), jnp.float32, math.log(0.2), math.log(2.0))), 0.2, 2.0),
    }


def reference(half_slabs, virtuals, occupied_energy, virtual_energy, frequency):
    excitation = virtual_energy[None, :] - occupied_energy[:, None]
    weight = 4.0 * excitation / (excitation * excitation + frequency[0] * frequency[0])
    blocks = []
    for orbital in range(OCC):
        product = jnp.dot(virtuals.T, half_slabs[orbital], preferred_element_type=jnp.float32)
        blocks.append(product.astype(jnp.bfloat16))
    coupling = jnp.stack(blocks)
    weighted = (weight[:, :, None] * coupling.astype(jnp.float32)).astype(jnp.bfloat16)
    weighted_rows = weighted.reshape(OCC * NVIR, NAUX)
    plain_rows = coupling.reshape(OCC * NVIR, NAUX)
    return jnp.dot(weighted_rows.T, plain_rows, preferred_element_type=jnp.float32)
```

```python
import jax
import jax.numpy as jnp
from jax import lax
from jax.experimental import pallas as pl
from jax.experimental.pallas import tpu as pltpu
from jax.sharding import PartitionSpec as P

MESH = pl.DeviceIdType.MESH
BF = jnp.bfloat16
F32 = jnp.float32
RING = 8
LANES = 128


class Links:
    def __init__(self, send_sems, recv_sems):
        self.send_sems, self.recv_sems, self.copies = send_sems, recv_sems, []

    def plan(self, src, dst, **target):
        at = len(self.copies)
        copy = pltpu.make_async_remote_copy(
            src_ref=src,
            dst_ref=dst,
            send_sem=self.send_sems.at[at],
            recv_sem=self.recv_sems.at[at],
            device_id=target,
            device_id_type=MESH,
        )
        self.copies.append(copy)
        return copy

    def send(self, src, dst, **target):
        copy = self.plan(src, dst, **target)
        copy.start()
        return copy

    def finish(self):
        for copy in self.copies:
            copy.wait_send()


def around(me):
    up, down, far = lax.rem(me + 2, RING), lax.rem(me + 6, RING), lax.rem(me + 4, RING)
    return up, down, far, me + 1 - 2 * lax.rem(me, 2)


def other(at):
    return at + 1 - 2 * lax.rem(at, 2)


def gather_kernel(
    slabs_ref, virt_ref, vir_energy_ref, occ_ref, freq_ref, out_ref,
    slab_in, virt_in, energy_in, occ_in, freq_in, vpad, vq, hs, acc, rp, qp, wrow, wcol, wl,
    a_raw, a_land, a_keep, a_own, a_sib, a_last,
    b_terms, b_raw, b_land, b_keep, b_own, b_give, b_take, red,
    local_sems, send_sems, recv_sems,
):
    d, r, c = lax.axis_index("depth"), lax.axis_index("row"), lax.axis_index("col")
    d_up, d_down, d_far, d_sib = around(d)
    c_up, c_down, c_far, c_sib = around(c)
    r_up, r_down = lax.rem(r + 1, RING), lax.rem(r + 7, RING)
    links = Links(send_sems, recv_sems)
    send = links.send

    loads = [
        pltpu.make_async_copy(src, dst, local_sems.at[at])
        for at, (src, dst) in enumerate(
            (
                (virt_ref, virt_in), (slabs_ref, slab_in), (vir_energy_ref, energy_in),
                (occ_ref, occ_in), (freq_ref, freq_in),
            )
        )
    ]
    for load in loads:
        load.start()
    barrier = pltpu.get_barrier_semaphore()
    partners = [{"depth": d_up}, {"depth": d_down}, {"depth": d_sib}, {"row": r_up}, {"row": r_down}]
    partners += [{"col": lax.rem(c + step, RING)} for step in range(1, RING)]
    for partner in partners:
        pl.semaphore_signal(barrier, inc=1, device_id=partner, device_id_type=MESH)

    nbas, nvir = virt_ref.shape
    vpad[...] = jnp.zeros_like(vpad)
    for load in loads:
        load.wait()
    vpad[0:nbas, 0:nvir] = virt_in[...]
    for quarter in range(4):
        block = vpad[128 * quarter : 128 * quarter + 128, :]
        vq[c, quarter] = block.T[0:nvir, :]
    for orbital in range(2):
        hs[d, orbital, 496:512, :] = jnp.zeros((16, LANES), BF)
        hs[d, orbital, 0:nbas, :] = slab_in[orbital]

    pl.semaphore_wait(barrier, len(partners))

    j = lax.rem(r, 4)
    j_up, j_down = lax.rem(j + 1, 4), lax.rem(j + 3, 4)
    spans = (pl.ds(0, 208), pl.ds(208, 224))

    def slab(n, orbital, **target):
        return send(hs.at[n, orbital], hs.at[n, orbital], **target)

    def virt(n, quarter, half, **target):
        piece = vq.at[n, quarter, spans[half]]
        return send(piece, piece, **target)

    def virt_rows(n, half):
        return virt(n, j, half, row=r_up), virt(n, j, half, row=r_down)

    pair = {1: slab(d, 1, depth=d_sib), 0: slab(d, 0, depth=d_sib)}
    z_up = {1: virt(c, j, 1, col=c_up)}
    z_down = {0: virt(c, j, 0, col=c_down)}
    z_up[0] = virt(c, j, 0, col=c_up)
    z_down[1] = virt(c, j, 1, col=c_down)
    up = {1: slab(d, 1, depth=d_up)}
    down = {0: slab(d, 0, depth=d_down)}
    up[0] = slab(d, 0, depth=d_up)
    down[1] = slab(d, 1, depth=d_down)
    share = [send(vq.at[c], vq.at[c], col=c_sib)]

    rows_a, rows_b, rows_c = {}, {}, {}
    z_up[1].wait_recv()
    z_up2 = virt(c_down, j, 1, col=c_up)
    rows_a[1] = virt_rows(c_down, 1)
    z_down[0].wait_recv()
    z_down2 = virt(c_up, j, 0, col=c_down)
    rows_b[0] = virt_rows(c_up, 0)
    up2, down2 = {}, {}
    pair[1].wait_recv()
    up2[1] = slab(d_sib, 1, depth=d_up)
    pair[0].wait_recv()
    down2[0] = slab(d_sib, 0, depth=d_down)
    up2[0] = slab(d_sib, 0, depth=d_up)
    down2[1] = slab(d_sib, 1, depth=d_down)
    z_up[0].wait_recv()
    rows_a[0] = virt_rows(c_down, 0)
    z_down[1].wait_recv()
    rows_b[1] = virt_rows(c_up, 1)
    up[1].wait_recv()
    up3 = slab(d_down, 1, depth=d_up)
    down[0].wait_recv()
    down3 = slab(d_up, 0, depth=d_down)

    def pass_up(n, rows):
        rows[1][0].wait_recv()
        return virt(n, j_down, 1, row=r_up)

    def pass_down(n, rows):
        rows[0][1].wait_recv()
        return virt(n, j_up, 0, row=r_down)

    z_up2.wait_recv()
    rows_c[1] = virt_rows(c_far, 1)
    z_down2.wait_recv()
    rows_c[0] = virt_rows(c_far, 0)
    on_a = [pass_up(c_down, rows_a)]
    on_b = [pass_down(c_up, rows_b)]
    on_a.append(pass_down(c_down, rows_a))
    on_b.append(pass_up(c_up, rows_b))
    up2[1].wait_recv()
    up4 = slab(other(d_down), 1, depth=d_up)
    down2[0].wait_recv()
    down4 = slab(other(d_up), 0, depth=d_down)
    on_c = [pass_up(c_far, rows_c), pass_down(c_far, rows_c)]

    wrow[...] = jnp.zeros_like(wrow)
    freq = freq_in[0]
    for orbital in range(2):
        gap = energy_in[...] - occ_in[orbital]
        weight = 4.0 * gap / (gap * gap + freq * freq)
        wrow[:, 0:nvir] = jnp.broadcast_to(weight, (LANES, nvir))
        wcol[432 * orbital : 432 * orbital + 432, :] = wrow[...].T[0:nvir, :]
    acc[...] = jnp.zeros_like(acc)

    for n, rows, on in ((c_down, rows_a, on_a), (c_up, rows_b, on_b), (c_far, rows_c, on_c)):
        for copy in (rows[0][0], rows[1][1], *on):
            copy.wait_recv()
        share.append(send(vq.at[n], vq.at[n], col=c_sib))
    for copy in (up[0], down[1], up2[0], down2[1], up3, down3, up4, down4):
        copy.wait_recv()

    def couple(parity):
        @pl.loop(0, 4)
        def _(at):
            n = 2 * at + parity
            left = jnp.concatenate([vq[n, 0], vq[n, 1], vq[n, 2], vq[n, 3]], axis=1)
            right = jnp.concatenate([hs[n, 0], hs[n, 1]], axis=1)
            acc[...] += jnp.dot(left, right, preferred_element_type=F32)

    couple(lax.rem(c, 2))
    for copy in share:
        copy.wait_recv()
    couple(1 - lax.rem(c, 2))
    halves = (pl.ds(0, 432), pl.ds(432, 432))
    for orbital in range(2):
        rp[c, halves[orbital], :] = acc[:, LANES * orbital : LANES * orbital + LANES].astype(BF)

    def panel(n, half, **target):
        piece = rp.at[n, halves[half]]
        return send(piece, piece, **target)

    def piece_on(slot, half, to, **target):
        return send(qp.at[slot, halves[half]], qp.at[to, halves[half]], **target)

    y_up = {1: send(rp.at[c, halves[1]], qp.at[1, halves[1]], row=r_up)}
    y_down = {0: send(rp.at[c, halves[0]], qp.at[2, halves[0]], row=r_down)}
    z_up = {1: panel(c, 1, col=c_up)}
    z_down = {0: panel(c, 0, col=c_down)}
    y_up[0] = send(rp.at[c, halves[0]], qp.at[1, halves[0]], row=r_up)
    y_down[1] = send(rp.at[c, halves[1]], qp.at[2, halves[1]], row=r_down)
    z_up[0] = panel(c, 0, col=c_up)
    z_down[1] = panel(c, 1, col=c_down)
    share_own = send(rp.at[c], rp.at[c], col=c_sib)
    qp[0] = rp[c]

    def weigh(n):
        product = wcol[...] * rp[n].astype(F32)
        wl[n] = product.astype(BF).T

    weigh(c)
    y_up2, y_down2, y_up3, y_down3 = {}, {}, {}, {}

    def y_step(before_up, before_down, after_up, after_down, slot):
        for half in (1, 0):
            before_up[half].wait_recv()
            after_up[half] = piece_on(slot, half, slot + 2, row=r_up)
            before_down[1 - half].wait_recv()
            after_down[1 - half] = piece_on(slot + 1, 1 - half, slot + 3, row=r_down)

    z_up[1].wait_recv()
    z_up2 = panel(c_down, 1, col=c_up)
    z_down[0].wait_recv()
    z_down2 = panel(c_up, 0, col=c_down)
    y_step(y_up, y_down, y_up2, y_down2, 1)
    z_up[0].wait_recv()
    share_down = send(rp.at[c_down], rp.at[c_down], col=c_sib)
    z_down[1].wait_recv()
    share_up = send(rp.at[c_up], rp.at[c_up], col=c_sib)
    share_own.wait_recv()
    weigh(c_sib)
    weigh(c_down)
    y_step(y_up2, y_down2, y_up3, y_down3, 3)
    weigh(c_up)
    z_up2.wait_recv()
    z_down2.wait_recv()
    share_far = send(rp.at[c_far], rp.at[c_far], col=c_sib)
    share_down.wait_recv()
    weigh(other(c_down))
    y_up3[1].wait_recv()
    y_up4 = piece_on(5, 1, 7, row=r_up)
    y_down3[0].wait_recv()
    y_down4 = piece_on(6, 0, 7, row=r_down)
    share_up.wait_recv()
    weigh(other(c_up))
    weigh(c_far)
    share_far.wait_recv()
    weigh(other(c_far))

    low, high = slice(0, 64), slice(64, 128)
    targets = {"far": d_far, "up": d_up, "down": d_down, "own": d}

    def terms_of(name, slots):
        rows = wl[pl.ds(2 * (targets[name] // 2), 2)].reshape(256, 864)
        columns = jnp.concatenate([qp[slot] for slot in slots], axis=1)
        terms = jnp.dot(rows, columns, preferred_element_type=F32)
        return terms.reshape(2, 128, LANES * len(slots))

    class RingSum:
        def __init__(self, raw, land, keep, own):
            self.raw, self.land, self.keep, self.own, self.copies = raw, land, keep, own, {}

        def send(self, at, value, **target):
            self.raw[at] = value.astype(BF)
            self.copies[at] = send(self.raw.at[at], self.land.at[at], **target)

        def give(self, name, block):
            if name == "far":
                self.send(0, block[:, high], depth=d_up)
                self.send(1, block[:, low], depth=d_down)
            elif name == "up":
                self.send(2, block[:, low], depth=d_up)
                self.keep[0] = block[:, high]
            elif name == "down":
                self.send(3, block[:, high], depth=d_down)
                self.keep[1] = block[:, low]
            else:
                self.own[...] = block

        def pass_on(self):
            for at, target in ((0, d_up), (1, d_down)):
                self.copies[at].wait_recv()
                self.send(at + 4, self.keep[at] + self.land[at].astype(F32), depth=target)

        def end(self):
            for at in (2, 3, 4, 5):
                self.copies[at].wait_recv()
            land = self.land
            self.own[:, low] = self.own[:, low] + land[2].astype(F32) + land[5].astype(F32)
            self.own[:, high] = self.own[:, high] + land[3].astype(F32) + land[4].astype(F32)

    plane = lax.rem(d, 2)
    slots_a, slots_b = (0, 1, 2, 3, 4), (5, 6, 7)
    ring_a = RingSum(a_raw, a_land, a_keep, a_own)
    ring_b = RingSum(b_raw, b_land, b_keep, b_own)
    for name in targets:
        ring_a.give(name, terms_of(name, slots_a))
    ring_a.pass_on()
    y_up3[0].wait_recv()
    y_down3[1].wait_recv()
    y_up4.wait_recv()
    y_down4.wait_recv()
    b_pair = {}
    for at, name in enumerate(targets):
        b_terms[at] = terms_of(name, slots_b)
        b_give[at] = b_terms[at, 1 - plane].astype(BF)
        b_pair[name] = send(b_give.at[at], b_take.at[at], depth=d_sib)
    ring_a.end()
    a_sib[...] = a_own[1 - plane].astype(BF)
    last = send(a_sib, a_last, depth=d_sib)
    for at, name in enumerate(targets):
        b_pair[name].wait_recv()
        ring_b.give(name, (b_terms[at, plane] + b_take[at].astype(F32))[None])

    rows_of = [r, r_down, r_up, *(lax.rem(r + step, RING) for step in (6, 2, 5, 3, 4))]

    def tile(at):
        return pl.ds(pl.multiple_of(at * LANES, LANES), LANES)

    def in_first(at):
        apart = lax.rem(at - r + RING, RING)
        return jnp.logical_or(apart <= 2, apart >= 6)

    last.wait_recv()
    total = (a_own[plane] + a_last[...].astype(F32)).astype(BF)
    for at, slot in enumerate(slots_a):
        red[rows_of[slot]] = total[:, LANES * at : LANES * at + LANES]
    spread = []
    for step in (4, 2, 6, 3, 5, 1, 7):
        to = lax.rem(c + step, RING)
        copy = links.plan(red.at[to], out_ref.at[d, :, tile(c)], col=to)
        spread.append((to, copy))
        pl.when(in_first(to))(copy.start)
    ring_b.pass_on()
    ring_b.end()
    for at, slot in enumerate(slots_b):
        red[rows_of[slot]] = b_own[0, :, LANES * at : LANES * at + LANES].astype(BF)
    for to, copy in spread:
        pl.when(jnp.logical_not(in_first(to)))(copy.start)
    out_ref[d, :, tile(c)] = red[c]
    for _, copy in spread:
        copy.wait_recv()

    def part(n, begin, size):
        return out_ref.at[n, pl.ds(begin, size)]

    def pass_on(n, begin, size, **target):
        return send(part(n, begin, size), part(n, begin, size), **target)

    pair = pass_on(d, 0, 64, depth=d_sib)
    b_up = pass_on(d, 64, 64, depth=d_up)
    b_down = pass_on(d, 64, 64, depth=d_down)
    b_pairs = [pass_on(d, 64, 64, depth=d_sib)]
    a_up = pass_on(d, 0, 64, depth=d_up)
    a_down = pass_on(d, 0, 64, depth=d_down)
    pair.wait_recv()
    a_up2 = pass_on(d_sib, 0, 64, depth=d_up)
    a_down2 = pass_on(d_sib, 0, 64, depth=d_down)
    b_up.wait_recv()
    b_up2 = pass_on(d_down, 96, 32, depth=d_up)
    b_pairs.append(pass_on(d_down, 64, 64, depth=d_sib))
    b_down.wait_recv()
    b_down2 = pass_on(d_up, 64, 32, depth=d_down)
    b_pairs.append(pass_on(d_up, 64, 64, depth=d_sib))
    a_up.wait_recv()
    a_up3 = pass_on(d_down, 32, 32, depth=d_up)
    a_down.wait_recv()
    a_down3 = pass_on(d_up, 0, 32, depth=d_down)
    b_up2.wait_recv()
    b_pairs.append(pass_on(d_far, 96, 32, depth=d_sib))
    b_down2.wait_recv()
    b_pairs.append(pass_on(d_far, 64, 32, depth=d_sib))
    a_up2.wait_recv()
    a_up4 = pass_on(other(d_down), 32, 32, depth=d_up)
    a_down2.wait_recv()
    a_down4 = pass_on(other(d_up), 0, 32, depth=d_down)
    for copy in (a_up3, a_down3, a_up4, a_down4, *b_pairs):
        copy.wait_recv()
    links.finish()


def on_device(half_slabs, virtuals, occupied_energy, virtual_energy, frequency):
    hbm = pl.BlockSpec(memory_space=pltpu.HBM)
    copies = 120
    gram = pl.pallas_call(
        gather_kernel,
        out_shape=jax.ShapeDtypeStruct((RING, 128, 1024), BF),
        in_specs=[hbm] * 5,
        out_specs=pl.BlockSpec(memory_space=pltpu.VMEM),
        scratch_shapes=[
            pltpu.VMEM((2, 500, LANES), BF),
            pltpu.VMEM((500, 432), BF),
            pltpu.VMEM((1, 432), F32),
            pltpu.SMEM((2,), F32),
            pltpu.SMEM((1,), F32),
            pltpu.VMEM((512, 512), BF),
            pltpu.VMEM((RING, 4, 432, LANES), BF),
            pltpu.VMEM((RING, 2, 512, LANES), BF),
            pltpu.VMEM((432, 2 * LANES), F32),
            pltpu.VMEM((RING, 864, LANES), BF),
            pltpu.VMEM((RING, 864, LANES), BF),
            pltpu.VMEM((LANES, 512), F32),
            pltpu.VMEM((864, LANES), F32),
            pltpu.VMEM((RING, 128, 864), BF),
            pltpu.VMEM((6, 2, 64, 640), BF),
            pltpu.VMEM((6, 2, 64, 640), BF),
            pltpu.VMEM((2, 2, 64, 640), F32),
            pltpu.VMEM((2, 128, 640), F32),
            pltpu.VMEM((128, 640), BF),
            pltpu.VMEM((128, 640), BF),
            pltpu.VMEM((4, 2, 128, 384), F32),
            pltpu.VMEM((6, 1, 64, 384), BF),
            pltpu.VMEM((6, 1, 64, 384), BF),
            pltpu.VMEM((2, 1, 64, 384), F32),
            pltpu.VMEM((1, 128, 384), F32),
            pltpu.VMEM((4, 128, 384), BF),
            pltpu.VMEM((4, 128, 384), BF),
            pltpu.VMEM((RING, 128, LANES), BF),
            pltpu.SemaphoreType.DMA((5,)),
            pltpu.SemaphoreType.DMA((copies,)),
            pltpu.SemaphoreType.DMA((copies,)),
        ],
        compiler_params=pltpu.CompilerParams(
            collective_id=0, has_side_effects=True, vmem_limit_bytes=48 * 2**20
        ),
        cost_estimate=pl.CostEstimate(flops=2_700_000_000, bytes_accessed=3_000_000, transcendentals=0),
    )(half_slabs, virtuals, virtual_energy.reshape(1, -1), occupied_energy, frequency)
    return gram.reshape(1024, 1024).astype(F32)


def solution(mesh):
    placed = (P(None, "depth", ("row", "col")), P("col", "depth"), P(), P("depth"), P())
    return jax.shard_map(
        on_device, mesh=mesh, in_specs=placed, out_specs=P("row", "col"), check_vma=False
    )
```

```python
import jax
import jax.numpy as jnp
from jax import lax
from jax.experimental import pallas as pl
from jax.experimental.pallas import tpu as pltpu
from jax.sharding import PartitionSpec as P

MESH = pl.DeviceIdType.MESH
BF = jnp.bfloat16
F32 = jnp.float32
RING = 8
LANES = 128


class Links:
    def __init__(self, send_sems, recv_sems):
        self.send_sems, self.recv_sems, self.copies = send_sems, recv_sems, []

    def plan(self, src, dst, **target):
        at = len(self.copies)
        copy = pltpu.make_async_remote_copy(
            src_ref=src,
            dst_ref=dst,
            send_sem=self.send_sems.at[at],
            recv_sem=self.recv_sems.at[at],
            device_id=target,
            device_id_type=MESH,
        )
        self.copies.append(copy)
        return copy

    def send(self, src, dst, **target):
        copy = self.plan(src, dst, **target)
        copy.start()
        return copy

    def finish(self):
        for copy in self.copies:
            copy.wait_send()


def around(me):
    up, down, far = lax.rem(me + 2, RING), lax.rem(me + 6, RING), lax.rem(me + 4, RING)
    return up, down, far, me + 1 - 2 * lax.rem(me, 2)


def other(at):
    return at + 1 - 2 * lax.rem(at, 2)


def gather_kernel(
    slabs_ref, virt_ref, weight_ref, out_ref,
    slab_in, virt_in, weight_in, vq, hs, acc, rp, qp, wrow, wcol, wl,
    a_raw, a_land, a_keep, a_own, a_sib, a_last,
    b_terms, b_raw, b_land, b_keep, b_own, b_give, b_take, red,
    local_sems, send_sems, recv_sems,
):
    d, r, c = lax.axis_index("depth"), lax.axis_index("row"), lax.axis_index("col")
    d_up, d_down, d_far, d_sib = around(d)
    c_up, c_down, c_far, c_sib = around(c)
    r_up, r_down = lax.rem(r + 1, RING), lax.rem(r + 7, RING)
    links = Links(send_sems, recv_sems)
    send = links.send

    loads = [
        pltpu.make_async_copy(src, dst, local_sems.at[at])
        for at, (src, dst) in enumerate(((virt_ref, virt_in), (slabs_ref, slab_in), (weight_ref, weight_in)))
    ]
    for load in loads:
        load.start()
    barrier = pltpu.get_barrier_semaphore()
    partners = [{"depth": d_up}, {"depth": d_down}, {"depth": d_sib}, {"row": r_up}, {"row": r_down}]
    partners += [{"col": lax.rem(c + step, RING)} for step in range(1, RING)]
    for partner in partners:
        pl.semaphore_signal(barrier, inc=1, device_id=partner, device_id_type=MESH)

    nvir, nbas = virt_ref.shape
    vq[c, 3] = jnp.zeros((nvir, LANES), BF)
    for load in loads:
        load.wait()
    for quarter in range(3):
        vq[c, quarter] = virt_in[:, LANES * quarter : LANES * quarter + LANES]
    vq[c, 3, :, 0 : nbas - 384] = virt_in[:, 384:nbas]
    for orbital in range(2):
        hs[d, orbital, 496:512, :] = jnp.zeros((16, LANES), BF)
        hs[d, orbital, 0:nbas, :] = slab_in[orbital]

    pl.semaphore_wait(barrier, len(partners))

    j = lax.rem(r, 4)
    j_up, j_down = lax.rem(j + 1, 4), lax.rem(j + 3, 4)
    spans = (pl.ds(0, 208), pl.ds(208, 224))

    def slab(n, orbital, half=None, **target):
        piece = hs.at[n, orbital] if half is None else hs.at[n, orbital, pl.ds(256 * half, 256)]
        return send(piece, piece, **target)

    def virt(n, quarter, half, **target):
        piece = vq.at[n, quarter, spans[half]]
        return send(piece, piece, **target)

    def virt_rows(n, half):
        return virt(n, j, half, row=r_up), virt(n, j, half, row=r_down)

    pair, up, down, up2, down2, up3, down3, up4, down4 = ({} for _ in range(9))

    def slabs_out(o):
        up[o], down[o] = slab(d, o, depth=d_up), slab(d, o, depth=d_down)

    def slabs_sib(o):
        pair[o].wait_recv()
        up2[o], down2[o] = slab(d_sib, o, depth=d_up), slab(d_sib, o, depth=d_down)

    def slabs_on(o):
        up[o].wait_recv()
        up3[o] = slab(d_down, o, 1, depth=d_up)
        down[o].wait_recv()
        down3[o] = slab(d_up, o, 0, depth=d_down)

    def slabs_sib_on(o):
        up2[o].wait_recv()
        up4[o] = slab(other(d_down), o, 1, depth=d_up)
        down2[o].wait_recv()
        down4[o] = slab(other(d_up), o, 0, depth=d_down)

    def slabs_end(o):
        for copy in (up3[o], down3[o], up4[o], down4[o]):
            copy.wait_recv()

    z_up = {1: virt(c, j, 1, col=c_up)}
    z_down = {0: virt(c, j, 0, col=c_down)}
    z_up[0] = virt(c, j, 0, col=c_up)
    z_down[1] = virt(c, j, 1, col=c_down)
    slabs_out(0)
    pair[0] = slab(d, 0, depth=d_sib)
    share_own = send(vq.at[c], vq.at[c], col=c_sib)

    rows_a, rows_b, rows_c = {}, {}, {}
    z_up[1].wait_recv()
    z_up2 = virt(c_down, j, 1, col=c_up)
    rows_a[1] = virt_rows(c_down, 1)
    z_down[0].wait_recv()
    z_down2 = virt(c_up, j, 0, col=c_down)
    rows_b[0] = virt_rows(c_up, 0)
    z_up[0].wait_recv()
    rows_a[0] = virt_rows(c_down, 0)
    z_down[1].wait_recv()
    rows_b[1] = virt_rows(c_up, 1)
    slabs_sib(0)
    slabs_on(0)
    z_up2.wait_recv()
    rows_c[1] = virt_rows(c_far, 1)
    z_down2.wait_recv()
    rows_c[0] = virt_rows(c_far, 0)
    pair[1] = slab(d, 1, depth=d_sib)
    slabs_out(1)

    def pass_up(n, rows):
        rows[1][0].wait_recv()
        return virt(n, j_down, 1, row=r_up)

    def pass_down(n, rows):
        rows[0][1].wait_recv()
        return virt(n, j_up, 0, row=r_down)

    on_a = [pass_up(c_down, rows_a)]
    on_b = [pass_down(c_up, rows_b)]
    on_a.append(pass_down(c_down, rows_a))
    on_b.append(pass_up(c_up, rows_b))
    slabs_sib_on(0)
    on_c = [pass_up(c_far, rows_c), pass_down(c_far, rows_c)]
    slabs_sib(1)
    slabs_on(1)

    wrow[...] = jnp.zeros_like(wrow)
    for orbital in range(2):
        wrow[:, 0:nvir] = jnp.broadcast_to(weight_in[orbital : orbital + 1, :], (LANES, nvir))
        wcol[orbital] = wrow[...].T[0:nvir, :]
    acc[...] = jnp.zeros_like(acc)

    def virt_end(n, rows, on):
        for copy in (rows[0][0], rows[1][1], *on):
            copy.wait_recv()
        return send(vq.at[n], vq.at[n], col=c_sib)

    def couple(n, orbital):
        left = jnp.concatenate([vq[n, 0], vq[n, 1], vq[n, 2], vq[n, 3]], axis=1)
        acc[orbital] += jnp.dot(left, hs[n, orbital], preferred_element_type=F32)

    share_a = virt_end(c_down, rows_a, on_a)
    share_b = virt_end(c_up, rows_b, on_b)
    slabs_end(0)
    couple(c, 0)
    share_own.wait_recv()
    couple(c_sib, 0)
    couple(c_down, 0)
    couple(c_up, 0)
    share_c = virt_end(c_far, rows_c, on_c)
    slabs_sib_on(1)
    share_a.wait_recv()
    couple(other(c_down), 0)
    share_b.wait_recv()
    couple(other(c_up), 0)
    couple(c_far, 0)
    share_c.wait_recv()
    couple(other(c_far), 0)

    def panel(n, orbital, **target):
        return send(rp.at[n, orbital], rp.at[n, orbital], **target)

    y_up, y_down, z_up, z_down = {}, {}, {}, {}
    share_own, share_down, share_up, share_far = {}, {}, {}, {}

    def panels_out(o):
        rp[c, o] = acc[o].astype(BF)
        y_up[1, o] = send(rp.at[c, o], qp.at[1, o], row=r_up)
        y_down[1, o] = send(rp.at[c, o], qp.at[2, o], row=r_down)
        z_up[o] = panel(c, o, col=c_up)
        z_down[o] = panel(c, o, col=c_down)
        share_own[o] = panel(c, o, col=c_sib)
        qp[0, o] = rp[c, o]

    def y_step(step, o):
        slot = 2 * step - 1
        y_up[step, o].wait_recv()
        y_up[step + 1, o] = send(qp.at[slot, o], qp.at[slot + 2, o], row=r_up)
        y_down[step, o].wait_recv()
        y_down[step + 1, o] = send(qp.at[slot + 1, o], qp.at[slot + 3, o], row=r_down)

    def z_step(o):
        z_up[o].wait_recv()
        if o == 1:
            z_up["far"] = panel(c_down, 1, col=c_up)
        share_down[o] = panel(c_down, o, col=c_sib)
        z_down[o].wait_recv()
        if o == 0:
            z_down["far"] = panel(c_up, 0, col=c_down)
        share_up[o] = panel(c_up, o, col=c_sib)

    def weigh(n, o):
        product = wcol[o] * rp[n, o].astype(F32)
        wl[o, n] = product.astype(BF).T

    panels_out(0)
    slabs_end(1)

    @pl.loop(0, RING)
    def _(n):
        couple(n, 1)

    panels_out(1)
    y_step(1, 0)
    z_step(0)
    weigh(c, 0)
    weigh(c, 1)
    y_step(1, 1)
    z_step(1)
    share_own[0].wait_recv()
    weigh(c_sib, 0)
    weigh(c_down, 0)
    y_step(2, 0)
    weigh(c_up, 0)
    z_down["far"].wait_recv()
    share_far[0] = panel(c_far, 0, col=c_sib)
    share_own[1].wait_recv()
    weigh(c_sib, 1)
    y_step(2, 1)
    weigh(c_down, 1)
    z_up["far"].wait_recv()
    share_far[1] = panel(c_far, 1, col=c_sib)
    weigh(c_up, 1)
    weigh(c_far, 0)
    for n, share in ((other(c_down), share_down), (other(c_up), share_up)):
        share[0].wait_recv()
        weigh(n, 0)
    y_down[3, 0].wait_recv()
    y_down[4, 0] = send(qp.at[6, 0], qp.at[7, 0], row=r_down)
    for n, share in ((other(c_down), share_down), (other(c_up), share_up)):
        share[1].wait_recv()
        weigh(n, 1)
    y_up[3, 1].wait_recv()
    y_up[4, 1] = send(qp.at[5, 1], qp.at[7, 1], row=r_up)
    weigh(c_far, 1)
    for o in range(2):
        share_far[o].wait_recv()
        weigh(other(c_far), o)

    low, high = slice(0, 64), slice(64, 128)
    targets = {"far": d_far, "up": d_up, "down": d_down, "own": d}

    def terms_of(name, slots):
        terms = 0.0
        for o in range(2):
            rows = wl[o, pl.ds(2 * (targets[name] // 2), 2)].reshape(256, 432)
            columns = jnp.concatenate([qp[slot, o] for slot in slots], axis=1)
            terms += jnp.dot(rows, columns, preferred_element_type=F32)
        return terms.reshape(2, 128, LANES * len(slots))

    class RingSum:
        def __init__(self, raw, land, keep, own):
            self.raw, self.land, self.keep, self.own, self.copies = raw, land, keep, own, {}

        def send(self, at, value, **target):
            self.raw[at] = value.astype(BF)
            self.copies[at] = send(self.raw.at[at], self.land.at[at], **target)

        def give(self, name, block):
            if name == "far":
                self.send(0, block[:, high], depth=d_up)
                self.send(1, block[:, low], depth=d_down)
            elif name == "up":
                self.send(2, block[:, low], depth=d_up)
                self.keep[0] = block[:, high]
            elif name == "down":
                self.send(3, block[:, high], depth=d_down)
                self.keep[1] = block[:, low]
            else:
                self.own[...] = block

        def pass_on(self):
            for at, target in ((0, d_up), (1, d_down)):
                self.copies[at].wait_recv()
                self.send(at + 4, self.keep[at] + self.land[at].astype(F32), depth=target)

        def end(self):
            for at in (2, 3, 4, 5):
                self.copies[at].wait_recv()
            land = self.land
            self.own[:, low] = self.own[:, low] + land[2].astype(F32) + land[5].astype(F32)
            self.own[:, high] = self.own[:, high] + land[3].astype(F32) + land[4].astype(F32)

    plane = lax.rem(d, 2)
    slots_a, slots_b = (0, 1, 2, 3, 4), (5, 6, 7)
    ring_a = RingSum(a_raw, a_land, a_keep, a_own)
    ring_b = RingSum(b_raw, b_land, b_keep, b_own)
    for name in targets:
        ring_a.give(name, terms_of(name, slots_a))
    y_up[3, 0].wait_recv()
    y_down[3, 1].wait_recv()
    y_up[4, 1].wait_recv()
    y_down[4, 0].wait_recv()
    b_pair = {}
    for at, name in enumerate(targets):
        b_terms[at] = terms_of(name, slots_b)
        b_give[at] = b_terms[at, 1 - plane].astype(BF)
        b_pair[name] = send(b_give.at[at], b_take.at[at], depth=d_sib)
        if at == 0:
            ring_a.pass_on()
    for at, name in enumerate(targets):
        b_pair[name].wait_recv()
        ring_b.give(name, (b_terms[at, plane] + b_take[at].astype(F32))[None])
    ring_a.end()
    a_sib[...] = a_own[1 - plane].astype(BF)
    last = send(a_sib, a_last, depth=d_sib)
    ring_b.pass_on()

    rows_of = [r, r_down, r_up, *(lax.rem(r + step, RING) for step in (6, 2, 5, 3, 4))]

    def tile(at):
        return pl.ds(pl.multiple_of(at * LANES, LANES), LANES)

    def in_first(at):
        apart = lax.rem(at - r + RING, RING)
        return jnp.logical_or(apart <= 2, apart >= 6)

    last.wait_recv()
    total = (a_own[plane] + a_last[...].astype(F32)).astype(BF)
    for at, slot in enumerate(slots_a):
        red[rows_of[slot]] = total[:, LANES * at : LANES * at + LANES]
    spread = []
    for step in (4, 2, 6, 3, 5, 1, 7):
        to = lax.rem(c + step, RING)
        copy = links.plan(red.at[to], out_ref.at[d, :, tile(c)], col=to)
        spread.append((to, copy))
        pl.when(in_first(to))(copy.start)
    ring_b.end()
    for at, slot in enumerate(slots_b):
        red[rows_of[slot]] = b_own[0, :, LANES * at : LANES * at + LANES].astype(BF)
    for to, copy in spread:
        pl.when(jnp.logical_not(in_first(to)))(copy.start)
    out_ref[d, :, tile(c)] = red[c]
    for _, copy in spread:
        copy.wait_recv()

    def part(n, begin, size):
        return out_ref.at[n, pl.ds(begin, size)]

    def pass_on(n, begin, size, **target):
        return send(part(n, begin, size), part(n, begin, size), **target)

    pair = pass_on(d, 0, 64, depth=d_sib)
    b_up = pass_on(d, 64, 64, depth=d_up)
    b_down = pass_on(d, 64, 64, depth=d_down)
    b_pairs = [pass_on(d, 64, 64, depth=d_sib)]
    a_up = pass_on(d, 0, 64, depth=d_up)
    a_down = pass_on(d, 0, 64, depth=d_down)
    pair.wait_recv()
    a_up2 = pass_on(d_sib, 0, 64, depth=d_up)
    a_down2 = pass_on(d_sib, 0, 64, depth=d_down)
    b_up.wait_recv()
    b_up2 = pass_on(d_down, 96, 32, depth=d_up)
    b_pairs.append(pass_on(d_down, 64, 64, depth=d_sib))
    b_down.wait_recv()
    b_down2 = pass_on(d_up, 64, 32, depth=d_down)
    b_pairs.append(pass_on(d_up, 64, 64, depth=d_sib))
    a_up.wait_recv()
    a_up3 = pass_on(d_down, 32, 32, depth=d_up)
    a_down.wait_recv()
    a_down3 = pass_on(d_up, 0, 32, depth=d_down)
    b_up2.wait_recv()
    b_pairs.append(pass_on(d_far, 96, 32, depth=d_sib))
    b_down2.wait_recv()
    b_pairs.append(pass_on(d_far, 64, 32, depth=d_sib))
    a_up2.wait_recv()
    a_up4 = pass_on(other(d_down), 32, 32, depth=d_up)
    a_down2.wait_recv()
    a_down4 = pass_on(other(d_up), 0, 32, depth=d_down)
    for copy in (a_up3, a_down3, a_up4, a_down4, *b_pairs):
        copy.wait_recv()
    links.finish()


def on_device(half_slabs, virtuals, occupied_energy, virtual_energy, frequency):
    hbm = pl.BlockSpec(memory_space=pltpu.HBM)
    excitation = virtual_energy[None, :] - occupied_energy[:, None]
    weight = 4.0 * excitation / (excitation * excitation + frequency[0] * frequency[0])
    copies = 128
    gram = pl.pallas_call(
        gather_kernel,
        out_shape=jax.ShapeDtypeStruct((RING, 128, 1024), BF),
        in_specs=[hbm] * 3,
        out_specs=pl.BlockSpec(memory_space=pltpu.VMEM),
        scratch_shapes=[
            pltpu.VMEM((2, 500, LANES), BF),
            pltpu.VMEM((432, 500), BF),
            pltpu.VMEM((2, 432), F32),
            pltpu.VMEM((RING, 4, 432, LANES), BF),
            pltpu.VMEM((RING, 2, 512, LANES), BF),
            pltpu.VMEM((2, 432, LANES), F32),
            pltpu.VMEM((RING, 2, 432, LANES), BF),
            pltpu.VMEM((RING, 2, 432, LANES), BF),
            pltpu.VMEM((LANES, 512), F32),
            pltpu.VMEM((2, 432, LANES), F32),
            pltpu.VMEM((2, RING, 128, 432), BF),
            pltpu.VMEM((6, 2, 64, 640), BF),
            pltpu.VMEM((6, 2, 64, 640), BF),
            pltpu.VMEM((2, 2, 64, 640), F32),
            pltpu.VMEM((2, 128, 640), F32),
            pltpu.VMEM((128, 640), BF),
            pltpu.VMEM((128, 640), BF),
            pltpu.VMEM((4, 2, 128, 384), F32),
            pltpu.VMEM((6, 1, 64, 384), BF),
            pltpu.VMEM((6, 1, 64, 384), BF),
            pltpu.VMEM((2, 1, 64, 384), F32),
            pltpu.VMEM((1, 128, 384), F32),
            pltpu.VMEM((4, 128, 384), BF),
            pltpu.VMEM((4, 128, 384), BF),
            pltpu.VMEM((RING, 128, LANES), BF),
            pltpu.SemaphoreType.DMA((3,)),
            pltpu.SemaphoreType.DMA((copies,)),
            pltpu.SemaphoreType.DMA((copies,)),
        ],
        compiler_params=pltpu.CompilerParams(
            collective_id=0, has_side_effects=True, vmem_limit_bytes=48 * 2**20
        ),
        cost_estimate=pl.CostEstimate(flops=2_700_000_000, bytes_accessed=3_000_000, transcendentals=0),
    )(half_slabs, virtuals.T, weight)
    return gram.reshape(1024, 1024).astype(F32)


def solution(mesh):
    placed = (P(None, "depth", ("row", "col")), P("col", "depth"), P(), P("depth"), P())
    return jax.shard_map(
        on_device, mesh=mesh, in_specs=placed, out_specs=P("row", "col"), check_vma=False
    )
```

```python
import jax
import jax.numpy as jnp
from jax import lax
from jax.experimental import pallas as pl
from jax.experimental.pallas import tpu as pltpu
from jax.sharding import PartitionSpec as P

MESH = pl.DeviceIdType.MESH
BF = jnp.bfloat16
F32 = jnp.float32
RING = 8
LANES = 128


class Links:
    def __init__(self, send_sems, recv_sems):
        self.send_sems, self.recv_sems, self.copies = send_sems, recv_sems, []

    def plan(self, src, dst, **target):
        at = len(self.copies)
        copy = pltpu.make_async_remote_copy(
            src_ref=src,
            dst_ref=dst,
            send_sem=self.send_sems.at[at],
            recv_sem=self.recv_sems.at[at],
            device_id=target,
            device_id_type=MESH,
        )
        self.copies.append(copy)
        return copy

    def send(self, src, dst, **target):
        copy = self.plan(src, dst, **target)
        copy.start()
        return copy

    def finish(self):
        for copy in self.copies:
            copy.wait_send()


def around(me):
    up, down, far = lax.rem(me + 2, RING), lax.rem(me + 6, RING), lax.rem(me + 4, RING)
    return up, down, far, me + 1 - 2 * lax.rem(me, 2)


def other(at):
    return at + 1 - 2 * lax.rem(at, 2)


def gather_kernel(
    slabs_ref, virt_ref, weight_ref, out_ref,
    slab_in, virt_in, weight_in, vq, hs, acc, qp, wrow, wcol, heavy, wl_a, wl_b,
    a_raw, a_land, a_keep, a_own, a_sib, a_last,
    b_terms, b_raw, b_land, b_keep, b_own, b_give, b_take, red, spread_land, relay,
    local_sems, send_sems, recv_sems,
):
    d, r, c = lax.axis_index("depth"), lax.axis_index("row"), lax.axis_index("col")
    d_up, d_down, d_far, d_sib = around(d)
    c_up, c_down, c_far, c_sib = around(c)
    r_up, r_down = lax.rem(r + 1, RING), lax.rem(r + 7, RING)
    links = Links(send_sems, recv_sems)
    send = links.send

    loads = [
        pltpu.make_async_copy(src, dst, local_sems.at[at])
        for at, (src, dst) in enumerate(((virt_ref, virt_in), (slabs_ref, slab_in), (weight_ref, weight_in)))
    ]
    for load in loads:
        load.start()
    barrier = pltpu.get_barrier_semaphore()
    partners = [{"depth": d_up}, {"depth": d_down}, {"depth": d_sib}, {"row": r_up}, {"row": r_down}]
    partners += [{"col": lax.rem(c + step, RING)} for step in range(1, RING)]
    for partner in partners:
        pl.semaphore_signal(barrier, inc=1, device_id=partner, device_id_type=MESH)

    nvir, nbas = virt_ref.shape
    vq[c, 3] = jnp.zeros((nvir, LANES), BF)
    for load in loads:
        load.wait()
    for quarter in range(3):
        vq[c, quarter] = virt_in[:, LANES * quarter : LANES * quarter + LANES]
    vq[c, 3, :, 0 : nbas - 384] = virt_in[:, 384:nbas]
    for orbital in range(2):
        hs[d, orbital, 496:512, :] = jnp.zeros((16, LANES), BF)
        hs[d, orbital, 0:nbas, :] = slab_in[orbital]

    pl.semaphore_wait(barrier, len(partners))

    j = lax.rem(r, 4)
    j_up, j_down = lax.rem(j + 1, 4), lax.rem(j + 3, 4)
    spans = (pl.ds(0, 208), pl.ds(208, 224))

    def slab(n, orbital, half=None, **target):
        piece = hs.at[n, orbital] if half is None else hs.at[n, orbital, pl.ds(256 * half, 256)]
        return send(piece, piece, **target)

    def virt(n, quarter, half, **target):
        piece = vq.at[n, quarter, spans[half]]
        return send(piece, piece, **target)

    def virt_rows(n, half):
        return virt(n, j, half, row=r_up), virt(n, j, half, row=r_down)

    pair, up, down, up2, down2, up3, down3, up4, down4 = ({} for _ in range(9))

    def slabs_out(o):
        up[o], down[o] = slab(d, o, depth=d_up), slab(d, o, depth=d_down)

    def slabs_sib(o):
        pair[o].wait_recv()
        up2[o], down2[o] = slab(d_sib, o, depth=d_up), slab(d_sib, o, depth=d_down)

    def slabs_on(o):
        up[o].wait_recv()
        up3[o] = slab(d_down, o, 1, depth=d_up)
        down[o].wait_recv()
        down3[o] = slab(d_up, o, 0, depth=d_down)

    def slabs_sib_on(o):
        up2[o].wait_recv()
        up4[o] = slab(other(d_down), o, 1, depth=d_up)
        down2[o].wait_recv()
        down4[o] = slab(other(d_up), o, 0, depth=d_down)

    def slabs_end(o):
        for copy in (up3[o], down3[o], up4[o], down4[o]):
            copy.wait_recv()

    z_up = {1: virt(c, j, 1, col=c_up)}
    z_down = {0: virt(c, j, 0, col=c_down)}
    z_up[0] = virt(c, j, 0, col=c_up)
    z_down[1] = virt(c, j, 1, col=c_down)
    slabs_out(0)
    pair[0] = slab(d, 0, depth=d_sib)
    share_own = send(vq.at[c], vq.at[c], col=c_sib)

    rows_a, rows_b, rows_c = {}, {}, {}
    z_up[1].wait_recv()
    z_up2 = virt(c_down, j, 1, col=c_up)
    rows_a[1] = virt_rows(c_down, 1)
    z_down[0].wait_recv()
    z_down2 = virt(c_up, j, 0, col=c_down)
    rows_b[0] = virt_rows(c_up, 0)
    z_up[0].wait_recv()
    rows_a[0] = virt_rows(c_down, 0)
    z_down[1].wait_recv()
    rows_b[1] = virt_rows(c_up, 1)
    slabs_sib(0)
    slabs_on(0)
    z_up2.wait_recv()
    rows_c[1] = virt_rows(c_far, 1)
    z_down2.wait_recv()
    rows_c[0] = virt_rows(c_far, 0)
    pair[1] = slab(d, 1, depth=d_sib)
    slabs_out(1)

    def pass_up(n, rows):
        rows[1][0].wait_recv()
        return virt(n, j_down, 1, row=r_up)

    def pass_down(n, rows):
        rows[0][1].wait_recv()
        return virt(n, j_up, 0, row=r_down)

    on_a = [pass_up(c_down, rows_a)]
    on_b = [pass_down(c_up, rows_b)]
    on_a.append(pass_down(c_down, rows_a))
    on_b.append(pass_up(c_up, rows_b))
    slabs_sib_on(0)
    on_c = [pass_up(c_far, rows_c), pass_down(c_far, rows_c)]
    slabs_sib(1)
    slabs_on(1)

    wrow[...] = jnp.zeros_like(wrow)
    for orbital in range(2):
        wrow[:, 0:nvir] = jnp.broadcast_to(weight_in[orbital : orbital + 1, :], (LANES, nvir))
        wcol[orbital] = wrow[...].T[0:nvir, :]
    acc[...] = jnp.zeros_like(acc)
    for slot in range(RING):
        qp[slot, 864:896, :] = jnp.zeros((32, LANES), BF)
    heavy[864:896, :] = jnp.zeros((32, LANES), BF)

    def virt_end(n, rows, on):
        for copy in (rows[0][0], rows[1][1], *on):
            copy.wait_recv()
        return send(vq.at[n], vq.at[n], col=c_sib)

    def couple(n, orbital):
        left = jnp.concatenate([vq[n, 0], vq[n, 1], vq[n, 2], vq[n, 3]], axis=1)
        acc[orbital] += jnp.dot(left, hs[n, orbital], preferred_element_type=F32)

    share_a = virt_end(c_down, rows_a, on_a)
    share_b = virt_end(c_up, rows_b, on_b)
    slabs_end(0)
    couple(c, 0)
    share_own.wait_recv()
    couple(c_sib, 0)
    couple(c_down, 0)
    couple(c_up, 0)
    share_c = virt_end(c_far, rows_c, on_c)
    slabs_sib_on(1)
    share_a.wait_recv()
    couple(other(c_down), 0)
    share_b.wait_recv()
    couple(other(c_up), 0)
    couple(c_far, 0)
    share_c.wait_recv()
    couple(other(c_far), 0)

    parts = (pl.ds(0, 384), pl.ds(384, 480))
    panels = (wl_a, wl_b)

    def panel(n, part, **target):
        piece = panels[part].at[n]
        return send(piece, piece, **target)

    def column(slot, to, part, **target):
        return send(qp.at[slot, parts[part]], qp.at[to, parts[part]], **target)

    y_up, y_down, z_up, z_down = {}, {}, {}, {}
    share_own, share_down, share_up, share_far = {}, {}, {}, {}

    def panels_out(o):
        rows = slice(432 * o, 432 * o + 432)
        plain = acc[o].astype(BF)
        qp[0, rows, :] = plain
        y_up[1, o] = column(0, 1, o, row=r_up)
        y_down[1, o] = column(0, 2, o, row=r_down)
        heavy[rows, :] = (wcol[o] * plain.astype(F32)).astype(BF)
        if o == 0:
            wl_a[c] = heavy[0:384, :].T
        else:
            wl_b[c] = heavy[384:896, :].T
        z_up[o] = panel(c, o, col=c_up)
        z_down[o] = panel(c, o, col=c_down)
        share_own[o] = panel(c, o, col=c_sib)

    def y_step(step, o):
        slot = 2 * step - 1
        y_up[step, o].wait_recv()
        y_up[step + 1, o] = column(slot, slot + 2, o, row=r_up)
        y_down[step, o].wait_recv()
        y_down[step + 1, o] = column(slot + 1, slot + 3, o, row=r_down)

    def z_step(o):
        z_up[o].wait_recv()
        if o == 1:
            z_up["far"] = panel(c_down, 1, col=c_up)
        share_down[o] = panel(c_down, o, col=c_sib)
        z_down[o].wait_recv()
        if o == 0:
            z_down["far"] = panel(c_up, 0, col=c_down)
        share_up[o] = panel(c_up, o, col=c_sib)

    panels_out(0)
    slabs_end(1)

    @pl.loop(0, RING)
    def _(n):
        couple(n, 1)

    panels_out(1)
    y_step(1, 0)
    z_step(0)
    y_step(1, 1)
    z_step(1)
    y_step(2, 0)
    z_down["far"].wait_recv()
    share_far[0] = panel(c_far, 0, col=c_sib)
    y_step(2, 1)
    z_up["far"].wait_recv()
    share_far[1] = panel(c_far, 1, col=c_sib)
    for share in (share_own, share_down, share_up):
        share[0].wait_recv()
        share[1].wait_recv()
    y_down[3, 0].wait_recv()
    y_down[4, 0] = column(6, 7, 0, row=r_down)
    share_far[0].wait_recv()
    share_far[1].wait_recv()

    low, high = slice(0, 64), slice(64, 128)
    targets = {"far": d_far, "up": d_up, "down": d_down, "own": d}

    def terms_of(name, slots):
        at = pl.ds(2 * (targets[name] // 2), 2)
        rows = jnp.concatenate([wl_a[at].reshape(256, 384), wl_b[at].reshape(256, 512)], axis=1)
        columns = jnp.concatenate([qp[slot] for slot in slots], axis=1)
        terms = jnp.dot(rows, columns, preferred_element_type=F32)
        return terms.reshape(2, 128, LANES * len(slots))

    class RingSum:
        def __init__(self, raw, land, keep, own):
            self.raw, self.land, self.keep, self.own, self.copies = raw, land, keep, own, {}

        def send(self, at, value, **target):
            self.raw[at] = value.astype(BF)
            self.copies[at] = send(self.raw.at[at], self.land.at[at], **target)

        def give(self, name, block):
            if name == "far":
                self.send(0, block[:, high], depth=d_up)
                self.send(1, block[:, low], depth=d_down)
            elif name == "up":
                self.send(2, block[:, low], depth=d_up)
                self.keep[0] = block[:, high]
            elif name == "down":
                self.send(3, block[:, high], depth=d_down)
                self.keep[1] = block[:, low]
            else:
                self.own[...] = block

        def pass_on(self):
            for at, target in ((0, d_up), (1, d_down)):
                self.copies[at].wait_recv()
                self.send(at + 4, self.keep[at] + self.land[at].astype(F32), depth=target)

        def end(self):
            for at in (2, 3, 4, 5):
                self.copies[at].wait_recv()
            land = self.land
            self.own[:, low] = self.own[:, low] + land[2].astype(F32) + land[5].astype(F32)
            self.own[:, high] = self.own[:, high] + land[3].astype(F32) + land[4].astype(F32)

    plane = lax.rem(d, 2)
    slots_a, slots_b = (0, 1, 2, 3, 4), (5, 6, 7)
    ring_a = RingSum(a_raw, a_land, a_keep, a_own)
    ring_b = RingSum(b_raw, b_land, b_keep, b_own)
    ring_a.give("far", terms_of("far", slots_a))
    y_up[3, 1].wait_recv()
    y_up[4, 1] = column(5, 7, 1, row=r_up)
    for name in ("up", "down", "own"):
        ring_a.give(name, terms_of(name, slots_a))
    y_up[3, 0].wait_recv()
    y_down[3, 1].wait_recv()
    y_up[4, 1].wait_recv()
    y_down[4, 0].wait_recv()
    b_pair = {}
    for at, name in enumerate(targets):
        b_terms[at] = terms_of(name, slots_b)
        b_give[at] = b_terms[at, 1 - plane].astype(BF)
        b_pair[name] = send(b_give.at[at], b_take.at[at], depth=d_sib)
        if at == 0:
            ring_a.pass_on()
    for at, name in enumerate(targets):
        b_pair[name].wait_recv()
        ring_b.give(name, (b_terms[at, plane] + b_take[at].astype(F32))[None])
    ring_a.end()
    a_sib[...] = a_own[1 - plane].astype(BF)
    last = send(a_sib, a_last, depth=d_sib)
    ring_b.pass_on()

    rows_of = [r, r_down, r_up, *(lax.rem(r + step, RING) for step in (6, 2, 5, 3, 4))]

    def in_first(at):
        apart = lax.rem(at - r + RING, RING)
        return jnp.logical_or(apart <= 2, apart >= 6)

    last.wait_recv()
    total = (a_own[plane] + a_last[...].astype(F32)).astype(BF)
    for at, slot in enumerate(slots_a):
        red[rows_of[slot]] = total[:, LANES * at : LANES * at + LANES]
    spread = []
    far_sib = other(c_far)
    for to, by in (
        (c_far, c_up), (far_sib, c_down), (c_up, None), (c_down, None),
        (other(c_up), None), (other(c_down), None), (c_sib, None),
    ):
        if by is None:
            copy = links.plan(red.at[to], spread_land.at[c], col=to)
        else:
            copy = links.plan(red.at[to], relay.at[len(spread)], col=by)
        spread.append((to, copy))
        pl.when(in_first(to))(copy.start)
    ring_b.end()
    for at, slot in enumerate(slots_b):
        red[rows_of[slot]] = b_own[0, :, LANES * at : LANES * at + LANES].astype(BF)
    for to, copy in spread:
        pl.when(jnp.logical_not(in_first(to)))(copy.start)
    spread_land[c] = red[c]
    spread[0][1].wait_recv()
    relayed = [send(relay.at[0], spread_land.at[c_down], col=c_up)]
    spread[1][1].wait_recv()
    relayed.append(send(relay.at[1], spread_land.at[c_up], col=other(c_down)))
    for _, copy in spread[2:]:
        copy.wait_recv()
    for copy in relayed:
        copy.wait_recv()
    for n in range(RING):
        out_ref[d, :, LANES * n : LANES * n + LANES] = spread_land[n]

    def part(n, begin, size):
        return out_ref.at[n, pl.ds(begin, size)]

    def pass_on(n, begin, size, **target):
        return send(part(n, begin, size), part(n, begin, size), **target)

    pair = pass_on(d, 0, 64, depth=d_sib)
    b_up = pass_on(d, 64, 64, depth=d_up)
    b_down = pass_on(d, 64, 64, depth=d_down)
    b_pairs = [pass_on(d, 64, 64, depth=d_sib)]
    a_up = pass_on(d, 0, 64, depth=d_up)
    a_down = pass_on(d, 0, 64, depth=d_down)
    pair.wait_recv()
    a_up2 = pass_on(d_sib, 0, 64, depth=d_up)
    a_down2 = pass_on(d_sib, 0, 64, depth=d_down)
    b_up.wait_recv()
    b_up2 = pass_on(d_down, 96, 32, depth=d_up)
    b_pairs.append(pass_on(d_down, 64, 64, depth=d_sib))
    b_down.wait_recv()
    b_down2 = pass_on(d_up, 64, 32, depth=d_down)
    b_pairs.append(pass_on(d_up, 64, 64, depth=d_sib))
    a_up.wait_recv()
    a_up3 = pass_on(d_down, 32, 32, depth=d_up)
    a_down.wait_recv()
    a_down3 = pass_on(d_up, 0, 32, depth=d_down)
    b_up2.wait_recv()
    b_pairs.append(pass_on(d_far, 96, 32, depth=d_sib))
    b_down2.wait_recv()
    b_pairs.append(pass_on(d_far, 64, 32, depth=d_sib))
    a_up2.wait_recv()
    a_up4 = pass_on(other(d_down), 32, 32, depth=d_up)
    a_down2.wait_recv()
    a_down4 = pass_on(other(d_up), 0, 32, depth=d_down)
    for copy in (a_up3, a_down3, a_up4, a_down4, *b_pairs):
        copy.wait_recv()
    links.finish()


def on_device(half_slabs, virtuals, occupied_energy, virtual_energy, frequency):
    hbm = pl.BlockSpec(memory_space=pltpu.HBM)
    excitation = virtual_energy[None, :] - occupied_energy[:, None]
    weight = 4.0 * excitation / (excitation * excitation + frequency[0] * frequency[0])
    copies = 128
    gram = pl.pallas_call(
        gather_kernel,
        out_shape=jax.ShapeDtypeStruct((RING, 128, 1024), BF),
        in_specs=[hbm] * 3,
        out_specs=pl.BlockSpec(memory_space=pltpu.VMEM),
        scratch_shapes=[
            pltpu.VMEM((2, 500, LANES), BF),
            pltpu.VMEM((432, 500), BF),
            pltpu.VMEM((2, 432), F32),
            pltpu.VMEM((RING, 4, 432, LANES), BF),
            pltpu.VMEM((RING, 2, 512, LANES), BF),
            pltpu.VMEM((2, 432, LANES), F32),
            pltpu.VMEM((RING, 896, LANES), BF),
            pltpu.VMEM((LANES, 512), F32),
            pltpu.VMEM((2, 432, LANES), F32),
            pltpu.VMEM((896, LANES), BF),
            pltpu.VMEM((RING, 128, 384), BF),
            pltpu.VMEM((RING, 128, 512), BF),
            pltpu.VMEM((6, 2, 64, 640), BF),
            pltpu.VMEM((6, 2, 64, 640), BF),
            pltpu.VMEM((2, 2, 64, 640), F32),
            pltpu.VMEM((2, 128, 640), F32),
            pltpu.VMEM((128, 640), BF),
            pltpu.VMEM((128, 640), BF),
            pltpu.VMEM((4, 2, 128, 384), F32),
            pltpu.VMEM((6, 1, 64, 384), BF),
            pltpu.VMEM((6, 1, 64, 384), BF),
            pltpu.VMEM((2, 1, 64, 384), F32),
            pltpu.VMEM((1, 128, 384), F32),
            pltpu.VMEM((4, 128, 384), BF),
            pltpu.VMEM((4, 128, 384), BF),
            pltpu.VMEM((RING, 128, LANES), BF),
            pltpu.VMEM((RING, 128, LANES), BF),
            pltpu.VMEM((2, 128, LANES), BF),
            pltpu.SemaphoreType.DMA((3,)),
            pltpu.SemaphoreType.DMA((copies,)),
            pltpu.SemaphoreType.DMA((copies,)),
        ],
        compiler_params=pltpu.CompilerParams(
            collective_id=0, has_side_effects=True, vmem_limit_bytes=48 * 2**20
        ),
        cost_estimate=pl.CostEstimate(flops=2_700_000_000, bytes_accessed=3_000_000, transcendentals=0),
    )(half_slabs, virtuals.T, weight)
    return gram.reshape(1024, 1024).astype(F32)


def solution(mesh):
    placed = (P(None, "depth", ("row", "col")), P("col", "depth"), P(), P("depth"), P())
    return jax.shard_map(
        on_device, mesh=mesh, in_specs=placed, out_specs=P("row", "col"), check_vma=False
    )
```

```python
import jax
import jax.numpy as jnp
from jax import lax
from jax.experimental import pallas as pl
from jax.experimental.pallas import tpu as pltpu
from jax.sharding import PartitionSpec as P

MESH = pl.DeviceIdType.MESH
BF = jnp.bfloat16
F32 = jnp.float32
RING = 8
LANES = 128


class Links:
    def __init__(self, send_sems, recv_sems):
        self.send_sems, self.recv_sems, self.copies = send_sems, recv_sems, []

    def plan(self, src, dst, **target):
        at = len(self.copies)
        copy = pltpu.make_async_remote_copy(
            src_ref=src,
            dst_ref=dst,
            send_sem=self.send_sems.at[at],
            recv_sem=self.recv_sems.at[at],
            device_id=target,
            device_id_type=MESH,
        )
        self.copies.append(copy)
        return copy

    def send(self, src, dst, **target):
        copy = self.plan(src, dst, **target)
        copy.start()
        return copy

    def finish(self):
        for copy in self.copies:
            copy.wait_send()


def around(me):
    up, down, far = lax.rem(me + 2, RING), lax.rem(me + 6, RING), lax.rem(me + 4, RING)
    return up, down, far, me + 1 - 2 * lax.rem(me, 2)


def other(at):
    return at + 1 - 2 * lax.rem(at, 2)


def gather_kernel(
    slabs_ref, virt_ref, weight_ref, out_ref,
    slab_in, virt_in, weight_in, vq, hs, acc, rp, qp, wrow, wcol, wl,
    a_raw, a_land, a_keep, a_own, a_sib, a_last,
    b_raw, b_land, b_keep, b_own, b_sib, b_last, red,
    local_sems, send_sems, recv_sems,
):
    d, r, c = lax.axis_index("depth"), lax.axis_index("row"), lax.axis_index("col")
    d_up, d_down, d_far, d_sib = around(d)
    c_up, c_down, c_far, c_sib = around(c)
    r_up, r_down = lax.rem(r + 1, RING), lax.rem(r + 7, RING)
    links = Links(send_sems, recv_sems)
    send = links.send

    loads = [
        pltpu.make_async_copy(src, dst, local_sems.at[at])
        for at, (src, dst) in enumerate(((virt_ref, virt_in), (slabs_ref, slab_in), (weight_ref, weight_in)))
    ]
    for load in loads:
        load.start()
    barrier = pltpu.get_barrier_semaphore()
    partners = [{"depth": d_up}, {"depth": d_down}, {"depth": d_sib}, {"row": r_up}, {"row": r_down}]
    partners += [{"col": lax.rem(c + step, RING)} for step in range(1, RING)]
    for partner in partners:
        pl.semaphore_signal(barrier, inc=1, device_id=partner, device_id_type=MESH)

    nvir, nbas = virt_ref.shape
    vq[c, 3] = jnp.zeros((nvir, LANES), BF)
    for load in loads:
        load.wait()
    for quarter in range(3):
        vq[c, quarter] = virt_in[:, LANES * quarter : LANES * quarter + LANES]
    vq[c, 3, :, 0 : nbas - 384] = virt_in[:, 384:nbas]
    for orbital in range(2):
        hs[d, orbital, 496:512, :] = jnp.zeros((16, LANES), BF)
        hs[d, orbital, 0:nbas, :] = slab_in[orbital]

    pl.semaphore_wait(barrier, len(partners))

    j = lax.rem(r, 4)
    j_up, j_down = lax.rem(j + 1, 4), lax.rem(j + 3, 4)
    spans = (pl.ds(0, 208), pl.ds(208, 224))

    def slab(n, orbital, half=None, **target):
        piece = hs.at[n, orbital] if half is None else hs.at[n, orbital, pl.ds(256 * half, 256)]
        return send(piece, piece, **target)

    def virt(n, quarter, half, **target):
        piece = vq.at[n, quarter, spans[half]]
        return send(piece, piece, **target)

    def virt_rows(n, half):
        return virt(n, j, half, row=r_up), virt(n, j, half, row=r_down)

    pair, up, down, up2, down2, up3, down3, up4, down4 = ({} for _ in range(9))

    def slabs_out(o):
        up[o], down[o] = slab(d, o, depth=d_up), slab(d, o, depth=d_down)

    def slabs_sib(o):
        pair[o].wait_recv()
        up2[o], down2[o] = slab(d_sib, o, depth=d_up), slab(d_sib, o, depth=d_down)

    def slabs_on(o):
        up[o].wait_recv()
        up3[o] = slab(d_down, o, 1, depth=d_up)
        down[o].wait_recv()
        down3[o] = slab(d_up, o, 0, depth=d_down)

    def slabs_sib_on(o):
        up2[o].wait_recv()
        up4[o] = slab(other(d_down), o, 1, depth=d_up)
        down2[o].wait_recv()
        down4[o] = slab(other(d_up), o, 0, depth=d_down)

    def slabs_end(o):
        for copy in (up3[o], down3[o], up4[o], down4[o]):
            copy.wait_recv()

    z_up = {1: virt(c, j, 1, col=c_up)}
    z_down = {0: virt(c, j, 0, col=c_down)}
    z_up[0] = virt(c, j, 0, col=c_up)
    z_down[1] = virt(c, j, 1, col=c_down)
    slabs_out(0)
    pair[0] = slab(d, 0, depth=d_sib)
    share_own = send(vq.at[c], vq.at[c], col=c_sib)

    rows_a, rows_b, rows_c = {}, {}, {}
    z_up[1].wait_recv()
    z_up2 = virt(c_down, j, 1, col=c_up)
    rows_a[1] = virt_rows(c_down, 1)
    z_down[0].wait_recv()
    z_down2 = virt(c_up, j, 0, col=c_down)
    rows_b[0] = virt_rows(c_up, 0)
    z_up[0].wait_recv()
    rows_a[0] = virt_rows(c_down, 0)
    z_down[1].wait_recv()
    rows_b[1] = virt_rows(c_up, 1)
    slabs_sib(0)
    slabs_on(0)
    z_up2.wait_recv()
    rows_c[1] = virt_rows(c_far, 1)
    z_down2.wait_recv()
    rows_c[0] = virt_rows(c_far, 0)
    pair[1] = slab(d, 1, depth=d_sib)
    slabs_out(1)

    def pass_up(n, rows):
        rows[1][0].wait_recv()
        return virt(n, j_down, 1, row=r_up)

    def pass_down(n, rows):
        rows[0][1].wait_recv()
        return virt(n, j_up, 0, row=r_down)

    on_a = [pass_up(c_down, rows_a)]
    on_b = [pass_down(c_up, rows_b)]
    on_a.append(pass_down(c_down, rows_a))
    on_b.append(pass_up(c_up, rows_b))
    slabs_sib_on(0)
    on_c = [pass_up(c_far, rows_c), pass_down(c_far, rows_c)]
    slabs_sib(1)
    slabs_on(1)

    wrow[...] = jnp.zeros_like(wrow)
    for orbital in range(2):
        wrow[:, 0:nvir] = jnp.broadcast_to(weight_in[orbital : orbital + 1, :], (LANES, nvir))
        wcol[orbital] = wrow[...].T[0:nvir, :]
    acc[...] = jnp.zeros_like(acc)

    def virt_end(n, rows, on):
        for copy in (rows[0][0], rows[1][1], *on):
            copy.wait_recv()
        return send(vq.at[n], vq.at[n], col=c_sib)

    def couple(n, orbital):
        left = jnp.concatenate([vq[n, 0], vq[n, 1], vq[n, 2], vq[n, 3]], axis=1)
        acc[orbital] += jnp.dot(left, hs[n, orbital], preferred_element_type=F32)

    share_a = virt_end(c_down, rows_a, on_a)
    share_b = virt_end(c_up, rows_b, on_b)
    slabs_end(0)
    couple(c, 0)
    share_own.wait_recv()
    couple(c_sib, 0)
    couple(c_down, 0)
    couple(c_up, 0)
    share_c = virt_end(c_far, rows_c, on_c)
    slabs_sib_on(1)
    share_a.wait_recv()
    couple(other(c_down), 0)
    share_b.wait_recv()
    couple(other(c_up), 0)
    couple(c_far, 0)
    share_c.wait_recv()
    couple(other(c_far), 0)

    def panel(n, orbital, **target):
        return send(rp.at[n, orbital], rp.at[n, orbital], **target)

    y_up, y_down, z_up, z_down = {}, {}, {}, {}
    share_own, share_down, share_up, share_far = {}, {}, {}, {}

    def panels_out(o):
        rp[c, o] = acc[o].astype(BF)
        y_up[1, o] = send(rp.at[c, o], qp.at[1, o], row=r_up)
        y_down[1, o] = send(rp.at[c, o], qp.at[2, o], row=r_down)
        z_up[o] = panel(c, o, col=c_up)
        z_down[o] = panel(c, o, col=c_down)
        share_own[o] = panel(c, o, col=c_sib)
        qp[0, o] = rp[c, o]

    def y_step(step, o):
        slot = 2 * step - 1
        y_up[step, o].wait_recv()
        y_up[step + 1, o] = send(qp.at[slot, o], qp.at[slot + 2, o], row=r_up)
        y_down[step, o].wait_recv()
        y_down[step + 1, o] = send(qp.at[slot + 1, o], qp.at[slot + 3, o], row=r_down)

    def z_step(o):
        z_up[o].wait_recv()
        if o == 1:
            z_up["far"] = panel(c_down, 1, col=c_up)
        share_down[o] = panel(c_down, o, col=c_sib)
        z_down[o].wait_recv()
        if o == 0:
            z_down["far"] = panel(c_up, 0, col=c_down)
        share_up[o] = panel(c_up, o, col=c_sib)

    def weigh(n, o):
        product = wcol[o] * rp[n, o].astype(F32)
        wl[o, n] = product.astype(BF).T

    panels_out(0)
    slabs_end(1)

    @pl.loop(0, RING)
    def _(n):
        couple(n, 1)

    panels_out(1)
    y_step(1, 0)
    z_step(0)
    weigh(c, 0)
    weigh(c, 1)
    y_step(1, 1)
    z_step(1)
    share_own[0].wait_recv()
    weigh(c_sib, 0)
    weigh(c_down, 0)
    y_step(2, 0)
    weigh(c_up, 0)
    z_down["far"].wait_recv()
    share_far[0] = panel(c_far, 0, col=c_sib)
    share_own[1].wait_recv()
    weigh(c_sib, 1)
    y_step(2, 1)
    weigh(c_down, 1)
    z_up["far"].wait_recv()
    share_far[1] = panel(c_far, 1, col=c_sib)
    weigh(c_up, 1)
    weigh(c_far, 0)
    for n, share in ((other(c_down), share_down), (other(c_up), share_up)):
        share[0].wait_recv()
        weigh(n, 0)
    y_down[3, 0].wait_recv()
    y_down[4, 0] = send(qp.at[6, 0], qp.at[7, 0], row=r_down)
    for n, share in ((other(c_down), share_down), (other(c_up), share_up)):
        share[1].wait_recv()
        weigh(n, 1)
    y_up[3, 1].wait_recv()
    y_up[4, 1] = send(qp.at[5, 1], qp.at[7, 1], row=r_up)
    weigh(c_far, 1)
    for o in range(2):
        share_far[o].wait_recv()
        weigh(other(c_far), o)

    low, high = slice(0, 64), slice(64, 128)
    targets = {"far": d_far, "up": d_up, "down": d_down, "own": d}

    def terms_of(name, slots):
        terms = 0.0
        for o in range(2):
            rows = wl[o, pl.ds(2 * (targets[name] // 2), 2)].reshape(256, 432)
            columns = jnp.concatenate([qp[slot, o] for slot in slots], axis=1)
            terms += jnp.dot(rows, columns, preferred_element_type=F32)
        return terms.reshape(2, 128, LANES * len(slots))

    class RingSum:
        def __init__(self, raw, land, keep, own):
            self.raw, self.land, self.keep, self.own, self.copies = raw, land, keep, own, {}

        def send(self, at, value, **target):
            self.raw[at] = value.astype(BF)
            self.copies[at] = send(self.raw.at[at], self.land.at[at], **target)

        def give(self, name, block):
            if name == "far":
                self.send(0, block[:, high], depth=d_up)
                self.send(1, block[:, low], depth=d_down)
            elif name == "up":
                self.send(2, block[:, low], depth=d_up)
                self.keep[0] = block[:, high]
            elif name == "down":
                self.send(3, block[:, high], depth=d_down)
                self.keep[1] = block[:, low]
            else:
                self.own[...] = block

        def pass_on(self):
            for at, target in ((0, d_up), (1, d_down)):
                self.copies[at].wait_recv()
                self.send(at + 4, self.keep[at] + self.land[at].astype(F32), depth=target)

        def end(self):
            for at in (2, 3, 4, 5):
                self.copies[at].wait_recv()
            land = self.land
            self.own[:, low] = self.own[:, low] + land[2].astype(F32) + land[5].astype(F32)
            self.own[:, high] = self.own[:, high] + land[3].astype(F32) + land[4].astype(F32)

    plane = lax.rem(d, 2)
    slots_a, slots_b = (0, 1, 2, 3, 4), (5, 6, 7)
    ring_a = RingSum(a_raw, a_land, a_keep, a_own)
    ring_b = RingSum(b_raw, b_land, b_keep, b_own)
    for name in targets:
        ring_a.give(name, terms_of(name, slots_a))
    y_up[3, 0].wait_recv()
    y_down[3, 1].wait_recv()
    y_up[4, 1].wait_recv()
    y_down[4, 0].wait_recv()
    ring_a.pass_on()
    for name in targets:
        ring_b.give(name, terms_of(name, slots_b))
    ring_a.end()
    a_sib[...] = a_own[1 - plane].astype(BF)
    last = send(a_sib, a_last, depth=d_sib)
    ring_b.pass_on()

    rows_of = [r, r_down, r_up, *(lax.rem(r + step, RING) for step in (6, 2, 5, 3, 4))]

    def tile(at):
        return pl.ds(pl.multiple_of(at * LANES, LANES), LANES)

    def in_first(at):
        apart = lax.rem(at - r + RING, RING)
        return jnp.logical_or(apart <= 2, apart >= 6)

    last.wait_recv()
    total = (a_own[plane] + a_last[...].astype(F32)).astype(BF)
    for at, slot in enumerate(slots_a):
        red[rows_of[slot]] = total[:, LANES * at : LANES * at + LANES]
    spread = []
    for step in (4, 2, 6, 3, 5, 1, 7):
        to = lax.rem(c + step, RING)
        copy = links.plan(red.at[to], out_ref.at[d, :, tile(c)], col=to)
        spread.append((to, copy))
        pl.when(in_first(to))(copy.start)
    ring_b.end()
    b_sib[...] = b_own[1 - plane].astype(BF)
    last = send(b_sib, b_last, depth=d_sib)
    last.wait_recv()
    total = (b_own[plane] + b_last[...].astype(F32)).astype(BF)
    for at, slot in enumerate(slots_b):
        red[rows_of[slot]] = total[:, LANES * at : LANES * at + LANES]
    for to, copy in spread:
        pl.when(jnp.logical_not(in_first(to)))(copy.start)
    out_ref[d, :, tile(c)] = red[c]
    for _, copy in spread:
        copy.wait_recv()

    def part(n, begin, size):
        return out_ref.at[n, pl.ds(begin, size)]

    def pass_on(n, begin, size, **target):
        return send(part(n, begin, size), part(n, begin, size), **target)

    pair = pass_on(d, 0, 96, depth=d_sib)
    b_up = pass_on(d, 96, 32, depth=d_up)
    b_down = pass_on(d, 96, 32, depth=d_down)
    b_pairs = [pass_on(d, 96, 32, depth=d_sib)]
    a_up = pass_on(d, 0, 96, depth=d_up)
    a_down = pass_on(d, 0, 96, depth=d_down)
    pair.wait_recv()
    a_up2 = pass_on(d_sib, 0, 96, depth=d_up)
    a_down2 = pass_on(d_sib, 0, 96, depth=d_down)
    b_up.wait_recv()
    b_up2 = pass_on(d_down, 112, 16, depth=d_up)
    b_pairs.append(pass_on(d_down, 96, 32, depth=d_sib))
    b_down.wait_recv()
    b_down2 = pass_on(d_up, 96, 16, depth=d_down)
    b_pairs.append(pass_on(d_up, 96, 32, depth=d_sib))
    a_up.wait_recv()
    a_up3 = pass_on(d_down, 48, 48, depth=d_up)
    a_down.wait_recv()
    a_down3 = pass_on(d_up, 0, 48, depth=d_down)
    b_up2.wait_recv()
    b_pairs.append(pass_on(d_far, 112, 16, depth=d_sib))
    b_down2.wait_recv()
    b_pairs.append(pass_on(d_far, 96, 16, depth=d_sib))
    a_up2.wait_recv()
    a_up4 = pass_on(other(d_down), 48, 48, depth=d_up)
    a_down2.wait_recv()
    a_down4 = pass_on(other(d_up), 0, 48, depth=d_down)
    for copy in (a_up3, a_down3, a_up4, a_down4, *b_pairs):
        copy.wait_recv()
    links.finish()


def on_device(half_slabs, virtuals, occupied_energy, virtual_energy, frequency):
    hbm = pl.BlockSpec(memory_space=pltpu.HBM)
    excitation = virtual_energy[None, :] - occupied_energy[:, None]
    weight = 4.0 * excitation / (excitation * excitation + frequency[0] * frequency[0])
    copies = 128
    gram = pl.pallas_call(
        gather_kernel,
        out_shape=jax.ShapeDtypeStruct((RING, 128, 1024), BF),
        in_specs=[hbm] * 3,
        out_specs=pl.BlockSpec(memory_space=pltpu.VMEM),
        scratch_shapes=[
            pltpu.VMEM((2, 500, LANES), BF),
            pltpu.VMEM((432, 500), BF),
            pltpu.VMEM((2, 432), F32),
            pltpu.VMEM((RING, 4, 432, LANES), BF),
            pltpu.VMEM((RING, 2, 512, LANES), BF),
            pltpu.VMEM((2, 432, LANES), F32),
            pltpu.VMEM((RING, 2, 432, LANES), BF),
            pltpu.VMEM((RING, 2, 432, LANES), BF),
            pltpu.VMEM((LANES, 512), F32),
            pltpu.VMEM((2, 432, LANES), F32),
            pltpu.VMEM((2, RING, 128, 432), BF),
            pltpu.VMEM((6, 2, 64, 640), BF),
            pltpu.VMEM((6, 2, 64, 640), BF),
            pltpu.VMEM((2, 2, 64, 640), F32),
            pltpu.VMEM((2, 128, 640), F32),
            pltpu.VMEM((128, 640), BF),
            pltpu.VMEM((128, 640), BF),
            pltpu.VMEM((6, 2, 64, 384), BF),
            pltpu.VMEM((6, 2, 64, 384), BF),
            pltpu.VMEM((2, 2, 64, 384), F32),
            pltpu.VMEM((2, 128, 384), F32),
            pltpu.VMEM((128, 384), BF),
            pltpu.VMEM((128, 384), BF),
            pltpu.VMEM((RING, 128, LANES), BF),
            pltpu.SemaphoreType.DMA((3,)),
            pltpu.SemaphoreType.DMA((copies,)),
            pltpu.SemaphoreType.DMA((copies,)),
        ],
        compiler_params=pltpu.CompilerParams(
            collective_id=0, has_side_effects=True, vmem_limit_bytes=48 * 2**20
        ),
        cost_estimate=pl.CostEstimate(flops=2_700_000_000, bytes_accessed=3_000_000, transcendentals=0),
    )(half_slabs, virtuals.T, weight)
    return gram.reshape(1024, 1024).astype(F32)


def solution(mesh):
    placed = (P(None, "depth", ("row", "col")), P("col", "depth"), P(), P("depth"), P())
    return jax.shard_map(
        on_device, mesh=mesh, in_specs=placed, out_specs=P("row", "col"), check_vma=False
    )
```

```python
import jax
import jax.numpy as jnp
from jax import lax
from jax.experimental import pallas as pl
from jax.experimental.pallas import tpu as pltpu
from jax.sharding import PartitionSpec as P

MESH = pl.DeviceIdType.MESH
BF = jnp.bfloat16
F32 = jnp.float32
RING = 8
LANES = 128


class Links:
    def __init__(self, here, send_sems, recv_sems):
        self.here, self.send_sems, self.recv_sems = here, send_sems, recv_sems
        self.copies, self.retired = [], 0

    def place(self, **target):
        at = {**self.here, **target}
        return at["depth"], at["row"], at["col"]

    def plan(self, src, dst, **target):
        at = len(self.copies)
        copy = pltpu.make_async_remote_copy(
            src_ref=src,
            dst_ref=dst,
            send_sem=self.send_sems.at[at],
            recv_sem=self.recv_sems.at[at],
            device_id=self.place(**target),
            device_id_type=MESH,
        )
        self.copies.append(copy)
        return copy

    def send(self, src, dst, **target):
        copy = self.plan(src, dst, **target)
        copy.start()
        return copy

    def retire(self, upto=None):
        for copy in self.copies[self.retired : upto]:
            copy.wait_send()
        self.retired = len(self.copies) if upto is None else upto


def around(me):
    up, down, far = lax.rem(me + 2, RING), lax.rem(me + 6, RING), lax.rem(me + 4, RING)
    return up, down, far, me + 1 - 2 * lax.rem(me, 2)


def other(at):
    return at + 1 - 2 * lax.rem(at, 2)


def gather_kernel(
    slabs_ref, virt_ref, weight_ref, out_ref,
    slab_in, virt_in, weight_in, vq, hs, acc, rp, qp, wrow, wcol, wl,
    a_raw, a_land, a_keep, a_own, a_sib, a_last,
    b_terms, b_raw, b_land, b_keep, b_own, b_give, b_take, red,
    local_sems, send_sems, recv_sems,
):
    d, r, c = lax.axis_index("depth"), lax.axis_index("row"), lax.axis_index("col")
    d_up, d_down, d_far, d_sib = around(d)
    c_up, c_down, c_far, c_sib = around(c)
    r_up, r_down = lax.rem(r + 1, RING), lax.rem(r + 7, RING)
    links = Links({"depth": d, "row": r, "col": c}, send_sems, recv_sems)
    send = links.send

    loads = [
        pltpu.make_async_copy(src, dst, local_sems.at[at])
        for at, (src, dst) in enumerate(((virt_ref, virt_in), (slabs_ref, slab_in), (weight_ref, weight_in)))
    ]
    for load in loads:
        load.start()
    barrier = pltpu.get_barrier_semaphore()
    c_far_sib, c_up_sib, c_down_sib = other(c_far), other(c_up), other(c_down)
    partners = [links.place(depth=to) for to in (d_up, d_down, d_sib)]
    partners += [links.place(row=to) for to in (r_up, r_down)]
    partners += [links.place(col=to) for to in (c_up, c_down, c_far, c_sib, c_up_sib, c_down_sib, c_far_sib)]
    for partner in partners:
        pl.semaphore_signal(barrier, inc=1, device_id=partner, device_id_type=MESH)

    nvir, nbas = virt_ref.shape
    vq[c, 3] = jnp.zeros((nvir, LANES), BF)
    for load in loads:
        load.wait()
    for quarter in range(3):
        vq[c, quarter] = virt_in[:, LANES * quarter : LANES * quarter + LANES]
    vq[c, 3, :, 0 : nbas - 384] = virt_in[:, 384:nbas]
    for orbital in range(2):
        hs[d, orbital, 496:512, :] = jnp.zeros((16, LANES), BF)
        hs[d, orbital, 0:nbas, :] = slab_in[orbital]

    pl.semaphore_wait(barrier, len(partners))

    j = lax.rem(r, 4)
    j_up, j_down = lax.rem(j + 1, 4), lax.rem(j + 3, 4)
    spans = (pl.ds(0, 208), pl.ds(208, 224))

    def slab(n, orbital, half=None, **target):
        piece = hs.at[n, orbital] if half is None else hs.at[n, orbital, pl.ds(256 * half, 256)]
        return send(piece, piece, **target)

    def virt(n, quarter, half, **target):
        piece = vq.at[n, quarter, spans[half]]
        return send(piece, piece, **target)

    def virt_rows(n, half):
        return virt(n, j, half, row=r_up), virt(n, j, half, row=r_down)

    pair, up, down, up2, down2, up3, down3, up4, down4 = ({} for _ in range(9))

    def slabs_out(o):
        up[o], down[o] = slab(d, o, depth=d_up), slab(d, o, depth=d_down)

    def slabs_sib(o):
        pair[o].wait_recv()
        up2[o], down2[o] = slab(d_sib, o, depth=d_up), slab(d_sib, o, depth=d_down)

    def slabs_on(o):
        up[o].wait_recv()
        up3[o] = slab(d_down, o, 1, depth=d_up)
        down[o].wait_recv()
        down3[o] = slab(d_up, o, 0, depth=d_down)

    def slabs_sib_on(o):
        up2[o].wait_recv()
        up4[o] = slab(other(d_down), o, 1, depth=d_up)
        down2[o].wait_recv()
        down4[o] = slab(other(d_up), o, 0, depth=d_down)

    def slabs_end(o):
        for copy in (up3[o], down3[o], up4[o], down4[o]):
            copy.wait_recv()

    z_up = {1: virt(c, j, 1, col=c_up)}
    z_down = {0: virt(c, j, 0, col=c_down)}
    z_up[0] = virt(c, j, 0, col=c_up)
    z_down[1] = virt(c, j, 1, col=c_down)
    slabs_out(0)
    pair[0] = slab(d, 0, depth=d_sib)
    share_own = send(vq.at[c], vq.at[c], col=c_sib)

    rows_a, rows_b, rows_c = {}, {}, {}
    z_up[1].wait_recv()
    z_up2 = virt(c_down, j, 1, col=c_up)
    rows_a[1] = virt_rows(c_down, 1)
    z_down[0].wait_recv()
    z_down2 = virt(c_up, j, 0, col=c_down)
    rows_b[0] = virt_rows(c_up, 0)
    z_up[0].wait_recv()
    rows_a[0] = virt_rows(c_down, 0)
    z_down[1].wait_recv()
    rows_b[1] = virt_rows(c_up, 1)
    slabs_sib(0)
    slabs_on(0)
    z_up2.wait_recv()
    rows_c[1] = virt_rows(c_far, 1)
    z_down2.wait_recv()
    rows_c[0] = virt_rows(c_far, 0)
    pair[1] = slab(d, 1, depth=d_sib)
    slabs_out(1)

    def pass_up(n, rows):
        rows[1][0].wait_recv()
        return virt(n, j_down, 1, row=r_up)

    def pass_down(n, rows):
        rows[0][1].wait_recv()
        return virt(n, j_up, 0, row=r_down)

    on_a = [pass_up(c_down, rows_a)]
    on_b = [pass_down(c_up, rows_b)]
    on_a.append(pass_down(c_down, rows_a))
    on_b.append(pass_up(c_up, rows_b))
    slabs_sib_on(0)
    on_c = [pass_up(c_far, rows_c), pass_down(c_far, rows_c)]
    slabs_sib(1)
    slabs_on(1)

    wrow[...] = jnp.zeros_like(wrow)
    for orbital in range(2):
        wrow[:, 0:nvir] = jnp.broadcast_to(weight_in[orbital : orbital + 1, :], (LANES, nvir))
        wcol[orbital] = wrow[...].T[0:nvir, :]
    acc[...] = jnp.zeros_like(acc)

    def virt_end(n, rows, on):
        for copy in (rows[0][0], rows[1][1], *on):
            copy.wait_recv()
        return send(vq.at[n], vq.at[n], col=c_sib)

    def couple(n, orbital):
        left = jnp.concatenate([vq[n, 0], vq[n, 1], vq[n, 2], vq[n, 3]], axis=1)
        acc[orbital] += jnp.dot(left, hs[n, orbital], preferred_element_type=F32)

    share_a = virt_end(c_down, rows_a, on_a)
    share_b = virt_end(c_up, rows_b, on_b)
    slabs_end(0)
    couple(c, 0)
    share_own.wait_recv()
    couple(c_sib, 0)
    couple(c_down, 0)
    couple(c_up, 0)
    share_c = virt_end(c_far, rows_c, on_c)
    slabs_sib_on(1)
    share_a.wait_recv()
    couple(other(c_down), 0)
    share_b.wait_recv()
    couple(other(c_up), 0)
    couple(c_far, 0)
    share_c.wait_recv()
    couple(other(c_far), 0)

    def panel(n, orbital, **target):
        return send(rp.at[n, orbital], rp.at[n, orbital], **target)

    y_up, y_down, z_up, z_down = {}, {}, {}, {}
    share_own, share_down, share_up, share_far = {}, {}, {}, {}

    def panels_out(o):
        rp[c, o] = acc[o].astype(BF)
        y_up[1, o] = send(rp.at[c, o], qp.at[1, o], row=r_up)
        y_down[1, o] = send(rp.at[c, o], qp.at[2, o], row=r_down)
        z_up[o] = panel(c, o, col=c_up)
        z_down[o] = panel(c, o, col=c_down)
        share_own[o] = panel(c, o, col=c_sib)
        qp[0, o] = rp[c, o]

    def y_step(step, o):
        slot = 2 * step - 1
        y_up[step, o].wait_recv()
        y_up[step + 1, o] = send(qp.at[slot, o], qp.at[slot + 2, o], row=r_up)
        y_down[step, o].wait_recv()
        y_down[step + 1, o] = send(qp.at[slot + 1, o], qp.at[slot + 3, o], row=r_down)

    def z_step(o):
        z_up[o].wait_recv()
        if o == 1:
            z_up["far"] = panel(c_down, 1, col=c_up)
        share_down[o] = panel(c_down, o, col=c_sib)
        z_down[o].wait_recv()
        if o == 0:
            z_down["far"] = panel(c_up, 0, col=c_down)
        share_up[o] = panel(c_up, o, col=c_sib)

    def weigh(n, o):
        product = wcol[o] * rp[n, o].astype(F32)
        wl[o, n] = product.astype(BF).T

    panels_out(0)
    slabs_end(1)

    @pl.loop(0, RING)
    def _(n):
        couple(n, 1)

    panels_out(1)
    first_stage = len(links.copies)
    y_step(1, 0)
    z_step(0)
    weigh(c, 0)
    weigh(c, 1)
    y_step(1, 1)
    links.retire(24)
    z_step(1)
    share_own[0].wait_recv()
    weigh(c_sib, 0)
    weigh(c_down, 0)
    y_step(2, 0)
    weigh(c_up, 0)
    links.retire(40)
    z_down["far"].wait_recv()
    share_far[0] = panel(c_far, 0, col=c_sib)
    share_own[1].wait_recv()
    weigh(c_sib, 1)
    y_step(2, 1)
    weigh(c_down, 1)
    z_up["far"].wait_recv()
    share_far[1] = panel(c_far, 1, col=c_sib)
    weigh(c_up, 1)
    weigh(c_far, 0)
    for n, share in ((other(c_down), share_down), (other(c_up), share_up)):
        share[0].wait_recv()
        weigh(n, 0)
    y_down[3, 0].wait_recv()
    y_down[4, 0] = send(qp.at[6, 0], qp.at[7, 0], row=r_down)
    for n, share in ((other(c_down), share_down), (other(c_up), share_up)):
        share[1].wait_recv()
        weigh(n, 1)
    y_up[3, 1].wait_recv()
    y_up[4, 1] = send(qp.at[5, 1], qp.at[7, 1], row=r_up)
    weigh(c_far, 1)
    for o in range(2):
        share_far[o].wait_recv()
        weigh(other(c_far), o)

    low, high = slice(0, 64), slice(64, 128)
    targets = {"far": d_far, "up": d_up, "down": d_down, "own": d}

    def terms_of(name, slots):
        terms = 0.0
        for o in range(2):
            rows = wl[o, pl.ds(2 * (targets[name] // 2), 2)].reshape(256, 432)
            columns = jnp.concatenate([qp[slot, o] for slot in slots], axis=1)
            terms += jnp.dot(rows, columns, preferred_element_type=F32)
        return terms.reshape(2, 128, LANES * len(slots))

    class RingSum:
        def __init__(self, raw, land, keep, own):
            self.raw, self.land, self.keep, self.own, self.copies = raw, land, keep, own, {}

        def send(self, at, value, **target):
            self.raw[at] = value.astype(BF)
            self.copies[at] = send(self.raw.at[at], self.land.at[at], **target)

        def give(self, name, block):
            if name == "far":
                self.send(0, block[:, high], depth=d_up)
                self.send(1, block[:, low], depth=d_down)
            elif name == "up":
                self.send(2, block[:, low], depth=d_up)
                self.keep[0] = block[:, high]
            elif name == "down":
                self.send(3, block[:, high], depth=d_down)
                self.keep[1] = block[:, low]
            else:
                self.own[...] = block

        def pass_on(self):
            for at, target in ((0, d_up), (1, d_down)):
                self.copies[at].wait_recv()
                self.send(at + 4, self.keep[at] + self.land[at].astype(F32), depth=target)

        def end(self):
            for at in (2, 3, 4, 5):
                self.copies[at].wait_recv()
            land = self.land
            self.own[:, low] = self.own[:, low] + land[2].astype(F32) + land[5].astype(F32)
            self.own[:, high] = self.own[:, high] + land[3].astype(F32) + land[4].astype(F32)

    plane = lax.rem(d, 2)
    slots_a, slots_b = (0, 1, 2, 3, 4), (5, 6, 7)
    ring_a = RingSum(a_raw, a_land, a_keep, a_own)
    ring_b = RingSum(b_raw, b_land, b_keep, b_own)
    for name in targets:
        ring_a.give(name, terms_of(name, slots_a))
    y_up[3, 0].wait_recv()
    y_down[3, 1].wait_recv()
    y_up[4, 1].wait_recv()
    y_down[4, 0].wait_recv()
    b_pair = {}
    for at, name in enumerate(targets):
        b_terms[at] = terms_of(name, slots_b)
        b_give[at] = b_terms[at, 1 - plane].astype(BF)
        b_pair[name] = send(b_give.at[at], b_take.at[at], depth=d_sib)
        if at == 0:
            ring_a.pass_on()
    links.retire(first_stage)
    for at, name in enumerate(targets):
        b_pair[name].wait_recv()
        ring_b.give(name, (b_terms[at, plane] + b_take[at].astype(F32))[None])
    ring_a.end()
    a_sib[...] = a_own[1 - plane].astype(BF)
    last = send(a_sib, a_last, depth=d_sib)
    ring_b.pass_on()

    rows_of = [r, r_down, r_up, *(lax.rem(r + step, RING) for step in (6, 2, 5, 3, 4))]

    def tile(at):
        return pl.ds(pl.multiple_of(at * LANES, LANES), LANES)

    def in_first(at):
        apart = lax.rem(at - r + RING, RING)
        return jnp.logical_or(apart <= 2, apart >= 6)

    links.retire(len(links.copies) - 4)
    last.wait_recv()
    total = (a_own[plane] + a_last[...].astype(F32)).astype(BF)
    for at, slot in enumerate(slots_a):
        red[rows_of[slot]] = total[:, LANES * at : LANES * at + LANES]
    spread = []
    for to in (c_far, c_far_sib, c_up, c_down, c_up_sib, c_down_sib, c_sib):
        copy = links.plan(red.at[to], out_ref.at[d, :, tile(c)], col=to)
        spread.append((to, copy))
        pl.when(in_first(to))(copy.start)
    ring_b.end()
    for at, slot in enumerate(slots_b):
        red[rows_of[slot]] = b_own[0, :, LANES * at : LANES * at + LANES].astype(BF)
    for to, copy in spread:
        pl.when(jnp.logical_not(in_first(to)))(copy.start)
    out_ref[d, :, tile(c)] = red[c]
    links.retire(len(links.copies) - 7)
    for _, copy in spread:
        copy.wait_recv()

    def part(n, begin, size):
        return out_ref.at[n, pl.ds(begin, size)]

    def pass_on(n, begin, size, **target):
        return send(part(n, begin, size), part(n, begin, size), **target)

    pair = pass_on(d, 0, 64, depth=d_sib)
    b_up = pass_on(d, 64, 64, depth=d_up)
    b_down = pass_on(d, 64, 64, depth=d_down)
    b_pairs = [pass_on(d, 64, 64, depth=d_sib)]
    a_up = pass_on(d, 0, 64, depth=d_up)
    a_down = pass_on(d, 0, 64, depth=d_down)
    links.retire(len(links.copies) - 6)
    pair.wait_recv()
    a_up2 = pass_on(d_sib, 0, 64, depth=d_up)
    a_down2 = pass_on(d_sib, 0, 64, depth=d_down)
    b_up.wait_recv()
    b_up2 = pass_on(d_down, 96, 32, depth=d_up)
    b_pairs.append(pass_on(d_down, 64, 64, depth=d_sib))
    b_down.wait_recv()
    b_down2 = pass_on(d_up, 64, 32, depth=d_down)
    b_pairs.append(pass_on(d_up, 64, 64, depth=d_sib))
    a_up.wait_recv()
    a_up3 = pass_on(d_down, 32, 32, depth=d_up)
    a_down.wait_recv()
    a_down3 = pass_on(d_up, 0, 32, depth=d_down)
    b_up2.wait_recv()
    b_pairs.append(pass_on(d_far, 96, 32, depth=d_sib))
    b_down2.wait_recv()
    b_pairs.append(pass_on(d_far, 64, 32, depth=d_sib))
    a_up2.wait_recv()
    a_up4 = pass_on(other(d_down), 32, 32, depth=d_up)
    a_down2.wait_recv()
    a_down4 = pass_on(other(d_up), 0, 32, depth=d_down)
    links.retire(len(links.copies) - 6)
    for copy in (a_up3, a_down3, a_up4, a_down4, *b_pairs):
        copy.wait_recv()
    links.retire()


def on_device(half_slabs, virtuals, occupied_energy, virtual_energy, frequency):
    hbm = pl.BlockSpec(memory_space=pltpu.HBM)
    excitation = virtual_energy[None, :] - occupied_energy[:, None]
    weight = 4.0 * excitation / (excitation * excitation + frequency[0] * frequency[0])
    copies = 128
    gram = pl.pallas_call(
        gather_kernel,
        out_shape=jax.ShapeDtypeStruct((RING, 128, 1024), BF),
        in_specs=[hbm] * 3,
        out_specs=pl.BlockSpec(memory_space=pltpu.VMEM),
        scratch_shapes=[
            pltpu.VMEM((2, 500, LANES), BF),
            pltpu.VMEM((432, 500), BF),
            pltpu.VMEM((2, 432), F32),
            pltpu.VMEM((RING, 4, 432, LANES), BF),
            pltpu.VMEM((RING, 2, 512, LANES), BF),
            pltpu.VMEM((2, 432, LANES), F32),
            pltpu.VMEM((RING, 2, 432, LANES), BF),
            pltpu.VMEM((RING, 2, 432, LANES), BF),
            pltpu.VMEM((LANES, 512), F32),
            pltpu.VMEM((2, 432, LANES), F32),
            pltpu.VMEM((2, RING, 128, 432), BF),
            pltpu.VMEM((6, 2, 64, 640), BF),
            pltpu.VMEM((6, 2, 64, 640), BF),
            pltpu.VMEM((2, 2, 64, 640), F32),
            pltpu.VMEM((2, 128, 640), F32),
            pltpu.VMEM((128, 640), BF),
            pltpu.VMEM((128, 640), BF),
            pltpu.VMEM((4, 2, 128, 384), F32),
            pltpu.VMEM((6, 1, 64, 384), BF),
            pltpu.VMEM((6, 1, 64, 384), BF),
            pltpu.VMEM((2, 1, 64, 384), F32),
            pltpu.VMEM((1, 128, 384), F32),
            pltpu.VMEM((4, 128, 384), BF),
            pltpu.VMEM((4, 128, 384), BF),
            pltpu.VMEM((RING, 128, LANES), BF),
            pltpu.SemaphoreType.DMA((3,)),
            pltpu.SemaphoreType.DMA((copies,)),
            pltpu.SemaphoreType.DMA((copies,)),
        ],
        compiler_params=pltpu.CompilerParams(
            collective_id=0, has_side_effects=True, vmem_limit_bytes=48 * 2**20
        ),
        cost_estimate=pl.CostEstimate(flops=2_700_000_000, bytes_accessed=3_000_000, transcendentals=0),
    )(half_slabs, virtuals.T, weight)
    return gram.reshape(1024, 1024).astype(F32)


def solution(mesh):
    placed = (P(None, "depth", ("row", "col")), P("col", "depth"), P(), P("depth"), P())
    return jax.shard_map(
        on_device, mesh=mesh, in_specs=placed, out_specs=P("row", "col"), check_vma=False
    )
```

```python
import jax
import jax.numpy as jnp
from jax import lax
from jax.experimental import pallas as pl
from jax.experimental.pallas import tpu as pltpu
from jax.sharding import PartitionSpec as P

MESH = pl.DeviceIdType.MESH
BF = jnp.bfloat16
F32 = jnp.float32
RING = 8
LANES = 128


class Links:
    def __init__(self, here, send_sems, recv_sems):
        self.here, self.send_sems, self.recv_sems = here, send_sems, recv_sems
        self.copies, self.retired = [], 0

    def place(self, **target):
        at = {**self.here, **target}
        return at["depth"], at["row"], at["col"]

    def plan(self, src, dst, recv_sem=None, **target):
        at = len(self.copies)
        copy = pltpu.make_async_remote_copy(
            src_ref=src,
            dst_ref=dst,
            send_sem=self.send_sems.at[at],
            recv_sem=self.recv_sems.at[at] if recv_sem is None else recv_sem,
            device_id=self.place(**target),
            device_id_type=MESH,
        )
        self.copies.append(copy)
        return copy

    def send(self, src, dst, **target):
        copy = self.plan(src, dst, **target)
        copy.start()
        return copy

    def retire(self, upto=None):
        for copy in self.copies[self.retired : upto]:
            copy.wait_send()
        self.retired = len(self.copies) if upto is None else upto


def around(me):
    up, down, far = lax.rem(me + 2, RING), lax.rem(me + 6, RING), lax.rem(me + 4, RING)
    return up, down, far, me + 1 - 2 * lax.rem(me, 2)


def other(at):
    return at + 1 - 2 * lax.rem(at, 2)


def gather_kernel(
    slabs_ref, virt_ref, weight_ref, out_ref,
    vq, hs, acc, rp, qp, wrow, wcol, wl,
    a_raw, a_land, a_keep, a_own, a_sib, a_last,
    b_terms, b_raw, b_land, b_keep, b_own, b_give, b_take, red, tile_land, parts,
    send_sems, recv_sems, tile_sems,
):
    d, r, c = lax.axis_index("depth"), lax.axis_index("row"), lax.axis_index("col")
    d_up, d_down, d_far, d_sib = around(d)
    c_up, c_down, c_far, c_sib = around(c)
    r_up, r_down = lax.rem(r + 1, RING), lax.rem(r + 7, RING)
    links = Links({"depth": d, "row": r, "col": c}, send_sems, recv_sems)
    send = links.send

    barrier = pltpu.get_barrier_semaphore()
    c_far_sib, c_up_sib, c_down_sib = other(c_far), other(c_up), other(c_down)
    partners = [links.place(depth=to) for to in (d_up, d_down, d_sib)]
    partners += [links.place(row=to) for to in (r_up, r_down)]
    partners += [links.place(col=to) for to in (c_up, c_down, c_far, c_sib, c_up_sib, c_down_sib, c_far_sib)]
    for partner in partners:
        pl.semaphore_signal(barrier, inc=1, device_id=partner, device_id_type=MESH)
    apart = lax.rem(c - r + RING, RING)
    turned = jnp.logical_or(jnp.logical_or(apart == 3, apart == 6), apart == 7)

    @pl.when(turned)
    def _():
        for n in range(RING):
            pl.semaphore_signal(barrier, inc=1, device_id=links.place(row=c, col=n), device_id_type=MESH)

    nvir, nbas = virt_ref.shape
    vq[c, 3] = jnp.zeros((nvir, LANES), BF)
    for quarter in range(3):
        vq[c, quarter] = virt_ref[:, LANES * quarter : LANES * quarter + LANES]
    vq[c, 3, :, 0 : nbas - 384] = virt_ref[:, 384:nbas]
    for orbital in range(2):
        hs[d, orbital, 496:512, :] = jnp.zeros((16, LANES), BF)
        hs[d, orbital, 0:nbas, :] = slabs_ref[orbital]

    pl.semaphore_wait(barrier, len(partners) + 3)

    j = lax.rem(r, 4)
    j_up, j_down = lax.rem(j + 1, 4), lax.rem(j + 3, 4)
    spans = (pl.ds(0, 208), pl.ds(208, 224))

    def slab(n, orbital, half=None, **target):
        piece = hs.at[n, orbital] if half is None else hs.at[n, orbital, pl.ds(256 * half, 256)]
        return send(piece, piece, **target)

    def virt(n, quarter, half, **target):
        piece = vq.at[n, quarter, spans[half]]
        return send(piece, piece, **target)

    def virt_rows(n, half):
        return virt(n, j, half, row=r_up), virt(n, j, half, row=r_down)

    pair, up, down, up2, down2, up3, down3, up4, down4 = ({} for _ in range(9))

    def slabs_out(o):
        up[o], down[o] = slab(d, o, depth=d_up), slab(d, o, depth=d_down)

    def slabs_sib(o):
        pair[o].wait_recv()
        up2[o], down2[o] = slab(d_sib, o, depth=d_up), slab(d_sib, o, depth=d_down)

    def slabs_on(o):
        up[o].wait_recv()
        up3[o] = slab(d_down, o, 1, depth=d_up)
        down[o].wait_recv()
        down3[o] = slab(d_up, o, 0, depth=d_down)

    def slabs_sib_on(o):
        up2[o].wait_recv()
        up4[o] = slab(other(d_down), o, 1, depth=d_up)
        down2[o].wait_recv()
        down4[o] = slab(other(d_up), o, 0, depth=d_down)

    def slabs_end(o):
        for copy in (up3[o], down3[o], up4[o], down4[o]):
            copy.wait_recv()

    z_up = {1: virt(c, j, 1, col=c_up)}
    z_down = {0: virt(c, j, 0, col=c_down)}
    z_up[0] = virt(c, j, 0, col=c_up)
    z_down[1] = virt(c, j, 1, col=c_down)
    slabs_out(0)
    pair[0] = slab(d, 0, depth=d_sib)
    share_own = send(vq.at[c], vq.at[c], col=c_sib)

    rows_a, rows_b, rows_c = {}, {}, {}
    z_up[1].wait_recv()
    z_up2 = virt(c_down, j, 1, col=c_up)
    rows_a[1] = virt_rows(c_down, 1)
    z_down[0].wait_recv()
    z_down2 = virt(c_up, j, 0, col=c_down)
    rows_b[0] = virt_rows(c_up, 0)
    z_up[0].wait_recv()
    rows_a[0] = virt_rows(c_down, 0)
    z_down[1].wait_recv()
    rows_b[1] = virt_rows(c_up, 1)
    slabs_sib(0)
    slabs_on(0)
    z_up2.wait_recv()
    rows_c[1] = virt_rows(c_far, 1)
    z_down2.wait_recv()
    rows_c[0] = virt_rows(c_far, 0)
    pair[1] = slab(d, 1, depth=d_sib)
    slabs_out(1)

    def pass_up(n, rows):
        rows[1][0].wait_recv()
        return virt(n, j_down, 1, row=r_up)

    def pass_down(n, rows):
        rows[0][1].wait_recv()
        return virt(n, j_up, 0, row=r_down)

    on_a = [pass_up(c_down, rows_a)]
    on_b = [pass_down(c_up, rows_b)]
    on_a.append(pass_down(c_down, rows_a))
    on_b.append(pass_up(c_up, rows_b))
    slabs_sib_on(0)
    on_c = [pass_up(c_far, rows_c), pass_down(c_far, rows_c)]
    slabs_sib(1)
    slabs_on(1)

    wrow[...] = jnp.zeros_like(wrow)
    for orbital in range(2):
        wrow[:, 0:nvir] = jnp.broadcast_to(weight_ref[orbital : orbital + 1, :], (LANES, nvir))
        wcol[orbital] = wrow[...].T[0:nvir, :]
    acc[...] = jnp.zeros_like(acc)

    def virt_end(n, rows, on):
        for copy in (rows[0][0], rows[1][1], *on):
            copy.wait_recv()
        return send(vq.at[n], vq.at[n], col=c_sib)

    def couple(n, orbital):
        left = jnp.concatenate([vq[n, 0], vq[n, 1], vq[n, 2], vq[n, 3]], axis=1)
        acc[orbital] += jnp.dot(left, hs[n, orbital], preferred_element_type=F32)

    share_a = virt_end(c_down, rows_a, on_a)
    share_b = virt_end(c_up, rows_b, on_b)
    slabs_end(0)
    couple(c, 0)
    share_own.wait_recv()
    couple(c_sib, 0)
    couple(c_down, 0)
    couple(c_up, 0)
    share_c = virt_end(c_far, rows_c, on_c)
    slabs_sib_on(1)
    share_a.wait_recv()
    couple(other(c_down), 0)
    share_b.wait_recv()
    couple(other(c_up), 0)
    couple(c_far, 0)
    share_c.wait_recv()
    couple(other(c_far), 0)

    def panel(n, orbital, **target):
        return send(rp.at[n, orbital], rp.at[n, orbital], **target)

    y_up, y_down, z_up, z_down = {}, {}, {}, {}
    share_own, share_down, share_up, share_far = {}, {}, {}, {}

    def panels_out(o):
        rp[c, o] = acc[o].astype(BF)
        y_up[1, o] = send(rp.at[c, o], qp.at[1, o], row=r_up)
        y_down[1, o] = send(rp.at[c, o], qp.at[2, o], row=r_down)
        z_up[o] = panel(c, o, col=c_up)
        z_down[o] = panel(c, o, col=c_down)
        share_own[o] = panel(c, o, col=c_sib)
        qp[0, o] = rp[c, o]

    def y_step(step, o):
        slot = 2 * step - 1
        y_up[step, o].wait_recv()
        y_up[step + 1, o] = send(qp.at[slot, o], qp.at[slot + 2, o], row=r_up)
        y_down[step, o].wait_recv()
        if step == 2 and o == 1:
            return
        y_down[step + 1, o] = send(qp.at[slot + 1, o], qp.at[slot + 3, o], row=r_down)

    def z_step(o):
        z_up[o].wait_recv()
        if o == 1:
            z_up["far"] = panel(c_down, 1, col=c_up)
        share_down[o] = panel(c_down, o, col=c_sib)
        z_down[o].wait_recv()
        if o == 0:
            z_down["far"] = panel(c_up, 0, col=c_down)
        share_up[o] = panel(c_up, o, col=c_sib)

    def weigh(n, o):
        product = wcol[o] * rp[n, o].astype(F32)
        wl[o, n] = product.astype(BF).T

    panels_out(0)
    slabs_end(1)

    @pl.loop(0, RING)
    def _(n):
        couple(n, 1)

    panels_out(1)
    first_stage = len(links.copies)
    y_step(1, 0)
    z_step(0)
    weigh(c, 0)
    weigh(c, 1)
    y_step(1, 1)
    links.retire(24)
    z_step(1)
    share_own[0].wait_recv()
    weigh(c_sib, 0)
    weigh(c_down, 0)
    y_step(2, 0)
    weigh(c_up, 0)
    links.retire(40)
    z_down["far"].wait_recv()
    share_far[0] = panel(c_far, 0, col=c_sib)
    share_own[1].wait_recv()
    weigh(c_sib, 1)
    y_step(2, 1)
    weigh(c_down, 1)
    z_up["far"].wait_recv()
    share_far[1] = panel(c_far, 1, col=c_sib)
    weigh(c_up, 1)
    weigh(c_far, 0)
    for n, share in ((other(c_down), share_down), (other(c_up), share_up)):
        share[0].wait_recv()
        weigh(n, 0)
    y_down[3, 0].wait_recv()
    y_down[4, 0] = send(qp.at[6, 0], qp.at[7, 0], row=r_down)
    for n, share in ((other(c_down), share_down), (other(c_up), share_up)):
        share[1].wait_recv()
        weigh(n, 1)
    y_up[3, 1].wait_recv()
    y_up[4, 1] = send(qp.at[5, 1], qp.at[7, 1], row=r_up)
    weigh(c_far, 1)
    for o in range(2):
        share_far[o].wait_recv()
        weigh(other(c_far), o)

    low, high = slice(0, 64), slice(64, 128)
    targets = {"far": d_far, "up": d_up, "down": d_down, "own": d}

    def terms_of(name, slots):
        terms = 0.0
        for o in range(2):
            rows = wl[o, pl.ds(2 * (targets[name] // 2), 2)].reshape(256, 432)
            columns = jnp.concatenate([qp[slot, o] for slot in slots], axis=1)
            terms += jnp.dot(rows, columns, preferred_element_type=F32)
        return terms.reshape(2, 128, LANES * len(slots))

    class RingSum:
        def __init__(self, raw, land, keep, own):
            self.raw, self.land, self.keep, self.own, self.copies = raw, land, keep, own, {}

        def send(self, at, value, **target):
            self.raw[at] = value.astype(BF)
            self.copies[at] = send(self.raw.at[at], self.land.at[at], **target)

        def give(self, name, block):
            if name == "far":
                self.send(0, block[:, high], depth=d_up)
                self.send(1, block[:, low], depth=d_down)
            elif name == "up":
                self.send(2, block[:, low], depth=d_up)
                self.keep[0] = block[:, high]
            elif name == "down":
                self.send(3, block[:, high], depth=d_down)
                self.keep[1] = block[:, low]
            else:
                self.own[...] = block

        def pass_on(self):
            for at, target in ((0, d_up), (1, d_down)):
                self.copies[at].wait_recv()
                self.send(at + 4, self.keep[at] + self.land[at].astype(F32), depth=target)

        def end(self):
            for at in (2, 3, 4, 5):
                self.copies[at].wait_recv()
            land = self.land
            self.own[:, low] = self.own[:, low] + land[2].astype(F32) + land[5].astype(F32)
            self.own[:, high] = self.own[:, high] + land[3].astype(F32) + land[4].astype(F32)

    plane = lax.rem(d, 2)
    slots_a, slots_b = (5, 7), (0, 2, 4)
    ring_a = RingSum(a_raw, a_land, a_keep, a_own)
    ring_b = RingSum(b_raw, b_land, b_keep, b_own)
    b_pair = {}
    for at, name in enumerate(targets):
        b_terms[at] = terms_of(name, slots_b)
        b_give[at] = b_terms[at, 1 - plane].astype(BF)
        b_pair[name] = send(b_give.at[at], b_take.at[at], depth=d_sib)
    y_up[3, 0].wait_recv()
    y_up[4, 1].wait_recv()
    y_down[4, 0].wait_recv()
    for name in targets:
        ring_a.give(name, terms_of(name, slots_a))
    ring_a.pass_on()
    links.retire(first_stage)
    for at, name in enumerate(targets):
        b_pair[name].wait_recv()
        ring_b.give(name, (b_terms[at, plane] + b_take[at].astype(F32))[None])
    ring_a.end()
    a_sib[...] = a_own[1 - plane].astype(BF)
    last = send(a_sib, a_last, depth=d_sib)
    ring_b.pass_on()

    rows_of = {0: r, 2: r_up, 4: lax.rem(r + 2, RING), 5: lax.rem(r + 5, RING), 7: lax.rem(r + 4, RING)}
    mine = tile_sems.at[c]

    def tiles_out(slots, total):
        for at, slot in enumerate(slots):
            red[slot] = total[:, LANES * at : LANES * at + LANES]
        for slot in slots:
            to = rows_of[slot]
            copy = links.plan(red.at[slot], tile_land.at[c], recv_sem=mine, col=to)
            straight[slot] = to, copy
            pl.when(to != c)(copy.start)
            if slot in (2, 4, 5):
                links.plan(red.at[slot], tile_land.at[c], recv_sem=mine, row=to, col=r).start()

    straight = {}
    last.wait_recv()
    tiles_out(slots_a, (a_own[plane] + a_last[...].astype(F32)).astype(BF))
    ring_b.end()
    tiles_out(slots_b, b_own[0].astype(BF))

    before = len(links.copies) - 8
    links.retire(before)
    for slot, (to, _) in straight.items():

        @pl.when(to == c)
        def _(slot=slot):
            tile_land[c] = red[slot]

    for n in range(RING):

        @pl.when(jnp.logical_or(turned, c != n))
        def _(n=n):
            pltpu.make_async_remote_copy(
                src_ref=red.at[0],
                dst_ref=tile_land.at[n],
                send_sem=send_sems.at[before],
                recv_sem=tile_sems.at[n],
                device_id=links.place(col=c_sib),
                device_id_type=MESH,
            ).wait_recv()

    @pl.when(turned)
    def _():
        for n in range(RING):
            parts[d, n] = tile_land[n].T

    @pl.when(jnp.logical_not(turned))
    def _():
        parts[d] = tile_land[...]

    def pass_on(n, begin, size, **target):
        piece = parts.at[n, pl.ds(begin, size)]
        return send(piece, piece, **target)

    def settle(n):
        @pl.when(turned)
        def _():
            at = pl.ds(pl.multiple_of(LANES * n, LANES), LANES)
            for m in range(RING):
                out_ref[m, :, at] = parts[n, m]

        @pl.when(jnp.logical_not(turned))
        def _():
            for m in range(RING):
                out_ref[n, :, LANES * m : LANES * m + LANES] = parts[n, m]

    first_gather = len(links.copies)
    pair = pass_on(d, 0, 4, depth=d_sib)
    b_up = pass_on(d, 4, 4, depth=d_up)
    b_down = pass_on(d, 4, 4, depth=d_down)
    b_pairs = [pass_on(d, 4, 4, depth=d_sib)]
    a_up = pass_on(d, 0, 4, depth=d_up)
    a_down = pass_on(d, 0, 4, depth=d_down)
    for slot, (to, copy) in straight.items():
        pl.when(to != c)(copy.wait_send)
    for at in range(before, first_gather):
        if all(links.copies[at] is not copy for _, copy in straight.values()):
            links.copies[at].wait_send()
    links.retired = first_gather
    settle(d)
    pair.wait_recv()
    a_up2 = pass_on(d_sib, 0, 4, depth=d_up)
    a_down2 = pass_on(d_sib, 0, 4, depth=d_down)
    b_up.wait_recv()
    b_up2 = pass_on(d_down, 6, 2, depth=d_up)
    b_pairs.append(pass_on(d_down, 4, 4, depth=d_sib))
    b_down.wait_recv()
    b_down2 = pass_on(d_up, 4, 2, depth=d_down)
    b_pairs.append(pass_on(d_up, 4, 4, depth=d_sib))
    a_up.wait_recv()
    a_up3 = pass_on(d_down, 2, 2, depth=d_up)
    a_down.wait_recv()
    a_down3 = pass_on(d_up, 0, 2, depth=d_down)
    settle(d_up)
    settle(d_down)
    b_up2.wait_recv()
    b_pairs.append(pass_on(d_far, 6, 2, depth=d_sib))
    b_down2.wait_recv()
    b_pairs.append(pass_on(d_far, 4, 2, depth=d_sib))
    a_up2.wait_recv()
    a_up4 = pass_on(other(d_down), 2, 2, depth=d_up)
    a_down2.wait_recv()
    a_down4 = pass_on(other(d_up), 0, 2, depth=d_down)
    links.retire(len(links.copies) - 6)
    b_pairs[0].wait_recv()
    settle(d_sib)
    a_up3.wait_recv()
    a_down3.wait_recv()
    settle(d_far)
    b_pairs[1].wait_recv()
    settle(other(d_down))
    b_pairs[2].wait_recv()
    settle(other(d_up))
    for copy in (a_up4, a_down4, *b_pairs[3:]):
        copy.wait_recv()
    settle(other(d_far))
    links.retire()


def on_device(half_slabs, virtuals, occupied_energy, virtual_energy, frequency):
    vmem = pl.BlockSpec(memory_space=pltpu.VMEM)
    excitation = virtual_energy[None, :] - occupied_energy[:, None]
    weight = 4.0 * excitation / (excitation * excitation + frequency[0] * frequency[0])
    copies = 128
    gram = pl.pallas_call(
        gather_kernel,
        out_shape=jax.ShapeDtypeStruct((RING, 128, 1024), BF),
        in_specs=[vmem] * 3,
        out_specs=vmem,
        scratch_shapes=[
            pltpu.VMEM((RING, 4, 432, LANES), BF),
            pltpu.VMEM((RING, 2, 512, LANES), BF),
            pltpu.VMEM((2, 432, LANES), F32),
            pltpu.VMEM((RING, 2, 432, LANES), BF),
            pltpu.VMEM((RING, 2, 432, LANES), BF),
            pltpu.VMEM((LANES, 512), F32),
            pltpu.VMEM((2, 432, LANES), F32),
            pltpu.VMEM((2, RING, 128, 432), BF),
            pltpu.VMEM((6, 2, 64, 256), BF),
            pltpu.VMEM((6, 2, 64, 256), BF),
            pltpu.VMEM((2, 2, 64, 256), F32),
            pltpu.VMEM((2, 128, 256), F32),
            pltpu.VMEM((128, 256), BF),
            pltpu.VMEM((128, 256), BF),
            pltpu.VMEM((4, 2, 128, 384), F32),
            pltpu.VMEM((6, 1, 64, 384), BF),
            pltpu.VMEM((6, 1, 64, 384), BF),
            pltpu.VMEM((2, 1, 64, 384), F32),
            pltpu.VMEM((1, 128, 384), F32),
            pltpu.VMEM((4, 128, 384), BF),
            pltpu.VMEM((4, 128, 384), BF),
            pltpu.VMEM((RING, 128, LANES), BF),
            pltpu.VMEM((RING, 128, LANES), BF),
            pltpu.VMEM((RING, RING, 128, LANES), BF),
            pltpu.SemaphoreType.DMA((copies,)),
            pltpu.SemaphoreType.DMA((copies,)),
            pltpu.SemaphoreType.DMA((RING,)),
        ],
        compiler_params=pltpu.CompilerParams(
            collective_id=0, has_side_effects=True, vmem_limit_bytes=48 * 2**20
        ),
        cost_estimate=pl.CostEstimate(flops=2_700_000_000, bytes_accessed=3_000_000, transcendentals=0),
    )(half_slabs, virtuals.T, weight)
    return gram.reshape(1024, 1024).astype(F32)


def solution(mesh):
    placed = (P(None, "depth", ("row", "col")), P("col", "depth"), P(), P("depth"), P())
    return jax.shard_map(
        on_device, mesh=mesh, in_specs=placed, out_specs=P("row", "col"), check_vma=False
    )
```

```python
import jax
import jax.numpy as jnp
from jax import lax
from jax.experimental import pallas as pl
from jax.experimental.pallas import tpu as pltpu
from jax.sharding import PartitionSpec as P

MESH = pl.DeviceIdType.MESH
BF = jnp.bfloat16
F32 = jnp.float32
RING = 8
LANES = 128


class Links:
    def __init__(self, here, send_sems, recv_sems):
        self.here, self.send_sems, self.recv_sems = here, send_sems, recv_sems
        self.copies, self.retired = [], 0

    def place(self, **target):
        at = {**self.here, **target}
        return at["depth"], at["row"], at["col"]

    def plan(self, src, dst, recv_sem=None, **target):
        at = len(self.copies)
        copy = pltpu.make_async_remote_copy(
            src_ref=src,
            dst_ref=dst,
            send_sem=self.send_sems.at[at],
            recv_sem=self.recv_sems.at[at] if recv_sem is None else recv_sem,
            device_id=self.place(**target),
            device_id_type=MESH,
        )
        self.copies.append(copy)
        return copy

    def send(self, src, dst, **target):
        copy = self.plan(src, dst, **target)
        copy.start()
        return copy

    def retire(self, upto=None):
        for copy in self.copies[self.retired : upto]:
            copy.wait_send()
        self.retired = len(self.copies) if upto is None else upto


def around(me):
    up, down, far = lax.rem(me + 2, RING), lax.rem(me + 6, RING), lax.rem(me + 4, RING)
    return up, down, far, me + 1 - 2 * lax.rem(me, 2)


def other(at):
    return at + 1 - 2 * lax.rem(at, 2)


def gather_kernel(
    slabs_ref, virt_ref, weight_ref, out_ref,
    vq, hs, acc, rp, qp, wrow, wcol, wl,
    a_raw, a_land, a_keep, a_own, a_sib, a_last,
    b_terms, b_raw, b_land, b_keep, b_own, b_give, b_take, red, tile_land, parts,
    send_sems, recv_sems, tile_sems,
):
    d, r, c = lax.axis_index("depth"), lax.axis_index("row"), lax.axis_index("col")
    d_up, d_down, d_far, d_sib = around(d)
    c_up, c_down, c_far, c_sib = around(c)
    r_up, r_down = lax.rem(r + 1, RING), lax.rem(r + 7, RING)
    links = Links({"depth": d, "row": r, "col": c}, send_sems, recv_sems)
    send = links.send

    barrier = pltpu.get_barrier_semaphore()
    c_far_sib, c_up_sib, c_down_sib = other(c_far), other(c_up), other(c_down)
    partners = [links.place(depth=to) for to in (d_up, d_down, d_sib)]
    partners += [links.place(row=to) for to in (r_up, r_down)]
    partners += [links.place(col=to) for to in (c_up, c_down, c_far, c_sib, c_up_sib, c_down_sib, c_far_sib)]
    for partner in partners:
        pl.semaphore_signal(barrier, inc=1, device_id=partner, device_id_type=MESH)
    apart = lax.rem(c - r + RING, RING)
    turned = jnp.logical_or(jnp.logical_or(apart == 3, apart == 6), apart == 7)

    @pl.when(turned)
    def _():
        for n in range(RING):
            pl.semaphore_signal(barrier, inc=1, device_id=links.place(row=c, col=n), device_id_type=MESH)

    nvir, nbas = virt_ref.shape
    vq[c, 3] = jnp.zeros((nvir, LANES), BF)
    for quarter in range(3):
        vq[c, quarter] = virt_ref[:, LANES * quarter : LANES * quarter + LANES]
    vq[c, 3, :, 0 : nbas - 384] = virt_ref[:, 384:nbas]
    for orbital in range(2):
        hs[d, orbital, 496:512, :] = jnp.zeros((16, LANES), BF)
        hs[d, orbital, 0:nbas, :] = slabs_ref[orbital]

    pl.semaphore_wait(barrier, len(partners) + 3)

    j = lax.rem(r, 4)
    j_up, j_down = lax.rem(j + 1, 4), lax.rem(j + 3, 4)
    spans = (pl.ds(0, 208), pl.ds(208, 224))

    def slab(n, orbital, half=None, **target):
        piece = hs.at[n, orbital] if half is None else hs.at[n, orbital, pl.ds(256 * half, 256)]
        return send(piece, piece, **target)

    def virt(n, quarter, half=None, **target):
        piece = vq.at[n, quarter] if half is None else vq.at[n, quarter, spans[half]]
        return send(piece, piece, **target)

    def virt_rows(n):
        return virt(n, j, row=r_up), virt(n, j, row=r_down)

    pair, up, down, up2, down2, up3, down3, up4, down4 = ({} for _ in range(9))

    def slabs_out(o):
        up[o], down[o] = slab(d, o, depth=d_up), slab(d, o, depth=d_down)

    def slabs_sib(o):
        pair[o].wait_recv()
        up2[o], down2[o] = slab(d_sib, o, depth=d_up), slab(d_sib, o, depth=d_down)

    def slabs_on(o):
        up[o].wait_recv()
        up3[o] = slab(d_down, o, 1, depth=d_up)
        down[o].wait_recv()
        down3[o] = slab(d_up, o, 0, depth=d_down)

    def slabs_sib_on(o):
        up2[o].wait_recv()
        up4[o] = slab(other(d_down), o, 1, depth=d_up)
        down2[o].wait_recv()
        down4[o] = slab(other(d_up), o, 0, depth=d_down)

    def slabs_end(o):
        for copy in (up3[o], down3[o], up4[o], down4[o]):
            copy.wait_recv()

    z_up = virt(c, j, col=c_up)
    z_down = virt(c, j, col=c_down)
    slabs_out(0)
    pair[0] = slab(d, 0, depth=d_sib)
    share_own = send(vq.at[c], vq.at[c], col=c_sib)
    slabs_out(1)

    z_up.wait_recv()
    z_up2 = virt(c_down, j, 1, col=c_up)
    rows_a = virt_rows(c_down)
    z_down.wait_recv()
    z_down2 = virt(c_up, j, 0, col=c_down)
    rows_b = virt_rows(c_up)
    slabs_sib(0)
    slabs_on(0)
    z_up2.wait_recv()
    z_down2.wait_recv()
    rows_c = virt_rows(c_far)
    pair[1] = slab(d, 1, depth=d_sib)

    def pass_rows(n, rows):
        rows[0].wait_recv()
        if n is c_down:
            one = (virt(n, j_down, row=r_up),)
        elif n is c_far:
            one = (virt(n, j_down, 1, row=r_up),)
        else:
            one = ()
        rows[1].wait_recv()
        if n is c_up:
            one += (virt(n, j_up, row=r_down),)
        elif n is c_far:
            one += (virt(n, j_up, 0, row=r_down),)
        return one

    on_a = pass_rows(c_down, rows_a)
    on_b = pass_rows(c_up, rows_b)
    slabs_sib_on(0)
    on_c = pass_rows(c_far, rows_c)
    slabs_sib(1)
    slabs_on(1)

    wrow[...] = jnp.zeros_like(wrow)
    for orbital in range(2):
        wrow[:, 0:nvir] = jnp.broadcast_to(weight_ref[orbital : orbital + 1, :], (LANES, nvir))
        wcol[orbital] = wrow[...].T[0:nvir, :]
    acc[...] = jnp.zeros_like(acc)

    def virt_end(n, on):
        for copy in on:
            copy.wait_recv()
        return send(vq.at[n], vq.at[n], col=c_sib)

    def couple(n, orbital):
        left = jnp.concatenate([vq[n, 0], vq[n, 1], vq[n, 2], vq[n, 3]], axis=1)
        acc[orbital] += jnp.dot(left, hs[n, orbital], preferred_element_type=F32)

    share_a = virt_end(c_down, on_a)
    share_b = virt_end(c_up, on_b)
    slabs_end(0)
    couple(c, 0)
    share_own.wait_recv()
    couple(c_sib, 0)
    couple(c_down, 0)
    couple(c_up, 0)
    share_c = virt_end(c_far, on_c)
    slabs_sib_on(1)
    share_a.wait_recv()
    couple(other(c_down), 0)
    share_b.wait_recv()
    couple(other(c_up), 0)
    couple(c_far, 0)
    share_c.wait_recv()
    couple(other(c_far), 0)

    def panel(n, orbital, **target):
        return send(rp.at[n, orbital], rp.at[n, orbital], **target)

    y_up, y_down, z_up, z_down = {}, {}, {}, {}
    share_own, share_down, share_up, share_far = {}, {}, {}, {}

    def panels_out(o):
        rp[c, o] = acc[o].astype(BF)
        y_up[1, o] = send(rp.at[c, o], qp.at[1, o], row=r_up)
        y_down[1, o] = send(rp.at[c, o], qp.at[2, o], row=r_down)
        z_up[o] = panel(c, o, col=c_up)
        z_down[o] = panel(c, o, col=c_down)
        share_own[o] = panel(c, o, col=c_sib)
        qp[0, o] = rp[c, o]

    def y_step(step, o):
        slot = 2 * step - 1
        y_up[step, o].wait_recv()
        y_up[step + 1, o] = send(qp.at[slot, o], qp.at[slot + 2, o], row=r_up)
        y_down[step, o].wait_recv()
        if step == 2 and o == 1:
            return
        y_down[step + 1, o] = send(qp.at[slot + 1, o], qp.at[slot + 3, o], row=r_down)

    def z_step(o):
        z_up[o].wait_recv()
        if o == 1:
            z_up["far"] = panel(c_down, 1, col=c_up)
        share_down[o] = panel(c_down, o, col=c_sib)
        z_down[o].wait_recv()
        if o == 0:
            z_down["far"] = panel(c_up, 0, col=c_down)
        share_up[o] = panel(c_up, o, col=c_sib)

    def weigh(n, o):
        product = wcol[o] * rp[n, o].astype(F32)
        wl[o, n] = product.astype(BF).T

    panels_out(0)
    slabs_end(1)

    @pl.loop(0, RING)
    def _(n):
        couple(n, 1)

    panels_out(1)
    first_stage = len(links.copies)
    y_step(1, 0)
    z_step(0)
    weigh(c, 0)
    weigh(c, 1)
    y_step(1, 1)
    links.retire(24)
    z_step(1)
    share_own[0].wait_recv()
    weigh(c_sib, 0)
    weigh(c_down, 0)
    y_step(2, 0)
    weigh(c_up, 0)
    links.retire(40)
    z_down["far"].wait_recv()
    share_far[0] = panel(c_far, 0, col=c_sib)
    share_own[1].wait_recv()
    weigh(c_sib, 1)
    y_step(2, 1)
    weigh(c_down, 1)
    z_up["far"].wait_recv()
    share_far[1] = panel(c_far, 1, col=c_sib)
    weigh(c_up, 1)
    weigh(c_far, 0)
    for n, share in ((other(c_down), share_down), (other(c_up), share_up)):
        share[0].wait_recv()
        weigh(n, 0)
    y_down[3, 0].wait_recv()
    y_down[4, 0] = send(qp.at[6, 0], qp.at[7, 0], row=r_down)
    for n, share in ((other(c_down), share_down), (other(c_up), share_up)):
        share[1].wait_recv()
        weigh(n, 1)
    y_up[3, 1].wait_recv()
    y_up[4, 1] = send(qp.at[5, 1], qp.at[7, 1], row=r_up)
    weigh(c_far, 1)
    for o in range(2):
        share_far[o].wait_recv()
        weigh(other(c_far), o)

    low, high = slice(0, 64), slice(64, 128)
    targets = {"far": d_far, "up": d_up, "down": d_down, "own": d}

    def terms_of(name, slots):
        terms = 0.0
        for o in range(2):
            rows = wl[o, pl.ds(2 * (targets[name] // 2), 2)].reshape(256, 432)
            columns = jnp.concatenate([qp[slot, o] for slot in slots], axis=1)
            terms += jnp.dot(rows, columns, preferred_element_type=F32)
        return terms.reshape(2, 128, LANES * len(slots))

    class RingSum:
        def __init__(self, raw, land, keep, own):
            self.raw, self.land, self.keep, self.own, self.copies = raw, land, keep, own, {}

        def send(self, at, value, **target):
            self.raw[at] = value.astype(BF)
            self.copies[at] = send(self.raw.at[at], self.land.at[at], **target)

        def give(self, name, block):
            if name == "far":
                self.send(0, block[:, high], depth=d_up)
                self.send(1, block[:, low], depth=d_down)
            elif name == "up":
                self.send(2, block[:, low], depth=d_up)
                self.keep[0] = block[:, high]
            elif name == "down":
                self.send(3, block[:, high], depth=d_down)
                self.keep[1] = block[:, low]
            else:
                self.own[...] = block

        def pass_on(self, at):
            self.copies[at].wait_recv()
            self.send(at + 4, self.keep[at] + self.land[at].astype(F32), depth=(d_up, d_down)[at])

        def end(self):
            for at in (2, 3, 4, 5):
                self.copies[at].wait_recv()
            land = self.land
            self.own[:, low] = self.own[:, low] + land[2].astype(F32) + land[5].astype(F32)
            self.own[:, high] = self.own[:, high] + land[3].astype(F32) + land[4].astype(F32)

    plane = lax.rem(d, 2)
    slots_a, slots_b = (5, 7), (0, 2, 4)
    ring_a = RingSum(a_raw, a_land, a_keep, a_own)
    ring_b = RingSum(b_raw, b_land, b_keep, b_own)
    b_pair = {}
    def gram_b(at, name):
        b_terms[at] = terms_of(name, slots_b)
        b_give[at] = b_terms[at, 1 - plane].astype(BF)
        b_pair[name] = send(b_give.at[at], b_take.at[at], depth=d_sib)

    def pair_b(at, name):
        b_pair[name].wait_recv()
        ring_b.give(name, (b_terms[at, plane] + b_take[at].astype(F32))[None])

    rows_of = {0: r, 2: r_up, 4: lax.rem(r + 2, RING), 5: lax.rem(r + 5, RING), 7: lax.rem(r + 4, RING)}
    mine = tile_sems.at[c]

    def tiles_out(slots, total):
        for at, slot in enumerate(slots):
            red[slot] = total[:, LANES * at : LANES * at + LANES]
        for slot in slots:
            to = rows_of[slot]
            copy = links.plan(red.at[slot], tile_land.at[c], recv_sem=mine, col=to)
            straight[slot] = to, copy
            pl.when(to != c)(copy.start)
            if slot in (2, 4, 5):
                links.plan(red.at[slot], tile_land.at[c], recv_sem=mine, row=to, col=r).start()

    straight = {}

    gram_b(0, "far")
    gram_b(1, "up")
    gram_b(2, "down")
    y_up[3, 0].wait_recv()
    y_up[4, 1].wait_recv()
    y_down[4, 0].wait_recv()
    ring_a.give("far", terms_of("far", slots_a))
    ring_a.give("down", terms_of("down", slots_a))
    pair_b(0, "far")
    ring_a.give("up", terms_of("up", slots_a))
    gram_b(3, "own")
    ring_a.pass_on(1)
    ring_a.pass_on(0)
    pair_b(1, "up")
    pair_b(2, "down")
    ring_a.give("own", terms_of("own", slots_a))
    links.retire(first_stage)
    ring_b.pass_on(0)
    ring_b.pass_on(1)
    ring_a.end()
    a_sib[...] = a_own[1 - plane].astype(BF)
    last = send(a_sib, a_last, depth=d_sib)
    pair_b(3, "own")
    ring_b.end()
    tiles_out(slots_b, b_own[0].astype(BF))
    last.wait_recv()
    tiles_out(slots_a, (a_own[plane] + a_last[...].astype(F32)).astype(BF))

    before = len(links.copies) - 8
    links.retire(before)
    for slot, (to, _) in straight.items():

        @pl.when(to == c)
        def _(slot=slot):
            tile_land[c] = red[slot]

    for n in range(RING):

        @pl.when(jnp.logical_or(turned, c != n))
        def _(n=n):
            pltpu.make_async_remote_copy(
                src_ref=red.at[0],
                dst_ref=tile_land.at[n],
                send_sem=send_sems.at[before],
                recv_sem=tile_sems.at[n],
                device_id=links.place(col=c_sib),
                device_id_type=MESH,
            ).wait_recv()

    @pl.when(turned)
    def _():
        for n in range(RING):
            parts[d, n] = tile_land[n].T

    @pl.when(jnp.logical_not(turned))
    def _():
        parts[d] = tile_land[...]

    def pass_on(n, begin, size, **target):
        piece = parts.at[n, pl.ds(begin, size)]
        return send(piece, piece, **target)

    def settle(n):
        @pl.when(turned)
        def _():
            at = pl.ds(pl.multiple_of(LANES * n, LANES), LANES)
            for m in range(RING):
                out_ref[m, :, at] = parts[n, m]

        @pl.when(jnp.logical_not(turned))
        def _():
            for m in range(RING):
                out_ref[n, :, LANES * m : LANES * m + LANES] = parts[n, m]

    first_gather = len(links.copies)
    pair = pass_on(d, 0, 4, depth=d_sib)
    b_up = pass_on(d, 4, 4, depth=d_up)
    b_down = pass_on(d, 4, 4, depth=d_down)
    b_pairs = [pass_on(d, 4, 4, depth=d_sib)]
    a_up = pass_on(d, 0, 4, depth=d_up)
    a_down = pass_on(d, 0, 4, depth=d_down)
    for slot, (to, copy) in straight.items():
        pl.when(to != c)(copy.wait_send)
    for at in range(before, first_gather):
        if all(links.copies[at] is not copy for _, copy in straight.values()):
            links.copies[at].wait_send()
    links.retired = first_gather
    settle(d)
    pair.wait_recv()
    a_up2 = pass_on(d_sib, 0, 4, depth=d_up)
    a_down2 = pass_on(d_sib, 0, 4, depth=d_down)
    b_up.wait_recv()
    b_up2 = pass_on(d_down, 6, 2, depth=d_up)
    b_pairs.append(pass_on(d_down, 4, 4, depth=d_sib))
    b_down.wait_recv()
    b_down2 = pass_on(d_up, 4, 2, depth=d_down)
    b_pairs.append(pass_on(d_up, 4, 4, depth=d_sib))
    a_up.wait_recv()
    a_up3 = pass_on(d_down, 2, 2, depth=d_up)
    a_down.wait_recv()
    a_down3 = pass_on(d_up, 0, 2, depth=d_down)
    settle(d_up)
    settle(d_down)
    b_up2.wait_recv()
    b_pairs.append(pass_on(d_far, 6, 2, depth=d_sib))
    b_down2.wait_recv()
    b_pairs.append(pass_on(d_far, 4, 2, depth=d_sib))
    a_up2.wait_recv()
    a_up4 = pass_on(other(d_down), 2, 2, depth=d_up)
    a_down2.wait_recv()
    a_down4 = pass_on(other(d_up), 0, 2, depth=d_down)
    links.retire(len(links.copies) - 6)
    b_pairs[0].wait_recv()
    settle(d_sib)
    a_up3.wait_recv()
    a_down3.wait_recv()
    settle(d_far)
    b_pairs[1].wait_recv()
    settle(other(d_down))
    b_pairs[2].wait_recv()
    settle(other(d_up))
    for copy in (a_up4, a_down4, *b_pairs[3:]):
        copy.wait_recv()
    settle(other(d_far))
    links.retire()


def on_device(half_slabs, virtuals, occupied_energy, virtual_energy, frequency):
    vmem = pl.BlockSpec(memory_space=pltpu.VMEM)
    excitation = virtual_energy[None, :] - occupied_energy[:, None]
    weight = 4.0 * excitation / (excitation * excitation + frequency[0] * frequency[0])
    copies = 128
    gram = pl.pallas_call(
        gather_kernel,
        out_shape=jax.ShapeDtypeStruct((RING, 128, 1024), BF),
        in_specs=[vmem] * 3,
        out_specs=vmem,
        scratch_shapes=[
            pltpu.VMEM((RING, 4, 432, LANES), BF),
            pltpu.VMEM((RING, 2, 512, LANES), BF),
            pltpu.VMEM((2, 432, LANES), F32),
            pltpu.VMEM((RING, 2, 432, LANES), BF),
            pltpu.VMEM((RING, 2, 432, LANES), BF),
            pltpu.VMEM((LANES, 512), F32),
            pltpu.VMEM((2, 432, LANES), F32),
            pltpu.VMEM((2, RING, 128, 432), BF),
            pltpu.VMEM((6, 2, 64, 256), BF),
            pltpu.VMEM((6, 2, 64, 256), BF),
            pltpu.VMEM((2, 2, 64, 256), F32),
            pltpu.VMEM((2, 128, 256), F32),
            pltpu.VMEM((128, 256), BF),
            pltpu.VMEM((128, 256), BF),
            pltpu.VMEM((4, 2, 128, 384), F32),
            pltpu.VMEM((6, 1, 64, 384), BF),
            pltpu.VMEM((6, 1, 64, 384), BF),
            pltpu.VMEM((2, 1, 64, 384), F32),
            pltpu.VMEM((1, 128, 384), F32),
            pltpu.VMEM((4, 128, 384), BF),
            pltpu.VMEM((4, 128, 384), BF),
            pltpu.VMEM((RING, 128, LANES), BF),
            pltpu.VMEM((RING, 128, LANES), BF),
            pltpu.VMEM((RING, RING, 128, LANES), BF),
            pltpu.SemaphoreType.DMA((copies,)),
            pltpu.SemaphoreType.DMA((copies,)),
            pltpu.SemaphoreType.DMA((RING,)),
        ],
        compiler_params=pltpu.CompilerParams(
            collective_id=0, has_side_effects=True, vmem_limit_bytes=48 * 2**20
        ),
        cost_estimate=pl.CostEstimate(flops=2_700_000_000, bytes_accessed=3_000_000, transcendentals=0),
    )(half_slabs, virtuals.T, weight)
    return gram.reshape(1024, 1024).astype(F32)


def solution(mesh):
    placed = (P(None, "depth", ("row", "col")), P("col", "depth"), P(), P("depth"), P())
    return jax.shard_map(
        on_device, mesh=mesh, in_specs=placed, out_specs=P("row", "col"), check_vma=False
    )
```

```python
import jax
import jax.numpy as jnp
from jax import lax
from jax.experimental import pallas as pl
from jax.experimental.pallas import tpu as pltpu
from jax.sharding import PartitionSpec as P

MESH = pl.DeviceIdType.MESH
BF = jnp.bfloat16
F32 = jnp.float32
RING = 8
LANES = 128


class Links:
    def __init__(self, here, send_sems, recv_sems):
        self.here, self.send_sems, self.recv_sems = here, send_sems, recv_sems
        self.copies, self.retired = [], 0

    def place(self, **target):
        at = {**self.here, **target}
        return at["depth"], at["row"], at["col"]

    def plan(self, src, dst, recv_sem=None, **target):
        at = len(self.copies)
        copy = pltpu.make_async_remote_copy(
            src_ref=src,
            dst_ref=dst,
            send_sem=self.send_sems.at[at],
            recv_sem=self.recv_sems.at[at] if recv_sem is None else recv_sem,
            device_id=self.place(**target),
            device_id_type=MESH,
        )
        self.copies.append(copy)
        return copy

    def send(self, src, dst, **target):
        copy = self.plan(src, dst, **target)
        copy.start()
        return copy

    def retire(self, upto=None):
        for copy in self.copies[self.retired : upto]:
            copy.wait_send()
        self.retired = len(self.copies) if upto is None else upto


def around(me):
    up, down, far = lax.rem(me + 2, RING), lax.rem(me + 6, RING), lax.rem(me + 4, RING)
    return up, down, far, me + 1 - 2 * lax.rem(me, 2)


def other(at):
    return at + 1 - 2 * lax.rem(at, 2)


def gather_kernel(
    slabs_ref, virt_ref, weight_ref, out_ref,
    vq, hs, acc, rp, qp, wrow, wcol, wl,
    a_raw, a_land, a_keep, a_own, a_sib, a_last,
    b_terms, b_raw, b_land, b_keep, b_own, b_give, b_take, red, tile_land, parts,
    send_sems, recv_sems, tile_sems,
):
    d, r, c = lax.axis_index("depth"), lax.axis_index("row"), lax.axis_index("col")
    d_up, d_down, d_far, d_sib = around(d)
    c_up, c_down, c_far, c_sib = around(c)
    r_up, r_down = lax.rem(r + 1, RING), lax.rem(r + 7, RING)
    links = Links({"depth": d, "row": r, "col": c}, send_sems, recv_sems)
    send = links.send

    barrier = pltpu.get_barrier_semaphore()
    c_far_sib, c_up_sib, c_down_sib = other(c_far), other(c_up), other(c_down)
    partners = [links.place(depth=to) for to in (d_up, d_down, d_sib)]
    partners += [links.place(row=to) for to in (r_up, r_down)]
    partners += [links.place(col=to) for to in (c_up, c_down, c_far, c_sib, c_up_sib, c_down_sib, c_far_sib)]
    for partner in partners:
        pl.semaphore_signal(barrier, inc=1, device_id=partner, device_id_type=MESH)
    apart = lax.rem(c - r + RING, RING)
    turned = jnp.logical_or(jnp.logical_or(apart == 3, apart == 6), apart == 7)

    @pl.when(turned)
    def _():
        for n in range(RING):
            pl.semaphore_signal(barrier, inc=1, device_id=links.place(row=c, col=n), device_id_type=MESH)

    nvir, nbas = virt_ref.shape
    vq[c, 3] = jnp.zeros((nvir, LANES), BF)
    for quarter in range(3):
        vq[c, quarter] = virt_ref[:, LANES * quarter : LANES * quarter + LANES]
    vq[c, 3, :, 0 : nbas - 384] = virt_ref[:, 384:nbas]
    for orbital in range(2):
        hs[d, orbital, 496:512, :] = jnp.zeros((16, LANES), BF)
        hs[d, orbital, 0:nbas, :] = slabs_ref[orbital]

    pl.semaphore_wait(barrier, len(partners) + 3)

    j = lax.rem(r, 4)
    j_up, j_down = lax.rem(j + 1, 4), lax.rem(j + 3, 4)
    spans = (pl.ds(0, 208), pl.ds(208, 224))

    def slab(n, orbital, half=None, **target):
        piece = hs.at[n, orbital] if half is None else hs.at[n, orbital, pl.ds(256 * half, 256)]
        return send(piece, piece, **target)

    def virt(n, quarter, half=None, **target):
        piece = vq.at[n, quarter] if half is None else vq.at[n, quarter, spans[half]]
        return send(piece, piece, **target)

    def virt_rows(n):
        return virt(n, j, row=r_up), virt(n, j, row=r_down)

    pair, up, down, up2, down2, up3, down3, up4, down4 = ({} for _ in range(9))

    def slabs_out(o):
        up[o], down[o] = slab(d, o, depth=d_up), slab(d, o, depth=d_down)

    def slabs_sib(o):
        pair[o].wait_recv()
        up2[o], down2[o] = slab(d_sib, o, depth=d_up), slab(d_sib, o, depth=d_down)

    def slabs_on(o):
        up[o].wait_recv()
        up3[o] = slab(d_down, o, 1, depth=d_up)
        down[o].wait_recv()
        down3[o] = slab(d_up, o, 0, depth=d_down)

    def slabs_sib_on(o):
        up2[o].wait_recv()
        up4[o] = slab(other(d_down), o, 1, depth=d_up)
        down2[o].wait_recv()
        down4[o] = slab(other(d_up), o, 0, depth=d_down)

    def slabs_end(o):
        for copy in (up3[o], down3[o], up4[o], down4[o]):
            copy.wait_recv()

    z_up = virt(c, j, col=c_up)
    z_down = virt(c, j, col=c_down)
    slabs_out(0)
    pair[0] = slab(d, 0, depth=d_sib)
    share_virt = send(vq.at[c], vq.at[c], col=c_sib)
    slabs_out(1)

    z_up.wait_recv()
    z_up2 = virt(c_down, j, 1, col=c_up)
    rows_a = virt_rows(c_down)
    z_down.wait_recv()
    z_down2 = virt(c_up, j, 0, col=c_down)
    rows_b = virt_rows(c_up)
    slabs_sib(0)
    slabs_on(0)
    z_up2.wait_recv()
    z_down2.wait_recv()
    rows_c = virt_rows(c_far)
    pair[1] = slab(d, 1, depth=d_sib)

    def pass_rows(n, rows):
        rows[0].wait_recv()
        if n is c_down:
            one = (virt(n, j_down, row=r_up),)
        elif n is c_far:
            one = (virt(n, j_down, 1, row=r_up),)
        else:
            one = ()
        rows[1].wait_recv()
        if n is c_up:
            one += (virt(n, j_up, row=r_down),)
        elif n is c_far:
            one += (virt(n, j_up, 0, row=r_down),)
        return one

    on_a = pass_rows(c_down, rows_a)
    on_b = pass_rows(c_up, rows_b)
    slabs_sib_on(0)
    on_c = pass_rows(c_far, rows_c)
    slabs_sib(1)
    slabs_on(1)

    wrow[...] = jnp.zeros_like(wrow)
    for orbital in range(2):
        wrow[:, 0:nvir] = jnp.broadcast_to(weight_ref[orbital : orbital + 1, :], (LANES, nvir))
        wcol[orbital] = wrow[...].T[0:nvir, :]
    acc[...] = jnp.zeros_like(acc)

    def virt_end(n, on):
        for copy in on:
            copy.wait_recv()
        return send(vq.at[n], vq.at[n], col=c_sib)

    def couple(n, orbital):
        left = jnp.concatenate([vq[n, 0], vq[n, 1], vq[n, 2], vq[n, 3]], axis=1)
        acc[orbital] += jnp.dot(left, hs[n, orbital], preferred_element_type=F32)

    share_a = virt_end(c_down, on_a)
    share_b = virt_end(c_up, on_b)
    slabs_end(0)
    couple(c, 0)
    share_virt.wait_recv()
    couple(c_sib, 0)
    couple(c_down, 0)
    couple(c_up, 0)
    share_c = virt_end(c_far, on_c)
    slabs_sib_on(1)
    share_a.wait_recv()
    couple(other(c_down), 0)
    share_b.wait_recv()
    couple(other(c_up), 0)
    couple(c_far, 0)
    share_c.wait_recv()
    couple(other(c_far), 0)

    def panel(n, orbital, **target):
        return send(rp.at[n, orbital], rp.at[n, orbital], **target)

    y_up, y_down, z_up, z_down = {}, {}, {}, {}
    share = {}

    def whole(n):
        return send(rp.at[n], rp.at[n], col=c_sib)

    def panels_out(o):
        rp[c, o] = acc[o].astype(BF)
        y_up[1, o] = send(rp.at[c, o], qp.at[1, o], row=r_up)
        y_down[1, o] = send(rp.at[c, o], qp.at[2, o], row=r_down)
        z_up[o] = panel(c, o, col=c_up)
        z_down[o] = panel(c, o, col=c_down)
        qp[0, o] = rp[c, o]

    def y_step(step, o):
        slot = 2 * step - 1
        y_up[step, o].wait_recv()
        y_up[step + 1, o] = send(qp.at[slot, o], qp.at[slot + 2, o], row=r_up)
        y_down[step, o].wait_recv()
        if step == 2 and o == 1:
            return
        y_down[step + 1, o] = send(qp.at[slot + 1, o], qp.at[slot + 3, o], row=r_down)

    def weigh(n, o):
        product = wcol[o] * rp[n, o].astype(F32)
        wl[o, n] = product.astype(BF).T

    panels_out(0)
    slabs_end(1)

    @pl.loop(0, RING)
    def _(n):
        couple(n, 1)

    panels_out(1)
    first_stage = len(links.copies)
    y_step(1, 1)
    z_down[0].wait_recv()
    z_down["far"] = panel(c_up, 0, col=c_down)
    share["own"] = whole(c)
    y_step(1, 0)
    z_up[1].wait_recv()
    z_up["far"] = panel(c_down, 1, col=c_up)
    z_up[0].wait_recv()
    weigh(c, 1)
    z_down[1].wait_recv()
    weigh(c_up, 0)
    weigh(c_down, 0)
    links.retire(24)
    links.retire(40)
    share["down"] = whole(c_down)
    share["own"].wait_recv()
    weigh(c_sib, 0)
    weigh(c, 0)
    y_step(2, 1)
    y_step(2, 0)
    weigh(c_sib, 1)
    z_down["far"].wait_recv()
    weigh(c_down, 1)
    share["down"].wait_recv()
    share["up"] = whole(c_up)
    weigh(c_down_sib, 1)
    weigh(c_far, 0)
    z_up["far"].wait_recv()
    share["far"] = whole(c_far)
    weigh(c_down_sib, 0)
    weigh(c_far, 1)
    weigh(c_up, 1)
    y_up[3, 1].wait_recv()
    y_up[4, 1] = send(qp.at[5, 1], qp.at[7, 1], row=r_up)
    y_down[3, 0].wait_recv()
    y_down[4, 0] = send(qp.at[6, 0], qp.at[7, 0], row=r_down)
    share["up"].wait_recv()
    weigh(c_up_sib, 0)
    share["far"].wait_recv()
    weigh(c_far_sib, 0)
    weigh(c_up_sib, 1)
    weigh(c_far_sib, 1)

    low, high = slice(0, 64), slice(64, 128)
    targets = {"far": d_far, "up": d_up, "down": d_down, "own": d}

    def terms_of(name, slots):
        terms = 0.0
        for o in range(2):
            rows = wl[o, pl.ds(2 * (targets[name] // 2), 2)].reshape(256, 432)
            columns = jnp.concatenate([qp[slot, o] for slot in slots], axis=1)
            terms += jnp.dot(rows, columns, preferred_element_type=F32)
        return terms.reshape(2, 128, LANES * len(slots))

    class RingSum:
        def __init__(self, raw, land, keep, own):
            self.raw, self.land, self.keep, self.own, self.copies = raw, land, keep, own, {}

        def send(self, at, value, **target):
            self.raw[at] = value.astype(BF)
            self.copies[at] = send(self.raw.at[at], self.land.at[at], **target)

        def give(self, name, block):
            if name == "far":
                self.send(0, block[:, high], depth=d_up)
                self.send(1, block[:, low], depth=d_down)
            elif name == "up":
                self.send(2, block[:, low], depth=d_up)
                self.keep[0] = block[:, high]
            elif name == "down":
                self.send(3, block[:, high], depth=d_down)
                self.keep[1] = block[:, low]
            else:
                self.own[...] = block

        def pass_on(self, at):
            self.copies[at].wait_recv()
            self.send(at + 4, self.keep[at] + self.land[at].astype(F32), depth=(d_up, d_down)[at])

        def end(self):
            for at in (2, 3, 4, 5):
                self.copies[at].wait_recv()
            land = self.land
            self.own[:, low] = self.own[:, low] + land[2].astype(F32) + land[5].astype(F32)
            self.own[:, high] = self.own[:, high] + land[3].astype(F32) + land[4].astype(F32)

    plane = lax.rem(d, 2)
    slots_a, slots_b = (5, 7), (0, 2, 4)
    ring_a = RingSum(a_raw, a_land, a_keep, a_own)
    ring_b = RingSum(b_raw, b_land, b_keep, b_own)
    b_pair = {}
    def gram_b(at, name):
        b_terms[at] = terms_of(name, slots_b)
        b_give[at] = b_terms[at, 1 - plane].astype(BF)
        b_pair[name] = send(b_give.at[at], b_take.at[at], depth=d_sib)

    def pair_b(at, name):
        b_pair[name].wait_recv()
        ring_b.give(name, (b_terms[at, plane] + b_take[at].astype(F32))[None])

    rows_of = {0: r, 2: r_up, 4: lax.rem(r + 2, RING), 5: lax.rem(r + 5, RING), 7: lax.rem(r + 4, RING)}
    mine = tile_sems.at[c]

    def tiles_out(slots, total):
        for at, slot in enumerate(slots):
            red[slot] = total[:, LANES * at : LANES * at + LANES]
        for slot in slots:
            to = rows_of[slot]
            copy = links.plan(red.at[slot], tile_land.at[c], recv_sem=mine, col=to)
            straight[slot] = to, copy
            pl.when(to != c)(copy.start)
            if slot in (2, 4, 5):
                links.plan(red.at[slot], tile_land.at[c], recv_sem=mine, row=to, col=r).start()

    straight = {}

    gram_b(0, "far")
    gram_b(1, "up")
    gram_b(2, "down")
    y_up[3, 0].wait_recv()
    y_up[4, 1].wait_recv()
    y_down[4, 0].wait_recv()
    ring_a.give("far", terms_of("far", slots_a))
    ring_a.give("down", terms_of("down", slots_a))
    pair_b(0, "far")
    ring_a.give("up", terms_of("up", slots_a))
    gram_b(3, "own")
    ring_a.pass_on(1)
    ring_a.pass_on(0)
    pair_b(1, "up")
    pair_b(2, "down")
    ring_a.give("own", terms_of("own", slots_a))
    links.retire(first_stage)
    ring_b.pass_on(0)
    ring_b.pass_on(1)
    ring_a.end()
    a_sib[...] = a_own[1 - plane].astype(BF)
    last = send(a_sib, a_last, depth=d_sib)
    pair_b(3, "own")
    ring_b.end()
    tiles_out(slots_b, b_own[0].astype(BF))
    last.wait_recv()
    tiles_out(slots_a, (a_own[plane] + a_last[...].astype(F32)).astype(BF))

    before = len(links.copies) - 8
    links.retire(before)
    for slot, (to, _) in straight.items():

        @pl.when(to == c)
        def _(slot=slot):
            tile_land[c] = red[slot]

    for n in range(RING):

        @pl.when(jnp.logical_or(turned, c != n))
        def _(n=n):
            pltpu.make_async_remote_copy(
                src_ref=red.at[0],
                dst_ref=tile_land.at[n],
                send_sem=send_sems.at[before],
                recv_sem=tile_sems.at[n],
                device_id=links.place(col=c_sib),
                device_id_type=MESH,
            ).wait_recv()

    @pl.when(turned)
    def _():
        for n in range(RING):
            parts[d, n] = tile_land[n].T

    @pl.when(jnp.logical_not(turned))
    def _():
        parts[d] = tile_land[...]

    def pass_on(n, begin, size, **target):
        piece = parts.at[n, pl.ds(begin, size)]
        return send(piece, piece, **target)

    def settle(n):
        @pl.when(turned)
        def _():
            at = pl.ds(pl.multiple_of(LANES * n, LANES), LANES)
            for m in range(RING):
                out_ref[m, :, at] = parts[n, m]

        @pl.when(jnp.logical_not(turned))
        def _():
            for m in range(RING):
                out_ref[n, :, LANES * m : LANES * m + LANES] = parts[n, m]

    first_gather = len(links.copies)
    pair = pass_on(d, 0, 4, depth=d_sib)
    b_up = pass_on(d, 4, 4, depth=d_up)
    b_down = pass_on(d, 4, 4, depth=d_down)
    b_pairs = [pass_on(d, 4, 4, depth=d_sib)]
    a_up = pass_on(d, 0, 4, depth=d_up)
    a_down = pass_on(d, 0, 4, depth=d_down)
    for slot, (to, copy) in straight.items():
        pl.when(to != c)(copy.wait_send)
    for at in range(before, first_gather):
        if all(links.copies[at] is not copy for _, copy in straight.values()):
            links.copies[at].wait_send()
    links.retired = first_gather
    settle(d)
    pair.wait_recv()
    a_up2 = pass_on(d_sib, 0, 4, depth=d_up)
    a_down2 = pass_on(d_sib, 0, 4, depth=d_down)
    b_up.wait_recv()
    b_up2 = pass_on(d_down, 6, 2, depth=d_up)
    b_pairs.append(pass_on(d_down, 4, 4, depth=d_sib))
    b_down.wait_recv()
    b_down2 = pass_on(d_up, 4, 2, depth=d_down)
    b_pairs.append(pass_on(d_up, 4, 4, depth=d_sib))
    a_up.wait_recv()
    a_up3 = pass_on(d_down, 2, 2, depth=d_up)
    a_down.wait_recv()
    a_down3 = pass_on(d_up, 0, 2, depth=d_down)
    settle(d_up)
    settle(d_down)
    b_up2.wait_recv()
    b_pairs.append(pass_on(d_far, 6, 2, depth=d_sib))
    b_down2.wait_recv()
    b_pairs.append(pass_on(d_far, 4, 2, depth=d_sib))
    a_up2.wait_recv()
    a_up4 = pass_on(other(d_down), 2, 2, depth=d_up)
    a_down2.wait_recv()
    a_down4 = pass_on(other(d_up), 0, 2, depth=d_down)
    links.retire(len(links.copies) - 6)
    b_pairs[0].wait_recv()
    settle(d_sib)
    a_up3.wait_recv()
    a_down3.wait_recv()
    settle(d_far)
    b_pairs[1].wait_recv()
    settle(other(d_down))
    b_pairs[2].wait_recv()
    settle(other(d_up))
    for copy in (a_up4, a_down4, *b_pairs[3:]):
        copy.wait_recv()
    settle(other(d_far))
    links.retire()


def on_device(half_slabs, virtuals, occupied_energy, virtual_energy, frequency):
    vmem = pl.BlockSpec(memory_space=pltpu.VMEM)
    excitation = virtual_energy[None, :] - occupied_energy[:, None]
    weight = 4.0 * excitation / (excitation * excitation + frequency[0] * frequency[0])
    copies = 128
    gram = pl.pallas_call(
        gather_kernel,
        out_shape=jax.ShapeDtypeStruct((RING, 128, 1024), BF),
        in_specs=[vmem] * 3,
        out_specs=vmem,
        scratch_shapes=[
            pltpu.VMEM((RING, 4, 432, LANES), BF),
            pltpu.VMEM((RING, 2, 512, LANES), BF),
            pltpu.VMEM((2, 432, LANES), F32),
            pltpu.VMEM((RING, 2, 432, LANES), BF),
            pltpu.VMEM((RING, 2, 432, LANES), BF),
            pltpu.VMEM((LANES, 512), F32),
            pltpu.VMEM((2, 432, LANES), F32),
            pltpu.VMEM((2, RING, 128, 432), BF),
            pltpu.VMEM((6, 2, 64, 256), BF),
            pltpu.VMEM((6, 2, 64, 256), BF),
            pltpu.VMEM((2, 2, 64, 256), F32),
            pltpu.VMEM((2, 128, 256), F32),
            pltpu.VMEM((128, 256), BF),
            pltpu.VMEM((128, 256), BF),
            pltpu.VMEM((4, 2, 128, 384), F32),
            pltpu.VMEM((6, 1, 64, 384), BF),
            pltpu.VMEM((6, 1, 64, 384), BF),
            pltpu.VMEM((2, 1, 64, 384), F32),
            pltpu.VMEM((1, 128, 384), F32),
            pltpu.VMEM((4, 128, 384), BF),
            pltpu.VMEM((4, 128, 384), BF),
            pltpu.VMEM((RING, 128, LANES), BF),
            pltpu.VMEM((RING, 128, LANES), BF),
            pltpu.VMEM((RING, RING, 128, LANES), BF),
            pltpu.SemaphoreType.DMA((copies,)),
            pltpu.SemaphoreType.DMA((copies,)),
            pltpu.SemaphoreType.DMA((RING,)),
        ],
        compiler_params=pltpu.CompilerParams(
            collective_id=0, has_side_effects=True, vmem_limit_bytes=48 * 2**20
        ),
        cost_estimate=pl.CostEstimate(flops=2_700_000_000, bytes_accessed=3_000_000, transcendentals=0),
    )(half_slabs, virtuals.T, weight)
    return gram.reshape(1024, 1024).astype(F32)


def solution(mesh):
    placed = (P(None, "depth", ("row", "col")), P("col", "depth"), P(), P("depth"), P())
    return jax.shard_map(
        on_device, mesh=mesh, in_specs=placed, out_specs=P("row", "col"), check_vma=False
    )
```

```python
import jax
import jax.numpy as jnp
from jax import lax
from jax.experimental import pallas as pl
from jax.experimental.pallas import tpu as pltpu
from jax.sharding import PartitionSpec as P

MESH = pl.DeviceIdType.MESH
BF = jnp.bfloat16
F32 = jnp.float32
RING = 8
LANES = 128


class Links:
    def __init__(self, here, send_sems, recv_sems):
        self.here, self.send_sems, self.recv_sems = here, send_sems, recv_sems
        self.copies, self.retired = [], 0

    def place(self, **target):
        at = {**self.here, **target}
        return at["depth"], at["row"], at["col"]

    def plan(self, src, dst, recv_sem=None, **target):
        at = len(self.copies)
        copy = pltpu.make_async_remote_copy(
            src_ref=src,
            dst_ref=dst,
            send_sem=self.send_sems.at[at],
            recv_sem=self.recv_sems.at[at] if recv_sem is None else recv_sem,
            device_id=self.place(**target),
            device_id_type=MESH,
        )
        self.copies.append(copy)
        return copy

    def send(self, src, dst, **target):
        copy = self.plan(src, dst, **target)
        copy.start()
        return copy

    def retire(self, upto=None):
        for copy in self.copies[self.retired : upto]:
            copy.wait_send()
        self.retired = len(self.copies) if upto is None else upto


def around(me):
    up, down, far = lax.rem(me + 2, RING), lax.rem(me + 6, RING), lax.rem(me + 4, RING)
    return up, down, far, me + 1 - 2 * lax.rem(me, 2)


def other(at):
    return at + 1 - 2 * lax.rem(at, 2)


def gather_kernel(
    slabs_ref, virt_ref, weight_ref, out_ref,
    vq, hs, acc, rp, qp, wrow, wcol, wl,
    a_raw, a_land, a_keep, a_own, a_sib, a_last,
    b_terms, b_raw, b_land, b_keep, b_own, b_give, b_take, red, tile_land, parts,
    send_sems, recv_sems, tile_sems,
):
    d, r, c = lax.axis_index("depth"), lax.axis_index("row"), lax.axis_index("col")
    d_up, d_down, d_far, d_sib = around(d)
    c_up, c_down, c_far, c_sib = around(c)
    r_up, r_down = lax.rem(r + 1, RING), lax.rem(r + 7, RING)
    links = Links({"depth": d, "row": r, "col": c}, send_sems, recv_sems)
    send = links.send

    barrier = pltpu.get_barrier_semaphore()
    c_far_sib, c_up_sib, c_down_sib = other(c_far), other(c_up), other(c_down)
    partners = [links.place(depth=to) for to in (d_up, d_down, d_sib)]
    partners += [links.place(row=to) for to in (r_up, r_down)]
    partners += [links.place(col=to) for to in (c_up, c_down, c_far, c_sib, c_up_sib, c_down_sib, c_far_sib)]
    for partner in partners:
        pl.semaphore_signal(barrier, inc=1, device_id=partner, device_id_type=MESH)
    apart = lax.rem(c - r + RING, RING)
    turned = jnp.logical_or(jnp.logical_or(apart == 3, apart == 6), apart == 7)

    @pl.when(turned)
    def _():
        for n in range(RING):
            pl.semaphore_signal(barrier, inc=1, device_id=links.place(row=c, col=n), device_id_type=MESH)

    nvir, nbas = virt_ref.shape
    vq[c, 3] = jnp.zeros((nvir, LANES), BF)
    for quarter in range(3):
        vq[c, quarter] = virt_ref[:, LANES * quarter : LANES * quarter + LANES]
    vq[c, 3, :, 0 : nbas - 384] = virt_ref[:, 384:nbas]
    for orbital in range(2):
        hs[d, orbital, 496:512, :] = jnp.zeros((16, LANES), BF)
        hs[d, orbital, 0:nbas, :] = slabs_ref[orbital]

    pl.semaphore_wait(barrier, len(partners) + 3)

    j = lax.rem(r, 4)
    j_up, j_down = lax.rem(j + 1, 4), lax.rem(j + 3, 4)
    spans = (pl.ds(0, 208), pl.ds(208, 224))

    def slab(n, orbital, half=None, **target):
        piece = hs.at[n, orbital] if half is None else hs.at[n, orbital, pl.ds(256 * half, 256)]
        return send(piece, piece, **target)

    def virt(n, quarter, half=None, **target):
        piece = vq.at[n, quarter] if half is None else vq.at[n, quarter, spans[half]]
        return send(piece, piece, **target)

    def virt_rows(n):
        return virt(n, j, row=r_up), virt(n, j, row=r_down)

    pair, up, down, up2, down2, up3, down3, up4, down4 = ({} for _ in range(9))

    def slabs_out(o):
        up[o], down[o] = slab(d, o, depth=d_up), slab(d, o, depth=d_down)

    def slabs_sib(o):
        pair[o].wait_recv()
        up2[o], down2[o] = slab(d_sib, o, depth=d_up), slab(d_sib, o, depth=d_down)

    def slabs_on(o):
        up[o].wait_recv()
        up3[o] = slab(d_down, o, 1, depth=d_up)
        down[o].wait_recv()
        down3[o] = slab(d_up, o, 0, depth=d_down)

    def slabs_sib_on(o):
        up2[o].wait_recv()
        up4[o] = slab(other(d_down), o, 1, depth=d_up)
        down2[o].wait_recv()
        down4[o] = slab(other(d_up), o, 0, depth=d_down)

    def slabs_end(o):
        for copy in (up3[o], down3[o], up4[o], down4[o]):
            copy.wait_recv()

    z_up = virt(c, j, col=c_up)
    z_down = virt(c, j, col=c_down)
    slabs_out(0)
    pair[0] = slab(d, 0, depth=d_sib)
    share_virt = send(vq.at[c], vq.at[c], col=c_sib)
    slabs_out(1)

    z_up.wait_recv()
    z_up2 = virt(c_down, j, 1, col=c_up)
    rows_a = virt_rows(c_down)
    z_down.wait_recv()
    z_down2 = virt(c_up, j, 0, col=c_down)
    rows_b = virt_rows(c_up)
    slabs_sib(0)
    slabs_on(0)
    z_up2.wait_recv()
    z_down2.wait_recv()
    rows_c = virt_rows(c_far)
    pair[1] = slab(d, 1, depth=d_sib)

    def pass_rows(n, rows):
        rows[0].wait_recv()
        if n is c_down:
            one = (virt(n, j_down, row=r_up),)
        elif n is c_far:
            one = (virt(n, j_down, 1, row=r_up),)
        else:
            one = ()
        rows[1].wait_recv()
        if n is c_up:
            one += (virt(n, j_up, row=r_down),)
        elif n is c_far:
            one += (virt(n, j_up, 0, row=r_down),)
        return one

    on_a = pass_rows(c_down, rows_a)
    on_b = pass_rows(c_up, rows_b)
    slabs_sib_on(0)
    on_c = pass_rows(c_far, rows_c)
    slabs_sib(1)
    slabs_on(1)

    wrow[...] = jnp.zeros_like(wrow)
    for orbital in range(2):
        wrow[:, 0:nvir] = jnp.broadcast_to(weight_ref[orbital : orbital + 1, :], (LANES, nvir))
        wcol[orbital] = wrow[...].T[0:nvir, :]
    acc[...] = jnp.zeros_like(acc)

    def virt_end(n, on):
        for copy in on:
            copy.wait_recv()
        return send(vq.at[n], vq.at[n], col=c_sib)

    def couple(n, orbital):
        left = jnp.concatenate([vq[n, 0], vq[n, 1], vq[n, 2], vq[n, 3]], axis=1)
        acc[orbital] += jnp.dot(left, hs[n, orbital], preferred_element_type=F32)

    share_a = virt_end(c_down, on_a)
    share_b = virt_end(c_up, on_b)
    slabs_end(0)
    couple(c, 0)
    share_virt.wait_recv()
    couple(c_sib, 0)
    couple(c_down, 0)
    couple(c_up, 0)
    share_c = virt_end(c_far, on_c)
    slabs_sib_on(1)
    share_a.wait_recv()
    couple(other(c_down), 0)
    share_b.wait_recv()
    couple(other(c_up), 0)
    couple(c_far, 0)
    share_c.wait_recv()
    couple(other(c_far), 0)

    def panel(n, orbital, **target):
        return send(rp.at[n, orbital], rp.at[n, orbital], **target)

    y_up, y_down, z_up, z_down = {}, {}, {}, {}
    share = {}

    def whole(n):
        return send(rp.at[n], rp.at[n], col=c_sib)

    def panels_out(o):
        rp[c, o] = acc[o].astype(BF)
        y_up[1, o] = send(rp.at[c, o], qp.at[1, o], row=r_up)
        y_down[1, o] = send(rp.at[c, o], qp.at[2, o], row=r_down)
        z_up[o] = panel(c, o, col=c_up)
        z_down[o] = panel(c, o, col=c_down)
        qp[0, o] = rp[c, o]

    def y_step(step, o):
        slot = 2 * step - 1
        y_up[step, o].wait_recv()
        y_up[step + 1, o] = send(qp.at[slot, o], qp.at[slot + 2, o], row=r_up)
        y_down[step, o].wait_recv()
        if step == 2 and o == 1:
            return
        y_down[step + 1, o] = send(qp.at[slot + 1, o], qp.at[slot + 3, o], row=r_down)

    def weigh(n, o):
        product = wcol[o] * rp[n, o].astype(F32)
        wl[o, n] = product.astype(BF).T

    panels_out(0)
    slabs_end(1)

    @pl.loop(0, RING)
    def _(n):
        couple(n, 1)

    panels_out(1)
    first_stage = len(links.copies)
    y_step(1, 1)
    z_down[0].wait_recv()
    z_down["far"] = panel(c_up, 0, col=c_down)
    share["own"] = whole(c)
    y_step(1, 0)
    z_up[1].wait_recv()
    z_up["far"] = panel(c_down, 1, col=c_up)
    z_up[0].wait_recv()
    weigh(c, 1)
    z_down[1].wait_recv()
    weigh(c_up, 0)
    weigh(c_down, 0)
    links.retire(24)
    links.retire(40)
    share["down"] = whole(c_down)
    share["own"].wait_recv()
    weigh(c_sib, 0)
    weigh(c, 0)
    y_step(2, 1)
    y_step(2, 0)
    weigh(c_sib, 1)
    z_down["far"].wait_recv()
    weigh(c_down, 1)
    share["down"].wait_recv()
    share["up"] = whole(c_up)
    weigh(c_down_sib, 1)
    weigh(c_far, 0)
    z_up["far"].wait_recv()
    share["far"] = whole(c_far)
    weigh(c_down_sib, 0)
    weigh(c_far, 1)
    weigh(c_up, 1)
    y_up[3, 1].wait_recv()
    y_up[4, 1] = send(qp.at[5, 1], qp.at[7, 1], row=r_up)
    y_down[3, 0].wait_recv()
    y_down[4, 0] = send(qp.at[6, 0], qp.at[7, 0], row=r_down)
    share["up"].wait_recv()
    weigh(c_up_sib, 0)
    share["far"].wait_recv()
    weigh(c_far_sib, 0)
    weigh(c_up_sib, 1)
    weigh(c_far_sib, 1)

    low, high = slice(0, 64), slice(64, 128)
    targets = {"far": d_far, "up": d_up, "down": d_down, "own": d}

    def terms_of(name, slots):
        terms = 0.0
        for o in range(2):
            rows = wl[o, pl.ds(2 * (targets[name] // 2), 2)].reshape(256, 432)
            columns = jnp.concatenate([qp[slot, o] for slot in slots], axis=1)
            terms += jnp.dot(rows, columns, preferred_element_type=F32)
        return terms.reshape(2, 128, LANES * len(slots))

    class RingSum:
        def __init__(self, raw, land, keep, own):
            self.raw, self.land, self.keep, self.own, self.copies = raw, land, keep, own, {}

        def send(self, at, value, **target):
            self.raw[at] = value.astype(BF)
            self.copies[at] = send(self.raw.at[at], self.land.at[at], **target)

        def give(self, name, block):
            if name == "far":
                self.send(0, block[:, high], depth=d_up)
                self.send(1, block[:, low], depth=d_down)
            elif name == "up":
                self.send(2, block[:, low], depth=d_up)
                self.keep[0] = block[:, high]
            elif name == "down":
                self.send(3, block[:, high], depth=d_down)
                self.keep[1] = block[:, low]
            else:
                self.own[...] = block

        def pass_on(self, at):
            self.copies[at].wait_recv()
            self.send(at + 4, self.keep[at] + self.land[at].astype(F32), depth=(d_up, d_down)[at])

        def end(self):
            for at in (2, 3, 4, 5):
                self.copies[at].wait_recv()
            land = self.land
            self.own[:, low] = self.own[:, low] + land[2].astype(F32) + land[5].astype(F32)
            self.own[:, high] = self.own[:, high] + land[3].astype(F32) + land[4].astype(F32)

    plane = lax.rem(d, 2)
    slots_a, slots_b = (5, 7), (0, 2, 4)
    ring_a = RingSum(a_raw, a_land, a_keep, a_own)
    ring_b = RingSum(b_raw, b_land, b_keep, b_own)
    b_pair = {}
    def gram_b(at, name):
        b_terms[at] = terms_of(name, slots_b)
        b_give[at] = b_terms[at, 1 - plane].astype(BF)
        b_pair[name] = send(b_give.at[at], b_take.at[at], depth=d_sib)

    def pair_b(at, name):
        b_pair[name].wait_recv()
        ring_b.give(name, (b_terms[at, plane] + b_take[at].astype(F32))[None])

    rows_of = {0: r, 2: r_up, 4: lax.rem(r + 2, RING), 5: lax.rem(r + 5, RING), 7: lax.rem(r + 4, RING)}
    mine = tile_sems.at[c]

    def tiles_out(slots, total):
        for at, slot in enumerate(slots):
            red[slot] = total[:, LANES * at : LANES * at + LANES]
        for slot in slots:
            to = rows_of[slot]
            copy = links.plan(red.at[slot], tile_land.at[c], recv_sem=mine, col=to)
            straight[slot] = to, copy
            pl.when(to != c)(copy.start)
            if slot in (2, 4, 5):
                links.plan(red.at[slot], tile_land.at[c], recv_sem=mine, row=to, col=r).start()

    straight = {}

    gram_b(0, "far")
    gram_b(1, "up")
    gram_b(2, "down")
    y_up[3, 0].wait_recv()
    y_up[4, 1].wait_recv()
    y_down[4, 0].wait_recv()
    ring_a.give("far", terms_of("far", slots_a))
    ring_a.give("down", terms_of("down", slots_a))
    pair_b(0, "far")
    ring_a.give("up", terms_of("up", slots_a))
    gram_b(3, "own")
    ring_a.pass_on(1)
    ring_a.pass_on(0)
    pair_b(1, "up")
    pair_b(2, "down")
    ring_a.give("own", terms_of("own", slots_a))
    links.retire(first_stage)
    ring_b.pass_on(0)
    ring_b.pass_on(1)
    ring_a.end()
    a_sib[...] = a_own[1 - plane].astype(BF)
    last = send(a_sib, a_last, depth=d_sib)
    pair_b(3, "own")
    ring_b.end()
    tiles_out(slots_b, b_own[0].astype(BF))
    last.wait_recv()
    tiles_out(slots_a, (a_own[plane] + a_last[...].astype(F32)).astype(BF))

    before = len(links.copies) - 8
    links.retire(before)
    for slot, (to, _) in straight.items():

        @pl.when(to == c)
        def _(slot=slot):
            tile_land[c] = red[slot]

    def columns_of(place):
        pair_at = lax.rem(c // 2 + place, 4)
        return [(2 * place + core, 2 * pair_at + core) for core in range(2)]

    def tiles_in(places):
        for place in places:
            for at, n in columns_of(place):

                @pl.when(jnp.logical_or(turned, c != n))
                def _(n=n):
                    pltpu.make_async_remote_copy(
                        src_ref=red.at[0],
                        dst_ref=tile_land.at[n],
                        send_sem=send_sems.at[before],
                        recv_sem=tile_sems.at[n],
                        device_id=links.place(col=c_sib),
                        device_id_type=MESH,
                    ).wait_recv()

                @pl.when(turned)
                def _(at=at, n=n):
                    parts[d, at] = tile_land[n].T

                @pl.when(jnp.logical_not(turned))
                def _(at=at, n=n):
                    parts[d, at] = tile_land[n]

    def pass_on(n, begin, size, **target):
        piece = parts.at[n, pl.ds(begin, size)]
        return send(piece, piece, **target)

    def settle(n):
        targets_of = [pair for place in range(4) for pair in columns_of(place)]

        @pl.when(turned)
        def _():
            for at, m in targets_of:
                out_ref[m, :, pl.ds(pl.multiple_of(LANES * n, LANES), LANES)] = parts[n, at]

        @pl.when(jnp.logical_not(turned))
        def _():
            for at, m in targets_of:
                out_ref[n, :, pl.ds(pl.multiple_of(LANES * m, LANES), LANES)] = parts[n, at]

    first_gather = len(links.copies)
    tiles_in((0, 1))
    pair = pass_on(d, 0, 4, depth=d_sib)
    a_up = pass_on(d, 0, 4, depth=d_up)
    a_down = pass_on(d, 0, 4, depth=d_down)
    tiles_in((3, 2))
    b_up = pass_on(d, 4, 4, depth=d_up)
    b_down = pass_on(d, 4, 4, depth=d_down)
    b_pairs = [pass_on(d, 4, 4, depth=d_sib)]
    for slot, (to, copy) in straight.items():
        pl.when(to != c)(copy.wait_send)
    for at in range(before, first_gather):
        if all(links.copies[at] is not copy for _, copy in straight.values()):
            links.copies[at].wait_send()
    links.retired = first_gather
    settle(d)
    pair.wait_recv()
    a_up2 = pass_on(d_sib, 0, 4, depth=d_up)
    a_down2 = pass_on(d_sib, 0, 4, depth=d_down)
    b_up.wait_recv()
    b_up2 = pass_on(d_down, 6, 2, depth=d_up)
    b_pairs.append(pass_on(d_down, 4, 4, depth=d_sib))
    b_down.wait_recv()
    b_down2 = pass_on(d_up, 4, 2, depth=d_down)
    b_pairs.append(pass_on(d_up, 4, 4, depth=d_sib))
    a_up.wait_recv()
    a_up3 = pass_on(d_down, 2, 2, depth=d_up)
    a_down.wait_recv()
    a_down3 = pass_on(d_up, 0, 2, depth=d_down)
    settle(d_up)
    settle(d_down)
    b_up2.wait_recv()
    b_pairs.append(pass_on(d_far, 6, 2, depth=d_sib))
    b_down2.wait_recv()
    b_pairs.append(pass_on(d_far, 4, 2, depth=d_sib))
    a_up2.wait_recv()
    a_up4 = pass_on(other(d_down), 2, 2, depth=d_up)
    a_down2.wait_recv()
    a_down4 = pass_on(other(d_up), 0, 2, depth=d_down)
    links.retire(len(links.copies) - 6)
    b_pairs[0].wait_recv()
    settle(d_sib)
    a_up3.wait_recv()
    a_down3.wait_recv()
    settle(d_far)
    b_pairs[1].wait_recv()
    settle(other(d_down))
    b_pairs[2].wait_recv()
    settle(other(d_up))
    for copy in (a_up4, a_down4, *b_pairs[3:]):
        copy.wait_recv()
    settle(other(d_far))
    links.retire()


def on_device(half_slabs, virtuals, occupied_energy, virtual_energy, frequency):
    vmem = pl.BlockSpec(memory_space=pltpu.VMEM)
    excitation = virtual_energy[None, :] - occupied_energy[:, None]
    weight = 4.0 * excitation / (excitation * excitation + frequency[0] * frequency[0])
    copies = 128
    gram = pl.pallas_call(
        gather_kernel,
        out_shape=jax.ShapeDtypeStruct((RING, 128, 1024), BF),
        in_specs=[vmem] * 3,
        out_specs=vmem,
        scratch_shapes=[
            pltpu.VMEM((RING, 4, 432, LANES), BF),
            pltpu.VMEM((RING, 2, 512, LANES), BF),
            pltpu.VMEM((2, 432, LANES), F32),
            pltpu.VMEM((RING, 2, 432, LANES), BF),
            pltpu.VMEM((RING, 2, 432, LANES), BF),
            pltpu.VMEM((LANES, 512), F32),
            pltpu.VMEM((2, 432, LANES), F32),
            pltpu.VMEM((2, RING, 128, 432), BF),
            pltpu.VMEM((6, 2, 64, 256), BF),
            pltpu.VMEM((6, 2, 64, 256), BF),
            pltpu.VMEM((2, 2, 64, 256), F32),
            pltpu.VMEM((2, 128, 256), F32),
            pltpu.VMEM((128, 256), BF),
            pltpu.VMEM((128, 256), BF),
            pltpu.VMEM((4, 2, 128, 384), F32),
            pltpu.VMEM((6, 1, 64, 384), BF),
            pltpu.VMEM((6, 1, 64, 384), BF),
            pltpu.VMEM((2, 1, 64, 384), F32),
            pltpu.VMEM((1, 128, 384), F32),
            pltpu.VMEM((4, 128, 384), BF),
            pltpu.VMEM((4, 128, 384), BF),
            pltpu.VMEM((RING, 128, LANES), BF),
            pltpu.VMEM((RING, 128, LANES), BF),
            pltpu.VMEM((RING, RING, 128, LANES), BF),
            pltpu.SemaphoreType.DMA((copies,)),
            pltpu.SemaphoreType.DMA((copies,)),
            pltpu.SemaphoreType.DMA((RING,)),
        ],
        compiler_params=pltpu.CompilerParams(
            collective_id=0, has_side_effects=True, vmem_limit_bytes=48 * 2**20
        ),
        cost_estimate=pl.CostEstimate(flops=2_700_000_000, bytes_accessed=3_000_000, transcendentals=0),
    )(half_slabs, virtuals.T, weight)
    return gram.reshape(1024, 1024).astype(F32)


def solution(mesh):
    placed = (P(None, "depth", ("row", "col")), P("col", "depth"), P(), P("depth"), P())
    return jax.shard_map(
        on_device, mesh=mesh, in_specs=placed, out_specs=P("row", "col"), check_vma=False
    )
```

```python
import jax
import jax.numpy as jnp
from jax import lax
from jax.experimental import pallas as pl
from jax.experimental.pallas import tpu as pltpu
from jax.sharding import PartitionSpec as P

MESH = pl.DeviceIdType.MESH
BF = jnp.bfloat16
F32 = jnp.float32
RING = 8
LANES = 128


class Links:
    def __init__(self, here, send_sems, recv_sems):
        self.here, self.send_sems, self.recv_sems = here, send_sems, recv_sems
        self.copies, self.retired = [], 0

    def place(self, **target):
        at = {**self.here, **target}
        return at["depth"], at["row"], at["col"]

    def plan(self, src, dst, recv_sem=None, **target):
        at = len(self.copies)
        copy = pltpu.make_async_remote_copy(
            src_ref=src,
            dst_ref=dst,
            send_sem=self.send_sems.at[at],
            recv_sem=self.recv_sems.at[at] if recv_sem is None else recv_sem,
            device_id=self.place(**target),
            device_id_type=MESH,
        )
        self.copies.append(copy)
        return copy

    def send(self, src, dst, **target):
        copy = self.plan(src, dst, **target)
        copy.start()
        return copy

    def retire(self, upto=None):
        for copy in self.copies[self.retired : upto]:
            copy.wait_send()
        self.retired = len(self.copies) if upto is None else upto


def around(me):
    up, down, far = lax.rem(me + 2, RING), lax.rem(me + 6, RING), lax.rem(me + 4, RING)
    return up, down, far, me + 1 - 2 * lax.rem(me, 2)


def other(at):
    return at + 1 - 2 * lax.rem(at, 2)


def gather_kernel(
    slabs_ref, virt_ref, weight_ref, out_ref,
    vq, hs, acc, rp, qp, wrow, wcol, wl,
    a_raw, a_land, a_keep, a_own, a_sib, a_last,
    b_terms, b_raw, b_land, b_keep, b_own, b_give, b_take, red, tile_land, parts,
    send_sems, recv_sems, tile_sems,
):
    d, r, c = lax.axis_index("depth"), lax.axis_index("row"), lax.axis_index("col")
    d_up, d_down, d_far, d_sib = around(d)
    c_up, c_down, c_far, c_sib = around(c)
    r_up, r_down = lax.rem(r + 1, RING), lax.rem(r + 7, RING)
    links = Links({"depth": d, "row": r, "col": c}, send_sems, recv_sems)
    send = links.send

    barrier = pltpu.get_barrier_semaphore()
    c_far_sib, c_up_sib, c_down_sib = other(c_far), other(c_up), other(c_down)
    partners = [links.place(depth=to) for to in (d_up, d_down, d_sib)]
    partners += [links.place(row=to) for to in (r_up, r_down)]
    partners += [links.place(col=to) for to in (c_up, c_down, c_far, c_sib, c_up_sib, c_down_sib, c_far_sib)]
    for partner in partners:
        pl.semaphore_signal(barrier, inc=1, device_id=partner, device_id_type=MESH)
    apart = lax.rem(c - r + RING, RING)
    turned = jnp.logical_or(jnp.logical_or(apart == 3, apart == 6), apart == 7)

    @pl.when(turned)
    def _():
        for n in range(RING):
            pl.semaphore_signal(barrier, inc=1, device_id=links.place(row=c, col=n), device_id_type=MESH)

    nvir, nbas = virt_ref.shape
    vq[c, 3] = jnp.zeros((nvir, LANES), BF)
    for quarter in range(3):
        vq[c, quarter] = virt_ref[:, LANES * quarter : LANES * quarter + LANES]
    vq[c, 3, :, 0 : nbas - 384] = virt_ref[:, 384:nbas]
    for orbital in range(2):
        hs[d, orbital, 496:512, :] = jnp.zeros((16, LANES), BF)
        hs[d, orbital, 0:nbas, :] = slabs_ref[orbital]

    pl.semaphore_wait(barrier, len(partners) + 3)

    j = lax.rem(r, 4)
    j_up, j_down = lax.rem(j + 1, 4), lax.rem(j + 3, 4)
    spans = (pl.ds(0, 208), pl.ds(208, 224))

    def slab(n, orbital, half=None, **target):
        piece = hs.at[n, orbital] if half is None else hs.at[n, orbital, pl.ds(256 * half, 256)]
        return send(piece, piece, **target)

    def virt(n, quarter, half=None, **target):
        piece = vq.at[n, quarter] if half is None else vq.at[n, quarter, spans[half]]
        return send(piece, piece, **target)

    def virt_rows(n):
        return virt(n, j, row=r_up), virt(n, j, row=r_down)

    pair, up, down, up2, down2, up3, down3, up4, down4 = ({} for _ in range(9))

    def slabs_out(o):
        up[o], down[o] = slab(d, o, depth=d_up), slab(d, o, depth=d_down)

    def slabs_sib(o):
        pair[o].wait_recv()
        up2[o], down2[o] = slab(d_sib, o, depth=d_up), slab(d_sib, o, depth=d_down)

    def slabs_on(o):
        up[o].wait_recv()
        up3[o] = slab(d_down, o, 1, depth=d_up)
        down[o].wait_recv()
        down3[o] = slab(d_up, o, 0, depth=d_down)

    def slabs_sib_on(o):
        up2[o].wait_recv()
        up4[o] = slab(other(d_down), o, 1, depth=d_up)
        down2[o].wait_recv()
        down4[o] = slab(other(d_up), o, 0, depth=d_down)

    def slabs_end(o):
        for copy in (up3[o], down3[o], up4[o], down4[o]):
            copy.wait_recv()

    z_up = virt(c, j, col=c_up)
    z_down = virt(c, j, col=c_down)
    slabs_out(0)
    pair[0] = slab(d, 0, depth=d_sib)
    share_virt = send(vq.at[c], vq.at[c], col=c_sib)
    slabs_out(1)

    z_up.wait_recv()
    z_up2 = virt(c_down, j, 1, col=c_up)
    rows_a = virt_rows(c_down)
    z_down.wait_recv()
    z_down2 = virt(c_up, j, 0, col=c_down)
    rows_b = virt_rows(c_up)
    slabs_sib(0)
    slabs_on(0)
    z_up2.wait_recv()
    z_down2.wait_recv()
    rows_c = virt_rows(c_far)
    pair[1] = slab(d, 1, depth=d_sib)

    def pass_rows(n, rows):
        rows[0].wait_recv()
        if n is c_down:
            one = (virt(n, j_down, row=r_up),)
        elif n is c_far:
            one = (virt(n, j_down, 1, row=r_up),)
        else:
            one = ()
        rows[1].wait_recv()
        if n is c_up:
            one += (virt(n, j_up, row=r_down),)
        elif n is c_far:
            one += (virt(n, j_up, 0, row=r_down),)
        return one

    on_a = pass_rows(c_down, rows_a)
    on_b = pass_rows(c_up, rows_b)
    slabs_sib_on(0)
    on_c = pass_rows(c_far, rows_c)
    slabs_sib(1)
    slabs_on(1)

    wrow[...] = jnp.zeros_like(wrow)
    for orbital in range(2):
        wrow[:, 0:nvir] = jnp.broadcast_to(weight_ref[orbital : orbital + 1, :], (LANES, nvir))
        wcol[orbital] = wrow[...].T[0:nvir, :]
    acc[...] = jnp.zeros_like(acc)

    def virt_end(n, on):
        for copy in on:
            copy.wait_recv()
        return send(vq.at[n], vq.at[n], col=c_sib)

    def couple(n, orbital):
        left = jnp.concatenate([vq[n, 0], vq[n, 1], vq[n, 2], vq[n, 3]], axis=1)
        acc[orbital] += jnp.dot(left, hs[n, orbital], preferred_element_type=F32)

    share_a = virt_end(c_down, on_a)
    share_b = virt_end(c_up, on_b)
    slabs_end(0)
    couple(c, 0)
    share_virt.wait_recv()
    couple(c_sib, 0)
    couple(c_down, 0)
    couple(c_up, 0)
    share_c = virt_end(c_far, on_c)
    slabs_sib_on(1)
    share_a.wait_recv()
    couple(other(c_down), 0)
    share_b.wait_recv()
    couple(other(c_up), 0)
    couple(c_far, 0)
    share_c.wait_recv()
    couple(other(c_far), 0)

    def panel(n, orbital, **target):
        return send(rp.at[n, orbital], rp.at[n, orbital], **target)

    y_up, y_down, z_up, z_down = {}, {}, {}, {}
    share = {}

    def whole(n):
        return send(rp.at[n], rp.at[n], col=c_sib)

    def panels_out(o):
        rp[c, o] = acc[o].astype(BF)
        y_up[1, o] = send(rp.at[c, o], qp.at[1, o], row=r_up)
        y_down[1, o] = send(rp.at[c, o], qp.at[2, o], row=r_down)
        z_up[o] = panel(c, o, col=c_up)
        z_down[o] = panel(c, o, col=c_down)
        qp[0, o] = rp[c, o]

    def y_step(step, o):
        slot = 2 * step - 1
        y_up[step, o].wait_recv()
        y_up[step + 1, o] = send(qp.at[slot, o], qp.at[slot + 2, o], row=r_up)
        y_down[step, o].wait_recv()
        if step == 2 and o == 1:
            return
        y_down[step + 1, o] = send(qp.at[slot + 1, o], qp.at[slot + 3, o], row=r_down)

    def weigh(n, o):
        product = wcol[o] * rp[n, o].astype(F32)
        wl[o, n] = product.astype(BF).T

    panels_out(0)
    slabs_end(1)

    @pl.loop(0, RING)
    def _(n):
        couple(n, 1)

    panels_out(1)
    first_stage = len(links.copies)
    y_step(1, 1)
    z_down[0].wait_recv()
    z_down["far"] = panel(c_up, 0, col=c_down)
    share["own"] = whole(c)
    y_step(1, 0)
    z_up[1].wait_recv()
    z_up["far"] = panel(c_down, 1, col=c_up)
    z_up[0].wait_recv()
    weigh(c, 1)
    z_down[1].wait_recv()
    weigh(c_up, 0)
    weigh(c_down, 0)
    links.retire(24)
    links.retire(40)
    share["down"] = whole(c_down)
    share["own"].wait_recv()
    weigh(c_sib, 0)
    weigh(c, 0)
    y_step(2, 1)
    y_step(2, 0)
    weigh(c_sib, 1)
    z_down["far"].wait_recv()
    weigh(c_down, 1)
    share["down"].wait_recv()
    share["up"] = whole(c_up)
    weigh(c_down_sib, 1)
    weigh(c_far, 0)
    z_up["far"].wait_recv()
    share["far"] = whole(c_far)
    weigh(c_down_sib, 0)
    weigh(c_far, 1)
    weigh(c_up, 1)
    y_up[3, 1].wait_recv()
    y_up[4, 1] = send(qp.at[5, 1], qp.at[7, 1], row=r_up)
    y_down[3, 0].wait_recv()
    y_down[4, 0] = send(qp.at[6, 0], qp.at[7, 0], row=r_down)
    share["up"].wait_recv()
    weigh(c_up_sib, 0)
    share["far"].wait_recv()
    weigh(c_far_sib, 0)
    weigh(c_up_sib, 1)
    weigh(c_far_sib, 1)

    low, high = slice(0, 64), slice(64, 128)
    targets = {"far": d_far, "up": d_up, "down": d_down, "own": d}

    def terms_of(name, slots):
        terms = 0.0
        for o in range(2):
            rows = wl[o, pl.ds(2 * (targets[name] // 2), 2)].reshape(256, 432)
            columns = jnp.concatenate([qp[slot, o] for slot in slots], axis=1)
            terms += jnp.dot(rows, columns, preferred_element_type=F32)
        return terms.reshape(2, 128, LANES * len(slots))

    class RingSum:
        def __init__(self, raw, land, keep, own):
            self.raw, self.land, self.keep, self.own, self.copies = raw, land, keep, own, {}

        def send(self, at, value, **target):
            self.raw[at] = value.astype(BF)
            self.copies[at] = send(self.raw.at[at], self.land.at[at], **target)

        def give(self, name, block):
            if name == "far":
                self.send(0, block[:, high], depth=d_up)
                self.send(1, block[:, low], depth=d_down)
            elif name == "up":
                self.send(2, block[:, low], depth=d_up)
                self.keep[0] = block[:, high]
            elif name == "down":
                self.send(3, block[:, high], depth=d_down)
                self.keep[1] = block[:, low]
            else:
                self.own[...] = block

        def pass_on(self, at):
            self.copies[at].wait_recv()
            self.send(at + 4, self.keep[at] + self.land[at].astype(F32), depth=(d_up, d_down)[at])

        def end(self):
            for at in (2, 3, 4, 5):
                self.copies[at].wait_recv()
            land = self.land
            self.own[:, low] = self.own[:, low] + land[2].astype(F32) + land[5].astype(F32)
            self.own[:, high] = self.own[:, high] + land[3].astype(F32) + land[4].astype(F32)

    plane = lax.rem(d, 2)
    slots_a, slots_b = (5, 7), (0, 2, 4)
    ring_a = RingSum(a_raw, a_land, a_keep, a_own)
    ring_b = RingSum(b_raw, b_land, b_keep, b_own)
    b_pair = {}
    def gram_b(at, name):
        b_terms[at] = terms_of(name, slots_b)
        b_give[at] = b_terms[at, 1 - plane].astype(BF)
        if at % 2 == 1:
            b_pair[at] = send(b_give.at[pl.ds(at - 1, 2)], b_take.at[pl.ds(at - 1, 2)], depth=d_sib)

    def pair_b(at, name):
        if at % 2 == 0:
            b_pair[at + 1].wait_recv()
        ring_b.give(name, (b_terms[at, plane] + b_take[at].astype(F32))[None])

    rows_of = {0: r, 2: r_up, 4: lax.rem(r + 2, RING), 5: lax.rem(r + 5, RING), 7: lax.rem(r + 4, RING)}
    mine = tile_sems.at[c]

    def tiles_out(slots, total):
        for at, slot in enumerate(slots):
            red[slot] = total[:, LANES * at : LANES * at + LANES]
        for slot in slots:
            to = rows_of[slot]
            if slot in (2, 4, 5):
                links.plan(red.at[slot], tile_land.at[c], recv_sem=mine, row=to, col=r).start()
        for slot in slots:
            to = rows_of[slot]
            copy = links.plan(red.at[slot], tile_land.at[c], recv_sem=mine, col=to)
            straight[slot] = to, copy
            pl.when(to != c)(copy.start)

    straight = {}

    gram_b(0, "far")
    gram_b(1, "up")
    gram_b(2, "down")
    y_up[3, 0].wait_recv()
    y_up[4, 1].wait_recv()
    y_down[4, 0].wait_recv()
    ring_a.give("far", terms_of("far", slots_a))
    ring_a.give("down", terms_of("down", slots_a))
    ring_a.give("up", terms_of("up", slots_a))
    gram_b(3, "own")
    ring_a.pass_on(0)
    ring_a.give("own", terms_of("own", slots_a))
    ring_a.pass_on(1)
    pair_b(0, "far")
    ring_a.end()
    a_sib[...] = a_own[1 - plane].astype(BF)
    last = send(a_sib, a_last, depth=d_sib)
    pair_b(1, "up")
    pair_b(2, "down")
    ring_b.pass_on(0)
    pair_b(3, "own")
    ring_b.pass_on(1)
    last.wait_recv()
    tiles_out(slots_a, (a_own[plane] + a_last[...].astype(F32)).astype(BF))
    links.retire(first_stage)
    ring_b.end()
    tiles_out(slots_b, b_own[0].astype(BF))

    before = len(links.copies) - 8
    links.retire(before)
    for slot, (to, _) in straight.items():

        @pl.when(to == c)
        def _(slot=slot):
            tile_land[c] = red[slot]

    def columns_of(place):
        pair_at = lax.rem(c // 2 + place, 4)
        return [(2 * place + core, 2 * pair_at + core) for core in range(2)]

    def tiles_in(places):
        for place in places:
            for at, n in columns_of(place):

                @pl.when(jnp.logical_or(turned, c != n))
                def _(n=n):
                    pltpu.make_async_remote_copy(
                        src_ref=red.at[0],
                        dst_ref=tile_land.at[n],
                        send_sem=send_sems.at[before],
                        recv_sem=tile_sems.at[n],
                        device_id=links.place(col=c_sib),
                        device_id_type=MESH,
                    ).wait_recv()

                @pl.when(turned)
                def _(at=at, n=n):
                    parts[d, at] = tile_land[n].T

                @pl.when(jnp.logical_not(turned))
                def _(at=at, n=n):
                    parts[d, at] = tile_land[n]

    def pass_on(n, begin, size, **target):
        piece = parts.at[n, pl.ds(begin, size)]
        return send(piece, piece, **target)

    def settle(n):
        targets_of = [pair for place in range(4) for pair in columns_of(place)]

        @pl.when(turned)
        def _():
            for at, m in targets_of:
                out_ref[m, :, pl.ds(pl.multiple_of(LANES * n, LANES), LANES)] = parts[n, at]

        @pl.when(jnp.logical_not(turned))
        def _():
            for at, m in targets_of:
                out_ref[n, :, pl.ds(pl.multiple_of(LANES * m, LANES), LANES)] = parts[n, at]

    first_gather = len(links.copies)
    tiles_in((0, 1))
    pair = pass_on(d, 0, 4, depth=d_sib)
    a_up = pass_on(d, 0, 4, depth=d_up)
    a_down = pass_on(d, 0, 4, depth=d_down)
    tiles_in((3, 2))
    b_up = pass_on(d, 4, 4, depth=d_up)
    b_down = pass_on(d, 4, 4, depth=d_down)
    b_pairs = [pass_on(d, 4, 4, depth=d_sib)]
    for slot, (to, copy) in straight.items():
        pl.when(to != c)(copy.wait_send)
    for at in range(before, first_gather):
        if all(links.copies[at] is not copy for _, copy in straight.values()):
            links.copies[at].wait_send()
    links.retired = first_gather
    settle(d)
    pair.wait_recv()
    a_up2 = pass_on(d_sib, 0, 4, depth=d_up)
    a_down2 = pass_on(d_sib, 0, 4, depth=d_down)
    b_up.wait_recv()
    b_up2 = pass_on(d_down, 6, 2, depth=d_up)
    b_pairs.append(pass_on(d_down, 4, 4, depth=d_sib))
    b_down.wait_recv()
    b_down2 = pass_on(d_up, 4, 2, depth=d_down)
    b_pairs.append(pass_on(d_up, 4, 4, depth=d_sib))
    a_up.wait_recv()
    a_up3 = pass_on(d_down, 2, 2, depth=d_up)
    a_down.wait_recv()
    a_down3 = pass_on(d_up, 0, 2, depth=d_down)
    settle(d_up)
    settle(d_down)
    b_up2.wait_recv()
    b_pairs.append(pass_on(d_far, 6, 2, depth=d_sib))
    b_down2.wait_recv()
    b_pairs.append(pass_on(d_far, 4, 2, depth=d_sib))
    a_up2.wait_recv()
    a_up4 = pass_on(other(d_down), 2, 2, depth=d_up)
    a_down2.wait_recv()
    a_down4 = pass_on(other(d_up), 0, 2, depth=d_down)
    links.retire(len(links.copies) - 6)
    b_pairs[0].wait_recv()
    settle(d_sib)
    a_up3.wait_recv()
    a_down3.wait_recv()
    settle(d_far)
    b_pairs[1].wait_recv()
    settle(other(d_down))
    b_pairs[2].wait_recv()
    settle(other(d_up))
    for copy in (a_up4, a_down4, *b_pairs[3:]):
        copy.wait_recv()
    settle(other(d_far))
    links.retire()


def on_device(half_slabs, virtuals, occupied_energy, virtual_energy, frequency):
    vmem = pl.BlockSpec(memory_space=pltpu.VMEM)
    excitation = virtual_energy[None, :] - occupied_energy[:, None]
    weight = 4.0 * excitation / (excitation * excitation + frequency[0] * frequency[0])
    copies = 128
    gram = pl.pallas_call(
        gather_kernel,
        out_shape=jax.ShapeDtypeStruct((RING, 128, 1024), BF),
        in_specs=[vmem] * 3,
        out_specs=vmem,
        scratch_shapes=[
            pltpu.VMEM((RING, 4, 432, LANES), BF),
            pltpu.VMEM((RING, 2, 512, LANES), BF),
            pltpu.VMEM((2, 432, LANES), F32),
            pltpu.VMEM((RING, 2, 432, LANES), BF),
            pltpu.VMEM((RING, 2, 432, LANES), BF),
            pltpu.VMEM((LANES, 512), F32),
            pltpu.VMEM((2, 432, LANES), F32),
            pltpu.VMEM((2, RING, 128, 432), BF),
            pltpu.VMEM((6, 2, 64, 256), BF),
            pltpu.VMEM((6, 2, 64, 256), BF),
            pltpu.VMEM((2, 2, 64, 256), F32),
            pltpu.VMEM((2, 128, 256), F32),
            pltpu.VMEM((128, 256), BF),
            pltpu.VMEM((128, 256), BF),
            pltpu.VMEM((4, 2, 128, 384), F32),
            pltpu.VMEM((6, 1, 64, 384), BF),
            pltpu.VMEM((6, 1, 64, 384), BF),
            pltpu.VMEM((2, 1, 64, 384), F32),
            pltpu.VMEM((1, 128, 384), F32),
            pltpu.VMEM((4, 128, 384), BF),
            pltpu.VMEM((4, 128, 384), BF),
            pltpu.VMEM((RING, 128, LANES), BF),
            pltpu.VMEM((RING, 128, LANES), BF),
            pltpu.VMEM((RING, RING, 128, LANES), BF),
            pltpu.SemaphoreType.DMA((copies,)),
            pltpu.SemaphoreType.DMA((copies,)),
            pltpu.SemaphoreType.DMA((RING,)),
        ],
        compiler_params=pltpu.CompilerParams(
            collective_id=0, has_side_effects=True, vmem_limit_bytes=48 * 2**20
        ),
        cost_estimate=pl.CostEstimate(flops=2_700_000_000, bytes_accessed=3_000_000, transcendentals=0),
    )(half_slabs, virtuals.T, weight)
    return gram.reshape(1024, 1024).astype(F32)


def solution(mesh):
    placed = (P(None, "depth", ("row", "col")), P("col", "depth"), P(), P("depth"), P())
    return jax.shard_map(
        on_device, mesh=mesh, in_specs=placed, out_specs=P("row", "col"), check_vma=False
    )
```

```python
import jax
import jax.numpy as jnp
from jax import lax
from jax.experimental import pallas as pl
from jax.experimental.pallas import tpu as pltpu
from jax.sharding import PartitionSpec as P

MESH = pl.DeviceIdType.MESH
BF = jnp.bfloat16
F32 = jnp.float32
RING = 8
LANES = 128


class Links:
    def __init__(self, here, send_sems, recv_sems):
        self.here, self.send_sems, self.recv_sems = here, send_sems, recv_sems
        self.copies, self.retired = [], 0

    def place(self, **target):
        at = {**self.here, **target}
        return at["depth"], at["row"], at["col"]

    def plan(self, src, dst, recv_sem=None, **target):
        at = len(self.copies)
        copy = pltpu.make_async_remote_copy(
            src_ref=src,
            dst_ref=dst,
            send_sem=self.send_sems.at[at],
            recv_sem=self.recv_sems.at[at] if recv_sem is None else recv_sem,
            device_id=self.place(**target),
            device_id_type=MESH,
        )
        self.copies.append(copy)
        return copy

    def send(self, src, dst, **target):
        copy = self.plan(src, dst, **target)
        copy.start()
        return copy

    def retire(self, upto=None):
        for copy in self.copies[self.retired : upto]:
            copy.wait_send()
        self.retired = len(self.copies) if upto is None else upto


def around(me):
    up, down, far = lax.rem(me + 2, RING), lax.rem(me + 6, RING), lax.rem(me + 4, RING)
    return up, down, far, me + 1 - 2 * lax.rem(me, 2)


def other(at):
    return at + 1 - 2 * lax.rem(at, 2)


def gather_kernel(
    slabs_ref, virt_ref, weight_ref, out_ref,
    vq, hs, acc, rp, qp, wrow, wcol, wl,
    a_raw, a_land, a_keep, a_own, a_sib, a_last,
    b_terms, b_raw, b_land, b_keep, b_own, b_give, b_take, red, tile_land, parts,
    send_sems, recv_sems, tile_sems,
):
    d, r, c = lax.axis_index("depth"), lax.axis_index("row"), lax.axis_index("col")
    d_up, d_down, d_far, d_sib = around(d)
    c_up, c_down, c_far, c_sib = around(c)
    r_up, r_down = lax.rem(r + 1, RING), lax.rem(r + 7, RING)
    links = Links({"depth": d, "row": r, "col": c}, send_sems, recv_sems)
    send = links.send

    barrier = pltpu.get_barrier_semaphore()
    c_far_sib, c_up_sib, c_down_sib = other(c_far), other(c_up), other(c_down)
    partners = [links.place(depth=to) for to in (d_up, d_down, d_sib)]
    partners += [links.place(row=to) for to in (r_up, r_down)]
    partners += [links.place(col=to) for to in (c_up, c_down, c_far, c_sib, c_up_sib, c_down_sib, c_far_sib)]
    for partner in partners:
        pl.semaphore_signal(barrier, inc=1, device_id=partner, device_id_type=MESH)
    apart = lax.rem(c - r + RING, RING)
    turned = jnp.logical_or(jnp.logical_or(apart == 3, apart == 6), apart == 7)

    @pl.when(turned)
    def _():
        for n in range(RING):
            pl.semaphore_signal(barrier, inc=1, device_id=links.place(row=c, col=n), device_id_type=MESH)

    nvir, nbas = virt_ref.shape
    vq[c, 3] = jnp.zeros((nvir, LANES), BF)
    for quarter in range(3):
        vq[c, quarter] = virt_ref[:, LANES * quarter : LANES * quarter + LANES]
    vq[c, 3, :, 0 : nbas - 384] = virt_ref[:, 384:nbas]
    for orbital in range(2):
        hs[d, orbital, 496:512, :] = jnp.zeros((16, LANES), BF)
        hs[d, orbital, 0:nbas, :] = slabs_ref[orbital]

    pl.semaphore_wait(barrier, len(partners) + 3)

    j = lax.rem(r, 4)
    j_up, j_down = lax.rem(j + 1, 4), lax.rem(j + 3, 4)
    spans = (pl.ds(0, 208), pl.ds(208, 224))

    def slab(n, orbital, half=None, **target):
        piece = hs.at[n, orbital] if half is None else hs.at[n, orbital, pl.ds(256 * half, 256)]
        return send(piece, piece, **target)

    def virt(n, quarter, half=None, **target):
        piece = vq.at[n, quarter] if half is None else vq.at[n, quarter, spans[half]]
        return send(piece, piece, **target)

    def virt_rows(n):
        return virt(n, j, row=r_up), virt(n, j, row=r_down)

    pair, up, down, up2, down2, up3, down3 = ({} for _ in range(7))

    def slabs_out(o):
        up[o], down[o] = slab(d, o, depth=d_up), slab(d, o, depth=d_down)

    def slabs_sib(o):
        pair[o].wait_recv()
        up2[o], down2[o] = slab(d_sib, o, depth=d_up), slab(d_sib, o, depth=d_down)

    def slabs_sib_on(o):
        up[o].wait_recv()
        up2[o].wait_recv()
        piece = hs.at[pl.ds(2 * (d_down // 2), 2), o, pl.ds(256, 256)]
        up3[o] = send(piece, piece, depth=d_up)
        down[o].wait_recv()
        down2[o].wait_recv()
        piece = hs.at[pl.ds(2 * (d_up // 2), 2), o, pl.ds(0, 256)]
        down3[o] = send(piece, piece, depth=d_down)

    def slabs_end(o):
        for copy in (up3[o], down3[o]):
            copy.wait_recv()

    z_up = virt(c, j, col=c_up)
    z_down = virt(c, j, col=c_down)
    slabs_out(0)
    pair[0] = slab(d, 0, depth=d_sib)
    share_virt = send(vq.at[c], vq.at[c], col=c_sib)
    slabs_out(1)

    z_up.wait_recv()
    z_up2 = virt(c_down, j, 1, col=c_up)
    rows_a = virt_rows(c_down)
    z_down.wait_recv()
    z_down2 = virt(c_up, j, 0, col=c_down)
    rows_b = virt_rows(c_up)
    slabs_sib(0)
    z_up2.wait_recv()
    z_down2.wait_recv()
    rows_c = virt_rows(c_far)
    pair[1] = slab(d, 1, depth=d_sib)

    def pass_rows(n, rows):
        rows[0].wait_recv()
        if n is c_down:
            one = (virt(n, j_down, row=r_up),)
        elif n is c_far:
            one = (virt(n, j_down, 1, row=r_up),)
        else:
            one = ()
        rows[1].wait_recv()
        if n is c_up:
            one += (virt(n, j_up, row=r_down),)
        elif n is c_far:
            one += (virt(n, j_up, 0, row=r_down),)
        return one

    on_a = pass_rows(c_down, rows_a)
    on_b = pass_rows(c_up, rows_b)
    slabs_sib_on(0)
    on_c = pass_rows(c_far, rows_c)
    slabs_sib(1)

    wrow[...] = jnp.zeros_like(wrow)
    for orbital in range(2):
        wrow[:, 0:nvir] = jnp.broadcast_to(weight_ref[orbital : orbital + 1, :], (LANES, nvir))
        wcol[orbital] = wrow[...].T[0:nvir, :]
    acc[...] = jnp.zeros_like(acc)

    def virt_end(n, on):
        for copy in on:
            copy.wait_recv()
        return send(vq.at[n], vq.at[n], col=c_sib)

    def couple(n, orbital):
        left = jnp.concatenate([vq[n, 0], vq[n, 1], vq[n, 2], vq[n, 3]], axis=1)
        acc[orbital] += jnp.dot(left, hs[n, orbital], preferred_element_type=F32)

    share_a = virt_end(c_down, on_a)
    share_b = virt_end(c_up, on_b)
    slabs_end(0)
    couple(c, 0)
    share_virt.wait_recv()
    couple(c_sib, 0)
    couple(c_down, 0)
    couple(c_up, 0)
    share_c = virt_end(c_far, on_c)
    slabs_sib_on(1)
    share_a.wait_recv()
    couple(other(c_down), 0)
    share_b.wait_recv()
    couple(other(c_up), 0)
    couple(c_far, 0)
    share_c.wait_recv()
    couple(other(c_far), 0)

    def panel(n, orbital, **target):
        return send(rp.at[n, orbital], rp.at[n, orbital], **target)

    y_up, y_down, z_up, z_down = {}, {}, {}, {}
    share = {}

    def whole(n):
        return send(rp.at[n], rp.at[n], col=c_sib)

    def panels_out(o):
        rp[c, o] = acc[o].astype(BF)
        y_up[1, o] = send(rp.at[c, o], qp.at[1, o], row=r_up)
        y_down[1, o] = send(rp.at[c, o], qp.at[2, o], row=r_down)
        z_up[o] = panel(c, o, col=c_up)
        z_down[o] = panel(c, o, col=c_down)
        qp[0, o] = rp[c, o]

    def y_step(step, o):
        slot = 2 * step - 1
        y_up[step, o].wait_recv()
        y_up[step + 1, o] = send(qp.at[slot, o], qp.at[slot + 2, o], row=r_up)
        y_down[step, o].wait_recv()
        if step == 2 and o == 1:
            return
        y_down[step + 1, o] = send(qp.at[slot + 1, o], qp.at[slot + 3, o], row=r_down)

    def weigh(n, o):
        product = wcol[o] * rp[n, o].astype(F32)
        wl[o, n] = product.astype(BF).T

    panels_out(0)
    slabs_end(1)

    @pl.loop(0, RING)
    def _(n):
        couple(n, 1)

    panels_out(1)
    first_stage = len(links.copies)
    y_step(1, 1)
    z_down[0].wait_recv()
    z_down["far"] = panel(c_up, 0, col=c_down)
    share["own"] = whole(c)
    y_step(1, 0)
    z_up[1].wait_recv()
    z_up["far"] = panel(c_down, 1, col=c_up)
    z_up[0].wait_recv()
    weigh(c, 1)
    z_down[1].wait_recv()
    weigh(c_up, 0)
    weigh(c_down, 0)
    links.retire(24)
    links.retire(40)
    share["down"] = whole(c_down)
    share["own"].wait_recv()
    weigh(c_sib, 0)
    weigh(c, 0)
    y_step(2, 1)
    y_step(2, 0)
    weigh(c_sib, 1)
    z_down["far"].wait_recv()
    weigh(c_down, 1)
    share["down"].wait_recv()
    share["up"] = whole(c_up)
    weigh(c_down_sib, 1)
    weigh(c_far, 0)
    z_up["far"].wait_recv()
    share["far"] = whole(c_far)
    weigh(c_down_sib, 0)
    weigh(c_far, 1)
    weigh(c_up, 1)
    y_up[3, 1].wait_recv()
    y_up[4, 1] = send(qp.at[5, 1], qp.at[7, 1], row=r_up)
    y_down[3, 0].wait_recv()
    y_down[4, 0] = send(qp.at[6, 0], qp.at[7, 0], row=r_down)
    share["up"].wait_recv()
    weigh(c_up_sib, 0)
    share["far"].wait_recv()
    weigh(c_far_sib, 0)
    weigh(c_up_sib, 1)
    weigh(c_far_sib, 1)

    low, high = slice(0, 64), slice(64, 128)
    targets = {"far": d_far, "up": d_up, "down": d_down, "own": d}

    def terms_of(name, slots):
        terms = 0.0
        for o in range(2):
            rows = wl[o, pl.ds(2 * (targets[name] // 2), 2)].reshape(256, 432)
            columns = jnp.concatenate([qp[slot, o] for slot in slots], axis=1)
            terms += jnp.dot(rows, columns, preferred_element_type=F32)
        return terms.reshape(2, 128, LANES * len(slots))

    class RingSum:
        def __init__(self, raw, land, keep, own):
            self.raw, self.land, self.keep, self.own, self.copies = raw, land, keep, own, {}

        def send(self, at, value, **target):
            self.raw[at] = value.astype(BF)
            self.copies[at] = send(self.raw.at[at], self.land.at[at], **target)

        def give(self, name, block):
            if name == "far":
                self.send(0, block[:, high], depth=d_up)
                self.send(1, block[:, low], depth=d_down)
            elif name == "up":
                self.send(2, block[:, low], depth=d_up)
                self.keep[0] = block[:, high]
            elif name == "down":
                self.send(3, block[:, high], depth=d_down)
                self.keep[1] = block[:, low]
            else:
                self.own[...] = block

        def pass_on(self, at):
            self.copies[at].wait_recv()
            self.send(at + 4, self.keep[at] + self.land[at].astype(F32), depth=(d_up, d_down)[at])

        def end(self):
            for at in (2, 3, 4, 5):
                self.copies[at].wait_recv()
            land = self.land
            self.own[:, low] = self.own[:, low] + land[2].astype(F32) + land[5].astype(F32)
            self.own[:, high] = self.own[:, high] + land[3].astype(F32) + land[4].astype(F32)

    plane = lax.rem(d, 2)
    slots_a, slots_b = (5, 7), (0, 2, 4)
    ring_a = RingSum(a_raw, a_land, a_keep, a_own)
    ring_b = RingSum(b_raw, b_land, b_keep, b_own)
    b_pair = {}
    def gram_b(at, name):
        b_terms[at] = terms_of(name, slots_b)
        b_give[at] = b_terms[at, 1 - plane].astype(BF)
        b_pair[name] = send(b_give.at[at], b_take.at[at], depth=d_sib)

    def pair_b(at, name):
        b_pair[name].wait_recv()
        ring_b.give(name, (b_terms[at, plane] + b_take[at].astype(F32))[None])

    rows_of = {0: r, 2: r_up, 4: lax.rem(r + 2, RING), 5: lax.rem(r + 5, RING), 7: lax.rem(r + 4, RING)}
    mine = tile_sems.at[c]

    def tiles_out(slots, total):
        for at, slot in enumerate(slots):
            red[slot] = total[:, LANES * at : LANES * at + LANES]
        for slot in slots:
            to = rows_of[slot]
            if slot in (2, 4, 5):
                links.plan(red.at[slot], tile_land.at[c], recv_sem=mine, row=to, col=r).start()
        for slot in slots:
            to = rows_of[slot]
            copy = links.plan(red.at[slot], tile_land.at[c], recv_sem=mine, col=to)
            straight[slot] = to, copy
            pl.when(to != c)(copy.start)

    straight = {}

    gram_b(0, "far")
    gram_b(1, "up")
    gram_b(2, "down")
    y_up[3, 0].wait_recv()
    y_up[4, 1].wait_recv()
    y_down[4, 0].wait_recv()
    ring_a.give("far", terms_of("far", slots_a))
    ring_a.give("down", terms_of("down", slots_a))
    pair_b(0, "far")
    ring_a.give("up", terms_of("up", slots_a))
    gram_b(3, "own")
    ring_a.pass_on(1)
    ring_a.pass_on(0)
    pair_b(1, "up")
    pair_b(2, "down")
    ring_a.give("own", terms_of("own", slots_a))
    links.retire(first_stage)
    ring_b.pass_on(0)
    ring_b.pass_on(1)
    ring_a.end()
    a_sib[...] = a_own[1 - plane].astype(BF)
    last = send(a_sib, a_last, depth=d_sib)
    pair_b(3, "own")
    ring_b.end()
    tiles_out(slots_b, b_own[0].astype(BF))
    last.wait_recv()
    tiles_out(slots_a, (a_own[plane] + a_last[...].astype(F32)).astype(BF))

    before = len(links.copies) - 8
    links.retire(before)
    for slot, (to, _) in straight.items():

        @pl.when(to == c)
        def _(slot=slot):
            tile_land[c] = red[slot]

    def columns_of(place):
        pair_at = lax.rem(c // 2 + place, 4)
        return [(2 * place + core, 2 * pair_at + core) for core in range(2)]

    def tiles_in(places):
        for place in places:
            for at, n in columns_of(place):

                @pl.when(jnp.logical_or(turned, c != n))
                def _(n=n):
                    pltpu.make_async_remote_copy(
                        src_ref=red.at[0],
                        dst_ref=tile_land.at[n],
                        send_sem=send_sems.at[before],
                        recv_sem=tile_sems.at[n],
                        device_id=links.place(col=c_sib),
                        device_id_type=MESH,
                    ).wait_recv()

                @pl.when(turned)
                def _(at=at, n=n):
                    parts[d, at] = tile_land[n].T

                @pl.when(jnp.logical_not(turned))
                def _(at=at, n=n):
                    parts[d, at] = tile_land[n]

    def pass_on(n, begin, size, **target):
        piece = parts.at[n, pl.ds(begin, size)]
        return send(piece, piece, **target)

    def settle(n):
        targets_of = [pair for place in range(4) for pair in columns_of(place)]

        @pl.when(turned)
        def _():
            for at, m in targets_of:
                out_ref[m, :, pl.ds(pl.multiple_of(LANES * n, LANES), LANES)] = parts[n, at]

        @pl.when(jnp.logical_not(turned))
        def _():
            for at, m in targets_of:
                out_ref[n, :, pl.ds(pl.multiple_of(LANES * m, LANES), LANES)] = parts[n, at]

    first_gather = len(links.copies)
    tiles_in((0, 1))
    pair = pass_on(d, 0, 4, depth=d_sib)
    a_up = pass_on(d, 0, 4, depth=d_up)
    a_down = pass_on(d, 0, 4, depth=d_down)
    tiles_in((3, 2))
    b_up = pass_on(d, 4, 4, depth=d_up)
    b_down = pass_on(d, 4, 4, depth=d_down)
    b_pairs = [pass_on(d, 4, 4, depth=d_sib)]
    for slot, (to, copy) in straight.items():
        pl.when(to != c)(copy.wait_send)
    for at in range(before, first_gather):
        if all(links.copies[at] is not copy for _, copy in straight.values()):
            links.copies[at].wait_send()
    links.retired = first_gather
    settle(d)
    pair.wait_recv()
    a_up2 = pass_on(d_sib, 0, 4, depth=d_up)
    a_down2 = pass_on(d_sib, 0, 4, depth=d_down)
    b_up.wait_recv()
    b_up2 = pass_on(d_down, 6, 2, depth=d_up)
    b_pairs.append(pass_on(d_down, 4, 4, depth=d_sib))
    b_down.wait_recv()
    b_down2 = pass_on(d_up, 4, 2, depth=d_down)
    b_pairs.append(pass_on(d_up, 4, 4, depth=d_sib))
    a_up.wait_recv()
    a_up3 = pass_on(d_down, 2, 2, depth=d_up)
    a_down.wait_recv()
    a_down3 = pass_on(d_up, 0, 2, depth=d_down)
    settle(d_up)
    settle(d_down)
    b_up2.wait_recv()
    b_pairs.append(pass_on(d_far, 6, 2, depth=d_sib))
    b_down2.wait_recv()
    b_pairs.append(pass_on(d_far, 4, 2, depth=d_sib))
    a_up2.wait_recv()
    a_up4 = pass_on(other(d_down), 2, 2, depth=d_up)
    a_down2.wait_recv()
    a_down4 = pass_on(other(d_up), 0, 2, depth=d_down)
    links.retire(len(links.copies) - 6)
    b_pairs[0].wait_recv()
    settle(d_sib)
    a_up3.wait_recv()
    a_down3.wait_recv()
    settle(d_far)
    b_pairs[1].wait_recv()
    settle(other(d_down))
    b_pairs[2].wait_recv()
    settle(other(d_up))
    for copy in (a_up4, a_down4, *b_pairs[3:]):
        copy.wait_recv()
    settle(other(d_far))
    links.retire()


def on_device(half_slabs, virtuals, occupied_energy, virtual_energy, frequency):
    vmem = pl.BlockSpec(memory_space=pltpu.VMEM)
    excitation = virtual_energy[None, :] - occupied_energy[:, None]
    weight = 4.0 * excitation / (excitation * excitation + frequency[0] * frequency[0])
    copies = 128
    gram = pl.pallas_call(
        gather_kernel,
        out_shape=jax.ShapeDtypeStruct((RING, 128, 1024), BF),
        in_specs=[vmem] * 3,
        out_specs=vmem,
        scratch_shapes=[
            pltpu.VMEM((RING, 4, 432, LANES), BF),
            pltpu.VMEM((RING, 2, 512, LANES), BF),
            pltpu.VMEM((2, 432, LANES), F32),
            pltpu.VMEM((RING, 2, 432, LANES), BF),
            pltpu.VMEM((RING, 2, 432, LANES), BF),
            pltpu.VMEM((LANES, 512), F32),
            pltpu.VMEM((2, 432, LANES), F32),
            pltpu.VMEM((2, RING, 128, 432), BF),
            pltpu.VMEM((6, 2, 64, 256), BF),
            pltpu.VMEM((6, 2, 64, 256), BF),
            pltpu.VMEM((2, 2, 64, 256), F32),
            pltpu.VMEM((2, 128, 256), F32),
            pltpu.VMEM((128, 256), BF),
            pltpu.VMEM((128, 256), BF),
            pltpu.VMEM((4, 2, 128, 384), F32),
            pltpu.VMEM((6, 1, 64, 384), BF),
            pltpu.VMEM((6, 1, 64, 384), BF),
            pltpu.VMEM((2, 1, 64, 384), F32),
            pltpu.VMEM((1, 128, 384), F32),
            pltpu.VMEM((4, 128, 384), BF),
            pltpu.VMEM((4, 128, 384), BF),
            pltpu.VMEM((RING, 128, LANES), BF),
            pltpu.VMEM((RING, 128, LANES), BF),
            pltpu.VMEM((RING, RING, 128, LANES), BF),
            pltpu.SemaphoreType.DMA((copies,)),
            pltpu.SemaphoreType.DMA((copies,)),
            pltpu.SemaphoreType.DMA((RING,)),
        ],
        compiler_params=pltpu.CompilerParams(
            collective_id=0, has_side_effects=True, vmem_limit_bytes=48 * 2**20
        ),
        cost_estimate=pl.CostEstimate(flops=2_700_000_000, bytes_accessed=3_000_000, transcendentals=0),
    )(half_slabs, virtuals.T, weight)
    return gram.reshape(1024, 1024).astype(F32)


def solution(mesh):
    placed = (P(None, "depth", ("row", "col")), P("col", "depth"), P(), P("depth"), P())
    return jax.shard_map(
        on_device, mesh=mesh, in_specs=placed, out_specs=P("row", "col"), check_vma=False
    )
```

```python
import jax
import jax.numpy as jnp
from jax import lax
from jax.experimental import pallas as pl
from jax.experimental.pallas import tpu as pltpu
from jax.sharding import PartitionSpec as P

MESH = pl.DeviceIdType.MESH
BF = jnp.bfloat16
F32 = jnp.float32
RING = 8
LANES = 128


class Links:
    def __init__(self, here, send_sems, recv_sems):
        self.here, self.send_sems, self.recv_sems = here, send_sems, recv_sems
        self.copies, self.retired = [], 0

    def place(self, **target):
        at = {**self.here, **target}
        return at["depth"], at["row"], at["col"]

    def plan(self, src, dst, recv_sem=None, **target):
        at = len(self.copies)
        copy = pltpu.make_async_remote_copy(
            src_ref=src,
            dst_ref=dst,
            send_sem=self.send_sems.at[at],
            recv_sem=self.recv_sems.at[at] if recv_sem is None else recv_sem,
            device_id=self.place(**target),
            device_id_type=MESH,
        )
        self.copies.append(copy)
        return copy

    def send(self, src, dst, **target):
        copy = self.plan(src, dst, **target)
        copy.start()
        return copy

    def retire(self, upto=None):
        for copy in self.copies[self.retired : upto]:
            copy.wait_send()
        self.retired = len(self.copies) if upto is None else upto


def around(me):
    up, down, far = lax.rem(me + 2, RING), lax.rem(me + 6, RING), lax.rem(me + 4, RING)
    return up, down, far, me + 1 - 2 * lax.rem(me, 2)


def other(at):
    return at + 1 - 2 * lax.rem(at, 2)


def gather_kernel(
    slabs_ref, virt_ref, weight_ref, out_ref,
    vq, hs, acc, rp, qp, wrow, wcol, wl,
    a_raw, a_land, a_keep, a_own, a_sib, a_last,
    b_terms, b_raw, b_land, b_keep, b_own, b_give, b_take, red, tile_land, parts,
    send_sems, recv_sems, tile_sems,
):
    d, r, c = lax.axis_index("depth"), lax.axis_index("row"), lax.axis_index("col")
    d_up, d_down, d_far, d_sib = around(d)
    c_up, c_down, c_far, c_sib = around(c)
    r_up, r_down = lax.rem(r + 1, RING), lax.rem(r + 7, RING)
    links = Links({"depth": d, "row": r, "col": c}, send_sems, recv_sems)
    send = links.send

    barrier = pltpu.get_barrier_semaphore()
    c_far_sib, c_up_sib, c_down_sib = other(c_far), other(c_up), other(c_down)
    partners = [links.place(depth=to) for to in (d_up, d_down, d_sib)]
    partners += [links.place(row=to) for to in (r_up, r_down)]
    partners += [links.place(col=to) for to in (c_up, c_down, c_far, c_sib, c_up_sib, c_down_sib, c_far_sib)]
    for partner in partners:
        pl.semaphore_signal(barrier, inc=1, device_id=partner, device_id_type=MESH)
    apart = lax.rem(c - r + RING, RING)
    turned = jnp.logical_or(jnp.logical_or(apart == 3, apart == 6), apart == 7)

    @pl.when(turned)
    def _():
        for n in range(RING):
            pl.semaphore_signal(barrier, inc=1, device_id=links.place(row=c, col=n), device_id_type=MESH)

    nvir, nbas = virt_ref.shape
    vq[c, 3] = jnp.zeros((nvir, LANES), BF)
    for quarter in range(3):
        vq[c, quarter] = virt_ref[:, LANES * quarter : LANES * quarter + LANES]
    vq[c, 3, :, 0 : nbas - 384] = virt_ref[:, 384:nbas]
    for orbital in range(2):
        hs[d, orbital, 496:512, :] = jnp.zeros((16, LANES), BF)
        hs[d, orbital, 0:nbas, :] = slabs_ref[orbital]

    pl.semaphore_wait(barrier, len(partners) + 3)

    j = lax.rem(r, 4)
    j_up, j_down = lax.rem(j + 1, 4), lax.rem(j + 3, 4)
    spans = (pl.ds(0, 208), pl.ds(208, 224))

    def slab(n, orbital, half=None, **target):
        piece = hs.at[n, orbital] if half is None else hs.at[n, orbital, pl.ds(256 * half, 256)]
        return send(piece, piece, **target)

    def virt(n, quarter, half=None, **target):
        piece = vq.at[n, quarter] if half is None else vq.at[n, quarter, spans[half]]
        return send(piece, piece, **target)

    def virt_rows(n):
        return virt(n, j, row=r_up), virt(n, j, row=r_down)

    pair, up, down, up2, down2, up3, down3 = ({} for _ in range(7))

    def slabs_out(o):
        up[o], down[o] = slab(d, o, depth=d_up), slab(d, o, depth=d_down)

    def slabs_sib(o):
        pair[o].wait_recv()
        up2[o], down2[o] = slab(d_sib, o, depth=d_up), slab(d_sib, o, depth=d_down)

    def slabs_sib_on(o):
        up[o].wait_recv()
        up2[o].wait_recv()
        piece = hs.at[pl.ds(2 * (d_down // 2), 2), o, pl.ds(256, 256)]
        up3[o] = send(piece, piece, depth=d_up)
        down[o].wait_recv()
        down2[o].wait_recv()
        piece = hs.at[pl.ds(2 * (d_up // 2), 2), o, pl.ds(0, 256)]
        down3[o] = send(piece, piece, depth=d_down)

    def slabs_end(o):
        for copy in (up3[o], down3[o]):
            copy.wait_recv()

    z_up = virt(c, j, col=c_up)
    z_down = virt(c, j, col=c_down)
    slabs_out(0)
    pair[0] = slab(d, 0, depth=d_sib)
    share_virt = send(vq.at[c], vq.at[c], col=c_sib)
    slabs_out(1)

    z_up.wait_recv()
    z_up2 = virt(c_down, j, 1, col=c_up)
    rows_a = virt_rows(c_down)
    z_down.wait_recv()
    z_down2 = virt(c_up, j, 0, col=c_down)
    rows_b = virt_rows(c_up)
    slabs_sib(0)
    z_up2.wait_recv()
    z_down2.wait_recv()
    rows_c = virt_rows(c_far)
    pair[1] = slab(d, 1, depth=d_sib)

    def pass_rows(n, rows):
        rows[0].wait_recv()
        if n is c_down:
            one = (virt(n, j_down, row=r_up),)
        elif n is c_far:
            one = (virt(n, j_down, 1, row=r_up),)
        else:
            one = ()
        rows[1].wait_recv()
        if n is c_up:
            one += (virt(n, j_up, row=r_down),)
        elif n is c_far:
            one += (virt(n, j_up, 0, row=r_down),)
        return one

    on_a = pass_rows(c_down, rows_a)
    on_b = pass_rows(c_up, rows_b)
    slabs_sib_on(0)
    on_c = pass_rows(c_far, rows_c)
    slabs_sib(1)

    wrow[...] = jnp.zeros_like(wrow)
    for orbital in range(2):
        wrow[:, 0:nvir] = jnp.broadcast_to(weight_ref[orbital : orbital + 1, :], (LANES, nvir))
        wcol[orbital] = wrow[...].T[0:nvir, :]
    acc[...] = jnp.zeros_like(acc)

    def virt_end(n, on):
        for copy in on:
            copy.wait_recv()
        return send(vq.at[n], vq.at[n], col=c_sib)

    def couple(n, orbital):
        left = jnp.concatenate([vq[n, 0], vq[n, 1], vq[n, 2], vq[n, 3]], axis=1)
        acc[orbital] += jnp.dot(left, hs[n, orbital], preferred_element_type=F32)

    share_a = virt_end(c_down, on_a)
    share_b = virt_end(c_up, on_b)
    slabs_end(0)
    couple(c, 0)
    share_virt.wait_recv()
    couple(c_sib, 0)
    couple(c_down, 0)
    couple(c_up, 0)
    share_c = virt_end(c_far, on_c)
    slabs_sib_on(1)
    share_a.wait_recv()
    couple(other(c_down), 0)
    share_b.wait_recv()
    couple(other(c_up), 0)
    couple(c_far, 0)
    share_c.wait_recv()
    couple(other(c_far), 0)

    def panel(n, orbital, **target):
        return send(rp.at[n, orbital], rp.at[n, orbital], **target)

    y_up, y_down, z_up, z_down = {}, {}, {}, {}
    share = {}

    def whole(n):
        return send(rp.at[n], rp.at[n], col=c_sib)

    def panels_out(o):
        rp[c, o] = acc[o].astype(BF)
        y_up[1, o] = send(rp.at[c, o], qp.at[1, o], row=r_up)
        y_down[1, o] = send(rp.at[c, o], qp.at[2, o], row=r_down)
        z_up[o] = panel(c, o, col=c_up)
        z_down[o] = panel(c, o, col=c_down)
        qp[0, o] = rp[c, o]

    def y_step(step, o):
        slot = 2 * step - 1
        y_up[step, o].wait_recv()
        y_up[step + 1, o] = send(qp.at[slot, o], qp.at[slot + 2, o], row=r_up)
        y_down[step, o].wait_recv()
        if step == 2 and o == 1:
            return
        y_down[step + 1, o] = send(qp.at[slot + 1, o], qp.at[slot + 3, o], row=r_down)

    def weigh(n, o):
        product = wcol[o] * rp[n, o].astype(F32)
        wl[o, n] = product.astype(BF).T

    panels_out(0)
    slabs_end(1)

    @pl.loop(0, RING)
    def _(n):
        couple(n, 1)

    panels_out(1)
    first_stage = len(links.copies)
    y_step(1, 1)
    z_down[0].wait_recv()
    z_down["far"] = panel(c_up, 0, col=c_down)
    share["own"] = whole(c)
    y_step(1, 0)
    z_up[1].wait_recv()
    z_up["far"] = panel(c_down, 1, col=c_up)
    z_up[0].wait_recv()
    weigh(c, 1)
    z_down[1].wait_recv()
    weigh(c_up, 0)
    weigh(c_down, 0)
    links.retire(24)
    links.retire(40)
    share["down"] = whole(c_down)
    share["own"].wait_recv()
    weigh(c_sib, 0)
    weigh(c, 0)
    y_step(2, 1)
    y_step(2, 0)
    weigh(c_sib, 1)
    z_down["far"].wait_recv()
    weigh(c_down, 1)
    share["down"].wait_recv()
    share["up"] = whole(c_up)
    weigh(c_down_sib, 1)
    weigh(c_far, 0)
    z_up["far"].wait_recv()
    share["far"] = whole(c_far)
    weigh(c_down_sib, 0)
    weigh(c_far, 1)
    weigh(c_up, 1)
    y_up[3, 1].wait_recv()
    y_up[4, 1] = send(qp.at[5, 1], qp.at[7, 1], row=r_up)
    y_down[3, 0].wait_recv()
    y_down[4, 0] = send(qp.at[6, 0], qp.at[7, 0], row=r_down)
    share["up"].wait_recv()
    weigh(c_up_sib, 0)
    share["far"].wait_recv()
    weigh(c_far_sib, 0)
    weigh(c_up_sib, 1)
    weigh(c_far_sib, 1)

    low, high = slice(0, 64), slice(64, 128)
    targets = {"far": d_far, "up": d_up, "down": d_down, "own": d}

    def terms_of(name, slots):
        terms = 0.0
        for o in range(2):
            rows = wl[o, pl.ds(2 * (targets[name] // 2), 2)].reshape(256, 432)
            columns = jnp.concatenate([qp[slot, o] for slot in slots], axis=1)
            terms += jnp.dot(rows, columns, preferred_element_type=F32)
        return terms.reshape(2, 128, LANES * len(slots))

    class RingSum:
        def __init__(self, raw, land, keep, own):
            self.raw, self.land, self.keep, self.own, self.copies = raw, land, keep, own, {}

        def send(self, at, value, **target):
            self.raw[at] = value.astype(BF)
            self.copies[at] = send(self.raw.at[at], self.land.at[at], **target)

        def give(self, name, block):
            if name == "far":
                self.send(0, block[:, high], depth=d_up)
                self.send(1, block[:, low], depth=d_down)
            elif name == "up":
                self.send(2, block[:, low], depth=d_up)
                self.keep[0] = block[:, high]
            elif name == "down":
                self.send(3, block[:, high], depth=d_down)
                self.keep[1] = block[:, low]
            else:
                self.own[...] = block

        def pass_on(self, at):
            self.copies[at].wait_recv()
            self.send(at + 4, self.keep[at] + self.land[at].astype(F32), depth=(d_up, d_down)[at])

        def end(self):
            for at in (2, 3, 4, 5):
                self.copies[at].wait_recv()
            land = self.land
            self.own[:, low] = self.own[:, low] + land[2].astype(F32) + land[5].astype(F32)
            self.own[:, high] = self.own[:, high] + land[3].astype(F32) + land[4].astype(F32)

    plane = lax.rem(d, 2)
    slots_a, slots_b = (4, 7), (0, 2, 5)
    ring_a = RingSum(a_raw, a_land, a_keep, a_own)
    ring_b = RingSum(b_raw, b_land, b_keep, b_own)
    b_pair = {}
    def gram_b(at, name):
        b_terms[at] = terms_of(name, slots_b)
        b_give[at] = b_terms[at, 1 - plane].astype(BF)
        b_pair[name] = send(b_give.at[at], b_take.at[at], depth=d_sib)

    def pair_b(at, name):
        b_pair[name].wait_recv()
        ring_b.give(name, (b_terms[at, plane] + b_take[at].astype(F32))[None])

    rows_of = {0: r, 2: r_up, 4: lax.rem(r + 2, RING), 5: lax.rem(r + 5, RING), 7: lax.rem(r + 4, RING)}
    mine = tile_sems.at[c]

    def tiles_out(slots, total):
        for at, slot in enumerate(slots):
            red[slot] = total[:, LANES * at : LANES * at + LANES]
        for slot in slots:
            to = rows_of[slot]
            if slot in (2, 4, 5):
                links.plan(red.at[slot], tile_land.at[c], recv_sem=mine, row=to, col=r).start()
        for slot in slots:
            to = rows_of[slot]
            copy = links.plan(red.at[slot], tile_land.at[c], recv_sem=mine, col=to)
            straight[slot] = to, copy
            pl.when(to != c)(copy.start)

    straight = {}

    y_up[3, 0].wait_recv()
    gram_b(0, "far")
    gram_b(1, "up")
    gram_b(2, "down")
    y_up[4, 1].wait_recv()
    y_down[4, 0].wait_recv()
    ring_a.give("far", terms_of("far", slots_a))
    ring_a.give("down", terms_of("down", slots_a))
    pair_b(0, "far")
    ring_a.give("up", terms_of("up", slots_a))
    gram_b(3, "own")
    ring_a.pass_on(1)
    ring_a.pass_on(0)
    pair_b(1, "up")
    pair_b(2, "down")
    ring_a.give("own", terms_of("own", slots_a))
    links.retire(first_stage)
    ring_b.pass_on(0)
    ring_b.pass_on(1)
    ring_a.end()
    a_sib[...] = a_own[1 - plane].astype(BF)
    last = send(a_sib, a_last, depth=d_sib)
    pair_b(3, "own")
    ring_b.end()
    tiles_out(slots_b, b_own[0].astype(BF))
    last.wait_recv()
    tiles_out(slots_a, (a_own[plane] + a_last[...].astype(F32)).astype(BF))

    before = len(links.copies) - 8
    links.retire(before)
    for slot, (to, _) in straight.items():

        @pl.when(to == c)
        def _(slot=slot):
            tile_land[c] = red[slot]

    def columns_of(place):
        pair_at = lax.rem(c // 2 + place, 4)
        return [(2 * place + core, 2 * pair_at + core) for core in range(2)]

    def tiles_in(places):
        for place in places:
            for at, n in columns_of(place):

                @pl.when(jnp.logical_or(turned, c != n))
                def _(n=n):
                    pltpu.make_async_remote_copy(
                        src_ref=red.at[0],
                        dst_ref=tile_land.at[n],
                        send_sem=send_sems.at[before],
                        recv_sem=tile_sems.at[n],
                        device_id=links.place(col=c_sib),
                        device_id_type=MESH,
                    ).wait_recv()

                @pl.when(turned)
                def _(at=at, n=n):
                    parts[d, at] = tile_land[n].T

                @pl.when(jnp.logical_not(turned))
                def _(at=at, n=n):
                    parts[d, at] = tile_land[n]

    def pass_on(n, begin, size, **target):
        piece = parts.at[n, pl.ds(begin, size)]
        return send(piece, piece, **target)

    def settle(n):
        targets_of = [pair for place in range(4) for pair in columns_of(place)]

        @pl.when(turned)
        def _():
            for at, m in targets_of:
                out_ref[m, :, pl.ds(pl.multiple_of(LANES * n, LANES), LANES)] = parts[n, at]

        @pl.when(jnp.logical_not(turned))
        def _():
            for at, m in targets_of:
                out_ref[n, :, pl.ds(pl.multiple_of(LANES * m, LANES), LANES)] = parts[n, at]

    first_gather = len(links.copies)
    tiles_in((0, 1))
    pair = pass_on(d, 0, 4, depth=d_sib)
    a_up = pass_on(d, 0, 4, depth=d_up)
    a_down = pass_on(d, 0, 4, depth=d_down)
    tiles_in((3, 2))
    b_up = pass_on(d, 4, 4, depth=d_up)
    b_down = pass_on(d, 4, 4, depth=d_down)
    b_pairs = [pass_on(d, 4, 4, depth=d_sib)]
    for slot, (to, copy) in straight.items():
        pl.when(to != c)(copy.wait_send)
    for at in range(before, first_gather):
        if all(links.copies[at] is not copy for _, copy in straight.values()):
            links.copies[at].wait_send()
    links.retired = first_gather
    settle(d)
    pair.wait_recv()
    a_up2 = pass_on(d_sib, 0, 4, depth=d_up)
    a_down2 = pass_on(d_sib, 0, 4, depth=d_down)
    b_up.wait_recv()
    b_up2 = pass_on(d_down, 6, 2, depth=d_up)
    b_pairs.append(pass_on(d_down, 4, 4, depth=d_sib))
    b_down.wait_recv()
    b_down2 = pass_on(d_up, 4, 2, depth=d_down)
    b_pairs.append(pass_on(d_up, 4, 4, depth=d_sib))
    a_up.wait_recv()
    a_up3 = pass_on(d_down, 2, 2, depth=d_up)
    a_down.wait_recv()
    a_down3 = pass_on(d_up, 0, 2, depth=d_down)
    settle(d_up)
    settle(d_down)
    b_up2.wait_recv()
    b_pairs.append(pass_on(d_far, 6, 2, depth=d_sib))
    b_down2.wait_recv()
    b_pairs.append(pass_on(d_far, 4, 2, depth=d_sib))
    a_up2.wait_recv()
    a_up4 = pass_on(other(d_down), 2, 2, depth=d_up)
    a_down2.wait_recv()
    a_down4 = pass_on(other(d_up), 0, 2, depth=d_down)
    links.retire(len(links.copies) - 6)
    b_pairs[0].wait_recv()
    settle(d_sib)
    a_up3.wait_recv()
    a_down3.wait_recv()
    settle(d_far)
    b_pairs[1].wait_recv()
    settle(other(d_down))
    b_pairs[2].wait_recv()
    settle(other(d_up))
    for copy in (a_up4, a_down4, *b_pairs[3:]):
        copy.wait_recv()
    settle(other(d_far))
    links.retire()


def on_device(half_slabs, virtuals, occupied_energy, virtual_energy, frequency):
    vmem = pl.BlockSpec(memory_space=pltpu.VMEM)
    excitation = virtual_energy[None, :] - occupied_energy[:, None]
    weight = 4.0 * excitation / (excitation * excitation + frequency[0] * frequency[0])
    copies = 128
    gram = pl.pallas_call(
        gather_kernel,
        out_shape=jax.ShapeDtypeStruct((RING, 128, 1024), BF),
        in_specs=[vmem] * 3,
        out_specs=vmem,
        scratch_shapes=[
            pltpu.VMEM((RING, 4, 432, LANES), BF),
            pltpu.VMEM((RING, 2, 512, LANES), BF),
            pltpu.VMEM((2, 432, LANES), F32),
            pltpu.VMEM((RING, 2, 432, LANES), BF),
            pltpu.VMEM((RING, 2, 432, LANES), BF),
            pltpu.VMEM((LANES, 512), F32),
            pltpu.VMEM((2, 432, LANES), F32),
            pltpu.VMEM((2, RING, 128, 432), BF),
            pltpu.VMEM((6, 2, 64, 256), BF),
            pltpu.VMEM((6, 2, 64, 256), BF),
            pltpu.VMEM((2, 2, 64, 256), F32),
            pltpu.VMEM((2, 128, 256), F32),
            pltpu.VMEM((128, 256), BF),
            pltpu.VMEM((128, 256), BF),
            pltpu.VMEM((4, 2, 128, 384), F32),
            pltpu.VMEM((6, 1, 64, 384), BF),
            pltpu.VMEM((6, 1, 64, 384), BF),
            pltpu.VMEM((2, 1, 64, 384), F32),
            pltpu.VMEM((1, 128, 384), F32),
            pltpu.VMEM((4, 128, 384), BF),
            pltpu.VMEM((4, 128, 384), BF),
            pltpu.VMEM((RING, 128, LANES), BF),
            pltpu.VMEM((RING, 128, LANES), BF),
            pltpu.VMEM((RING, RING, 128, LANES), BF),
            pltpu.SemaphoreType.DMA((copies,)),
            pltpu.SemaphoreType.DMA((copies,)),
            pltpu.SemaphoreType.DMA((RING,)),
        ],
        compiler_params=pltpu.CompilerParams(
            collective_id=0, has_side_effects=True, vmem_limit_bytes=48 * 2**20
        ),
        cost_estimate=pl.CostEstimate(flops=2_700_000_000, bytes_accessed=3_000_000, transcendentals=0),
    )(half_slabs, virtuals.T, weight)
    return gram.reshape(1024, 1024).astype(F32)


def solution(mesh):
    placed = (P(None, "depth", ("row", "col")), P("col", "depth"), P(), P("depth"), P())
    return jax.shard_map(
        on_device, mesh=mesh, in_specs=placed, out_specs=P("row", "col"), check_vma=False
    )
```

```python
import jax
import jax.numpy as jnp
from jax import lax
from jax.experimental import pallas as pl
from jax.experimental.pallas import tpu as pltpu
from jax.sharding import PartitionSpec as P

MESH = pl.DeviceIdType.MESH
BF = jnp.bfloat16
F32 = jnp.float32
RING = 8
LANES = 128


class Links:
    def __init__(self, here, send_sems, recv_sems):
        self.here, self.send_sems, self.recv_sems = here, send_sems, recv_sems
        self.copies, self.retired = [], 0

    def place(self, **target):
        at = {**self.here, **target}
        return at["depth"], at["row"], at["col"]

    def plan(self, src, dst, recv_sem=None, **target):
        at = len(self.copies)
        copy = pltpu.make_async_remote_copy(
            src_ref=src,
            dst_ref=dst,
            send_sem=self.send_sems.at[at],
            recv_sem=self.recv_sems.at[at] if recv_sem is None else recv_sem,
            device_id=self.place(**target),
            device_id_type=MESH,
        )
        self.copies.append(copy)
        return copy

    def send(self, src, dst, **target):
        copy = self.plan(src, dst, **target)
        copy.start()
        return copy

    def retire(self, upto=None):
        for copy in self.copies[self.retired : upto]:
            copy.wait_send()
        self.retired = len(self.copies) if upto is None else upto


def around(me):
    up, down, far = lax.rem(me + 2, RING), lax.rem(me + 6, RING), lax.rem(me + 4, RING)
    return up, down, far, me + 1 - 2 * lax.rem(me, 2)


def other(at):
    return at + 1 - 2 * lax.rem(at, 2)


def gather_kernel(
    slabs_ref, virt_ref, weight_ref, out_ref,
    vq, hs, acc, rp, qp, wrow, wcol, wl,
    a_raw, a_land, a_keep, a_own, a_sib, a_last,
    b_terms, b_raw, b_land, b_keep, b_own, b_give, b_take, red, tile_land, parts,
    send_sems, recv_sems, tile_sems,
):
    d, r, c = lax.axis_index("depth"), lax.axis_index("row"), lax.axis_index("col")
    d_up, d_down, d_far, d_sib = around(d)
    c_up, c_down, c_far, c_sib = around(c)
    r_up, r_down = lax.rem(r + 1, RING), lax.rem(r + 7, RING)
    links = Links({"depth": d, "row": r, "col": c}, send_sems, recv_sems)
    send = links.send

    barrier = pltpu.get_barrier_semaphore()
    c_far_sib, c_up_sib, c_down_sib = other(c_far), other(c_up), other(c_down)
    partners = [links.place(depth=to) for to in (d_up, d_down, d_sib)]
    partners += [links.place(row=to) for to in (r_up, r_down)]
    partners += [links.place(col=to) for to in (c_up, c_down, c_far, c_sib, c_up_sib, c_down_sib, c_far_sib)]
    for partner in partners:
        pl.semaphore_signal(barrier, inc=1, device_id=partner, device_id_type=MESH)
    apart = lax.rem(c - r + RING, RING)
    turned = jnp.logical_or(jnp.logical_or(apart == 3, apart == 6), apart == 7)

    @pl.when(turned)
    def _():
        for n in range(RING):
            pl.semaphore_signal(barrier, inc=1, device_id=links.place(row=c, col=n), device_id_type=MESH)

    nvir, nbas = virt_ref.shape
    vq[c, 3] = jnp.zeros((nvir, LANES), BF)
    for quarter in range(3):
        vq[c, quarter] = virt_ref[:, LANES * quarter : LANES * quarter + LANES]
    vq[c, 3, :, 0 : nbas - 384] = virt_ref[:, 384:nbas]
    for orbital in range(2):
        hs[d, orbital, 496:512, :] = jnp.zeros((16, LANES), BF)
        hs[d, orbital, 0:nbas, :] = slabs_ref[orbital]

    pl.semaphore_wait(barrier, len(partners) + 3)

    j = lax.rem(r, 4)
    j_up, j_down = lax.rem(j + 1, 4), lax.rem(j + 3, 4)
    spans = (pl.ds(0, 208), pl.ds(208, 224))

    def slab(n, orbital, half=None, **target):
        piece = hs.at[n, orbital] if half is None else hs.at[n, orbital, pl.ds(256 * half, 256)]
        return send(piece, piece, **target)

    def virt(n, quarter, half=None, **target):
        piece = vq.at[n, quarter] if half is None else vq.at[n, quarter, spans[half]]
        return send(piece, piece, **target)

    def virt_rows(n):
        return virt(n, j, row=r_up), virt(n, j, row=r_down)

    pair, up, down, up2, down2, up3, down3 = ({} for _ in range(7))

    def slabs_out(o):
        up[o], down[o] = slab(d, o, depth=d_up), slab(d, o, depth=d_down)

    def slabs_sib(o):
        pair[o].wait_recv()
        up2[o], down2[o] = slab(d_sib, o, depth=d_up), slab(d_sib, o, depth=d_down)

    def slabs_sib_on(o):
        up[o].wait_recv()
        up2[o].wait_recv()
        piece = hs.at[pl.ds(2 * (d_down // 2), 2), o, pl.ds(256, 256)]
        up3[o] = send(piece, piece, depth=d_up)
        down[o].wait_recv()
        down2[o].wait_recv()
        piece = hs.at[pl.ds(2 * (d_up // 2), 2), o, pl.ds(0, 256)]
        down3[o] = send(piece, piece, depth=d_down)

    def slabs_end(o):
        for copy in (up3[o], down3[o]):
            copy.wait_recv()

    z_up = virt(c, j, col=c_up)
    z_down = virt(c, j, col=c_down)
    slabs_out(0)
    pair[0] = slab(d, 0, depth=d_sib)
    share_virt = send(vq.at[c], vq.at[c], col=c_sib)
    slabs_out(1)

    z_up.wait_recv()
    z_up2 = virt(c_down, j, 1, col=c_up)
    rows_a = virt_rows(c_down)
    z_down.wait_recv()
    z_down2 = virt(c_up, j, 0, col=c_down)
    rows_b = virt_rows(c_up)
    slabs_sib(0)
    z_up2.wait_recv()
    z_down2.wait_recv()
    rows_c = virt_rows(c_far)
    pair[1] = slab(d, 1, depth=d_sib)

    def pass_rows(n, rows):
        rows[0].wait_recv()
        if n is c_down:
            one = (virt(n, j_down, row=r_up),)
        elif n is c_far:
            one = (virt(n, j_down, 1, row=r_up),)
        else:
            one = ()
        rows[1].wait_recv()
        if n is c_up:
            one += (virt(n, j_up, row=r_down),)
        elif n is c_far:
            one += (virt(n, j_up, 0, row=r_down),)
        return one

    on_a = pass_rows(c_down, rows_a)
    on_b = pass_rows(c_up, rows_b)
    slabs_sib_on(0)
    on_c = pass_rows(c_far, rows_c)
    slabs_sib(1)

    wrow[...] = jnp.zeros_like(wrow)
    for orbital in range(2):
        wrow[:, 0:nvir] = jnp.broadcast_to(weight_ref[orbital : orbital + 1, :], (LANES, nvir))
        wcol[orbital] = wrow[...].T[0:nvir, :]
    acc[...] = jnp.zeros_like(acc)

    def virt_end(n, on):
        for copy in on:
            copy.wait_recv()
        return send(vq.at[n], vq.at[n], col=c_sib)

    def couple(n, orbital):
        left = jnp.concatenate([vq[n, 0], vq[n, 1], vq[n, 2], vq[n, 3]], axis=1)
        acc[orbital] += jnp.dot(left, hs[n, orbital], preferred_element_type=F32)

    share_a = virt_end(c_down, on_a)
    share_b = virt_end(c_up, on_b)
    slabs_end(0)
    couple(c, 0)
    share_virt.wait_recv()
    couple(c_sib, 0)
    couple(c_down, 0)
    couple(c_up, 0)
    share_c = virt_end(c_far, on_c)
    slabs_sib_on(1)
    share_a.wait_recv()
    couple(other(c_down), 0)
    share_b.wait_recv()
    couple(other(c_up), 0)
    couple(c_far, 0)
    share_c.wait_recv()
    couple(other(c_far), 0)

    def panel(n, orbital, **target):
        return send(rp.at[n, orbital], rp.at[n, orbital], **target)

    y_up, y_down, z_up, z_down = {}, {}, {}, {}
    share = {}

    def whole(n):
        return send(rp.at[n], rp.at[n], col=c_sib)

    def panels_out(o):
        rp[c, o] = acc[o].astype(BF)
        y_up[1, o] = send(rp.at[c, o], qp.at[1, o], row=r_up)
        y_down[1, o] = send(rp.at[c, o], qp.at[2, o], row=r_down)
        z_up[o] = panel(c, o, col=c_up)
        z_down[o] = panel(c, o, col=c_down)
        qp[0, o] = rp[c, o]

    def y_step(step, o):
        slot = 2 * step - 1
        y_up[step, o].wait_recv()
        y_up[step + 1, o] = send(qp.at[slot, o], qp.at[slot + 2, o], row=r_up)
        y_down[step, o].wait_recv()
        if step == 2 and o == 1:
            return
        y_down[step + 1, o] = send(qp.at[slot + 1, o], qp.at[slot + 3, o], row=r_down)

    def weigh(n, o):
        product = wcol[o] * rp[n, o].astype(F32)
        wl[o, n] = product.astype(BF).T

    panels_out(0)
    slabs_end(1)

    left = jnp.concatenate([vq[n, quarter] for n in range(RING) for quarter in range(4)], axis=1)
    right = jnp.concatenate([hs[n, 1] for n in range(RING)], axis=0)
    acc[1] = jnp.dot(left, right, preferred_element_type=F32)

    panels_out(1)
    first_stage = len(links.copies)
    y_step(1, 1)
    z_down[0].wait_recv()
    z_down["far"] = panel(c_up, 0, col=c_down)
    share["own"] = whole(c)
    y_step(1, 0)
    z_up[1].wait_recv()
    z_up["far"] = panel(c_down, 1, col=c_up)
    z_up[0].wait_recv()
    weigh(c, 1)
    z_down[1].wait_recv()
    weigh(c_up, 0)
    weigh(c_down, 0)
    links.retire(24)
    links.retire(40)
    share["down"] = whole(c_down)
    share["own"].wait_recv()
    weigh(c_sib, 0)
    weigh(c, 0)
    y_step(2, 1)
    y_step(2, 0)
    weigh(c_sib, 1)
    z_down["far"].wait_recv()
    weigh(c_down, 1)
    share["down"].wait_recv()
    share["up"] = whole(c_up)
    weigh(c_down_sib, 1)
    weigh(c_far, 0)
    z_up["far"].wait_recv()
    share["far"] = whole(c_far)
    weigh(c_down_sib, 0)
    weigh(c_far, 1)
    weigh(c_up, 1)
    y_up[3, 1].wait_recv()
    y_up[4, 1] = send(qp.at[5, 1], qp.at[7, 1], row=r_up)
    y_down[3, 0].wait_recv()
    y_down[4, 0] = send(qp.at[6, 0], qp.at[7, 0], row=r_down)
    share["up"].wait_recv()
    weigh(c_up_sib, 0)
    share["far"].wait_recv()
    weigh(c_far_sib, 0)
    weigh(c_up_sib, 1)
    weigh(c_far_sib, 1)

    low, high = slice(0, 64), slice(64, 128)
    targets = {"far": d_far, "up": d_up, "down": d_down, "own": d}

    def terms_of(name, slots):
        terms = 0.0
        for o in range(2):
            rows = wl[o, pl.ds(2 * (targets[name] // 2), 2)].reshape(256, 432)
            columns = jnp.concatenate([qp[slot, o] for slot in slots], axis=1)
            terms += jnp.dot(rows, columns, preferred_element_type=F32)
        return terms.reshape(2, 128, LANES * len(slots))

    class RingSum:
        def __init__(self, raw, land, keep, own):
            self.raw, self.land, self.keep, self.own, self.copies = raw, land, keep, own, {}

        def send(self, at, value, **target):
            self.raw[at] = value.astype(BF)
            self.copies[at] = send(self.raw.at[at], self.land.at[at], **target)

        def give(self, name, block):
            if name == "far":
                self.send(0, block[:, high], depth=d_up)
                self.send(1, block[:, low], depth=d_down)
            elif name == "up":
                self.send(2, block[:, low], depth=d_up)
                self.keep[0] = block[:, high]
            elif name == "down":
                self.send(3, block[:, high], depth=d_down)
                self.keep[1] = block[:, low]
            else:
                self.own[...] = block

        def pass_on(self, at):
            self.copies[at].wait_recv()
            self.send(at + 4, self.keep[at] + self.land[at].astype(F32), depth=(d_up, d_down)[at])

        def end(self):
            for at in (2, 3, 4, 5):
                self.copies[at].wait_recv()
            land = self.land
            self.own[:, low] = self.own[:, low] + land[2].astype(F32) + land[5].astype(F32)
            self.own[:, high] = self.own[:, high] + land[3].astype(F32) + land[4].astype(F32)

    plane = lax.rem(d, 2)
    slots_a, slots_b = (4, 7), (0, 2, 5)
    ring_a = RingSum(a_raw, a_land, a_keep, a_own)
    ring_b = RingSum(b_raw, b_land, b_keep, b_own)
    b_pair = {}
    def gram_b(at, name):
        b_terms[at] = terms_of(name, slots_b)
        b_give[at] = b_terms[at, 1 - plane].astype(BF)
        b_pair[name] = send(b_give.at[at], b_take.at[at], depth=d_sib)

    def pair_b(at, name):
        b_pair[name].wait_recv()
        ring_b.give(name, (b_terms[at, plane] + b_take[at].astype(F32))[None])

    rows_of = {0: r, 2: r_up, 4: lax.rem(r + 2, RING), 5: lax.rem(r + 5, RING), 7: lax.rem(r + 4, RING)}
    mine = tile_sems.at[c]

    def tiles_out(slots, total):
        for at, slot in enumerate(slots):
            red[slot] = total[:, LANES * at : LANES * at + LANES]
        for slot in slots:
            to = rows_of[slot]
            if slot in (2, 4, 5):
                links.plan(red.at[slot], tile_land.at[c], recv_sem=mine, row=to, col=r).start()
        for slot in slots:
            to = rows_of[slot]
            copy = links.plan(red.at[slot], tile_land.at[c], recv_sem=mine, col=to)
            straight[slot] = to, copy
            pl.when(to != c)(copy.start)

    straight = {}

    y_up[3, 0].wait_recv()
    gram_b(0, "far")
    gram_b(1, "up")
    gram_b(2, "down")
    y_up[4, 1].wait_recv()
    y_down[4, 0].wait_recv()
    ring_a.give("far", terms_of("far", slots_a))
    ring_a.give("down", terms_of("down", slots_a))
    pair_b(0, "far")
    ring_a.give("up", terms_of("up", slots_a))
    gram_b(3, "own")
    ring_a.pass_on(1)
    ring_a.pass_on(0)
    pair_b(1, "up")
    pair_b(2, "down")
    ring_a.give("own", terms_of("own", slots_a))
    links.retire(first_stage)
    ring_b.pass_on(0)
    ring_b.pass_on(1)
    ring_a.end()
    a_sib[...] = a_own[1 - plane].astype(BF)
    last = send(a_sib, a_last, depth=d_sib)
    pair_b(3, "own")
    ring_b.end()
    tiles_out(slots_b, b_own[0].astype(BF))
    last.wait_recv()
    tiles_out(slots_a, (a_own[plane] + a_last[...].astype(F32)).astype(BF))

    before = len(links.copies) - 8
    links.retire(before)
    for slot, (to, _) in straight.items():

        @pl.when(to == c)
        def _(slot=slot):
            tile_land[c] = red[slot]

    def columns_of(place):
        pair_at = lax.rem(c // 2 + place, 4)
        return [(2 * place + core, 2 * pair_at + core) for core in range(2)]

    def tiles_in(places):
        for place in places:
            for at, n in columns_of(place):

                @pl.when(jnp.logical_or(turned, c != n))
                def _(n=n):
                    pltpu.make_async_remote_copy(
                        src_ref=red.at[0],
                        dst_ref=tile_land.at[n],
                        send_sem=send_sems.at[before],
                        recv_sem=tile_sems.at[n],
                        device_id=links.place(col=c_sib),
                        device_id_type=MESH,
                    ).wait_recv()

                @pl.when(turned)
                def _(at=at, n=n):
                    parts[d, at] = tile_land[n].T

                @pl.when(jnp.logical_not(turned))
                def _(at=at, n=n):
                    parts[d, at] = tile_land[n]

    def pass_on(n, begin, size, **target):
        piece = parts.at[n, pl.ds(begin, size)]
        return send(piece, piece, **target)

    def settle(n):
        targets_of = [pair for place in range(4) for pair in columns_of(place)]

        @pl.when(turned)
        def _():
            for at, m in targets_of:
                out_ref[m, :, pl.ds(pl.multiple_of(LANES * n, LANES), LANES)] = parts[n, at]

        @pl.when(jnp.logical_not(turned))
        def _():
            for at, m in targets_of:
                out_ref[n, :, pl.ds(pl.multiple_of(LANES * m, LANES), LANES)] = parts[n, at]

    first_gather = len(links.copies)
    tiles_in((0, 1))
    pair = pass_on(d, 0, 4, depth=d_sib)
    a_up = pass_on(d, 0, 4, depth=d_up)
    a_down = pass_on(d, 0, 4, depth=d_down)
    tiles_in((3, 2))
    b_up = pass_on(d, 4, 4, depth=d_up)
    b_down = pass_on(d, 4, 4, depth=d_down)
    b_pairs = [pass_on(d, 4, 4, depth=d_sib)]
    for slot, (to, copy) in straight.items():
        pl.when(to != c)(copy.wait_send)
    for at in range(before, first_gather):
        if all(links.copies[at] is not copy for _, copy in straight.values()):
            links.copies[at].wait_send()
    links.retired = first_gather
    settle(d)
    pair.wait_recv()
    a_up2 = pass_on(d_sib, 0, 4, depth=d_up)
    a_down2 = pass_on(d_sib, 0, 4, depth=d_down)
    b_up.wait_recv()
    b_up2 = pass_on(d_down, 6, 2, depth=d_up)
    b_pairs.append(pass_on(d_down, 4, 4, depth=d_sib))
    b_down.wait_recv()
    b_down2 = pass_on(d_up, 4, 2, depth=d_down)
    b_pairs.append(pass_on(d_up, 4, 4, depth=d_sib))
    a_up.wait_recv()
    a_up3 = pass_on(d_down, 2, 2, depth=d_up)
    a_down.wait_recv()
    a_down3 = pass_on(d_up, 0, 2, depth=d_down)
    settle(d_up)
    settle(d_down)
    b_up2.wait_recv()
    b_pairs.append(pass_on(d_far, 6, 2, depth=d_sib))
    b_down2.wait_recv()
    b_pairs.append(pass_on(d_far, 4, 2, depth=d_sib))
    a_up2.wait_recv()
    a_up4 = pass_on(other(d_down), 2, 2, depth=d_up)
    a_down2.wait_recv()
    a_down4 = pass_on(other(d_up), 0, 2, depth=d_down)
    links.retire(len(links.copies) - 6)
    b_pairs[0].wait_recv()
    settle(d_sib)
    a_up3.wait_recv()
    a_down3.wait_recv()
    settle(d_far)
    b_pairs[1].wait_recv()
    settle(other(d_down))
    b_pairs[2].wait_recv()
    settle(other(d_up))
    for copy in (a_up4, a_down4, *b_pairs[3:]):
        copy.wait_recv()
    settle(other(d_far))
    links.retire()


def on_device(half_slabs, virtuals, occupied_energy, virtual_energy, frequency):
    vmem = pl.BlockSpec(memory_space=pltpu.VMEM)
    excitation = virtual_energy[None, :] - occupied_energy[:, None]
    weight = 4.0 * excitation / (excitation * excitation + frequency[0] * frequency[0])
    copies = 128
    gram = pl.pallas_call(
        gather_kernel,
        out_shape=jax.ShapeDtypeStruct((RING, 128, 1024), BF),
        in_specs=[vmem] * 3,
        out_specs=vmem,
        scratch_shapes=[
            pltpu.VMEM((RING, 4, 432, LANES), BF),
            pltpu.VMEM((RING, 2, 512, LANES), BF),
            pltpu.VMEM((2, 432, LANES), F32),
            pltpu.VMEM((RING, 2, 432, LANES), BF),
            pltpu.VMEM((RING, 2, 432, LANES), BF),
            pltpu.VMEM((LANES, 512), F32),
            pltpu.VMEM((2, 432, LANES), F32),
            pltpu.VMEM((2, RING, 128, 432), BF),
            pltpu.VMEM((6, 2, 64, 256), BF),
            pltpu.VMEM((6, 2, 64, 256), BF),
            pltpu.VMEM((2, 2, 64, 256), F32),
            pltpu.VMEM((2, 128, 256), F32),
            pltpu.VMEM((128, 256), BF),
            pltpu.VMEM((128, 256), BF),
            pltpu.VMEM((4, 2, 128, 384), F32),
            pltpu.VMEM((6, 1, 64, 384), BF),
            pltpu.VMEM((6, 1, 64, 384), BF),
            pltpu.VMEM((2, 1, 64, 384), F32),
            pltpu.VMEM((1, 128, 384), F32),
            pltpu.VMEM((4, 128, 384), BF),
            pltpu.VMEM((4, 128, 384), BF),
            pltpu.VMEM((RING, 128, LANES), BF),
            pltpu.VMEM((RING, 128, LANES), BF),
            pltpu.VMEM((RING, RING, 128, LANES), BF),
            pltpu.SemaphoreType.DMA((copies,)),
            pltpu.SemaphoreType.DMA((copies,)),
            pltpu.SemaphoreType.DMA((RING,)),
        ],
        compiler_params=pltpu.CompilerParams(
            collective_id=0, has_side_effects=True, vmem_limit_bytes=48 * 2**20
        ),
        cost_estimate=pl.CostEstimate(flops=2_700_000_000, bytes_accessed=3_000_000, transcendentals=0),
    )(half_slabs, virtuals.T, weight)
    return gram.reshape(1024, 1024).astype(F32)


def solution(mesh):
    placed = (P(None, "depth", ("row", "col")), P("col", "depth"), P(), P("depth"), P())
    return jax.shard_map(
        on_device, mesh=mesh, in_specs=placed, out_specs=P("row", "col"), check_vma=False
    )
```

```python
import jax
import jax.numpy as jnp
from jax import lax
from jax.experimental import pallas as pl
from jax.experimental.pallas import tpu as pltpu
from jax.sharding import PartitionSpec as P

MESH = pl.DeviceIdType.MESH
BF = jnp.bfloat16
F32 = jnp.float32
RING = 8
LANES = 128


class Links:
    def __init__(self, here, send_sems, recv_sems):
        self.here, self.send_sems, self.recv_sems = here, send_sems, recv_sems
        self.copies, self.retired = [], 0

    def place(self, **target):
        at = {**self.here, **target}
        return at["depth"], at["row"], at["col"]

    def plan(self, src, dst, recv_sem=None, **target):
        at = len(self.copies)
        copy = pltpu.make_async_remote_copy(
            src_ref=src,
            dst_ref=dst,
            send_sem=self.send_sems.at[at],
            recv_sem=self.recv_sems.at[at] if recv_sem is None else recv_sem,
            device_id=self.place(**target),
            device_id_type=MESH,
        )
        self.copies.append(copy)
        return copy

    def send(self, src, dst, **target):
        copy = self.plan(src, dst, **target)
        copy.start()
        return copy

    def retire(self, upto=None):
        for copy in self.copies[self.retired : upto]:
            copy.wait_send()
        self.retired = len(self.copies) if upto is None else upto


def around(me):
    up, down, far = lax.rem(me + 2, RING), lax.rem(me + 6, RING), lax.rem(me + 4, RING)
    return up, down, far, me + 1 - 2 * lax.rem(me, 2)


def other(at):
    return at + 1 - 2 * lax.rem(at, 2)


def gather_kernel(
    slabs_ref, virt_ref, weight_ref, out_ref,
    vq, hs, acc, rp, qp, wrow, wcol, wl,
    a_raw, a_land, a_keep, a_own, a_sib, a_last,
    b_terms, b_raw, b_land, b_keep, b_own, b_give, b_take, red, tile_land, parts,
    send_sems, recv_sems, tile_sems,
):
    d, r, c = lax.axis_index("depth"), lax.axis_index("row"), lax.axis_index("col")
    d_up, d_down, d_far, d_sib = around(d)
    c_up, c_down, c_far, c_sib = around(c)
    r_up, r_down = lax.rem(r + 1, RING), lax.rem(r + 7, RING)
    links = Links({"depth": d, "row": r, "col": c}, send_sems, recv_sems)
    send = links.send

    barrier = pltpu.get_barrier_semaphore()
    c_far_sib, c_up_sib, c_down_sib = other(c_far), other(c_up), other(c_down)
    partners = [links.place(depth=to) for to in (d_up, d_down, d_sib)]
    partners += [links.place(row=to) for to in (r_up, r_down)]
    partners += [links.place(col=to) for to in (c_up, c_down, c_far, c_sib, c_up_sib, c_down_sib, c_far_sib)]
    for partner in partners:
        pl.semaphore_signal(barrier, inc=1, device_id=partner, device_id_type=MESH)
    apart = lax.rem(c - r + RING, RING)
    turned = jnp.logical_or(jnp.logical_or(apart == 3, apart == 6), apart == 7)

    @pl.when(turned)
    def _():
        for n in range(RING):
            pl.semaphore_signal(barrier, inc=1, device_id=links.place(row=c, col=n), device_id_type=MESH)

    nvir, nbas = virt_ref.shape
    vq[c, 3] = jnp.zeros((nvir, LANES), BF)
    for quarter in range(3):
        vq[c, quarter] = virt_ref[:, LANES * quarter : LANES * quarter + LANES]
    vq[c, 3, :, 0 : nbas - 384] = virt_ref[:, 384:nbas]
    for orbital in range(2):
        hs[d, orbital, 496:512, :] = jnp.zeros((16, LANES), BF)
        hs[d, orbital, 0:nbas, :] = slabs_ref[orbital]

    pl.semaphore_wait(barrier, len(partners) + 3)

    j = lax.rem(r, 4)
    j_up, j_down = lax.rem(j + 1, 4), lax.rem(j + 3, 4)
    spans = (pl.ds(0, 208), pl.ds(208, 224))

    def slab(n, orbital, half=None, **target):
        piece = hs.at[n, orbital] if half is None else hs.at[n, orbital, pl.ds(256 * half, 256)]
        return send(piece, piece, **target)

    def virt(n, quarter, half=None, **target):
        piece = vq.at[n, quarter] if half is None else vq.at[n, quarter, spans[half]]
        return send(piece, piece, **target)

    def virt_rows(n):
        return virt(n, j, row=r_up), virt(n, j, row=r_down)

    pair, up, down, up2, down2, up3, down3, up4, down4 = ({} for _ in range(9))

    def slabs_out(o):
        up[o], down[o] = slab(d, o, depth=d_up), slab(d, o, depth=d_down)

    def slabs_sib(o):
        pair[o].wait_recv()
        up2[o], down2[o] = slab(d_sib, o, depth=d_up), slab(d_sib, o, depth=d_down)

    def slabs_on(o):
        up[o].wait_recv()
        up3[o] = slab(d_down, o, 1, depth=d_up)
        down[o].wait_recv()
        down3[o] = slab(d_up, o, 0, depth=d_down)

    def slabs_sib_on(o):
        up2[o].wait_recv()
        up4[o] = slab(other(d_down), o, 1, depth=d_up)
        down2[o].wait_recv()
        down4[o] = slab(other(d_up), o, 0, depth=d_down)

    def slabs_end(o):
        for copy in (up3[o], down3[o], up4[o], down4[o]):
            copy.wait_recv()

    z_up = virt(c, j, col=c_up)
    z_down = virt(c, j, col=c_down)
    slabs_out(0)
    pair[0] = slab(d, 0, depth=d_sib)
    share_virt = send(vq.at[c], vq.at[c], col=c_sib)
    slabs_out(1)

    z_up.wait_recv()
    z_up2 = virt(c_down, j, 1, col=c_up)
    rows_a = virt_rows(c_down)
    z_down.wait_recv()
    z_down2 = virt(c_up, j, 0, col=c_down)
    rows_b = virt_rows(c_up)
    slabs_sib(0)
    slabs_on(0)
    z_up2.wait_recv()
    z_down2.wait_recv()
    rows_c = virt_rows(c_far)
    pair[1] = slab(d, 1, depth=d_sib)

    def pass_rows(n, rows):
        rows[0].wait_recv()
        if n is c_down:
            one = (virt(n, j_down, row=r_up),)
        elif n is c_far:
            one = (virt(n, j_down, 1, row=r_up),)
        else:
            one = ()
        rows[1].wait_recv()
        if n is c_up:
            one += (virt(n, j_up, row=r_down),)
        elif n is c_far:
            one += (virt(n, j_up, 0, row=r_down),)
        return one

    on_a = pass_rows(c_down, rows_a)
    on_b = pass_rows(c_up, rows_b)
    slabs_sib_on(0)
    on_c = pass_rows(c_far, rows_c)
    slabs_sib(1)
    slabs_on(1)

    wrow[...] = jnp.zeros_like(wrow)
    for orbital in range(2):
        wrow[:, 0:nvir] = jnp.broadcast_to(weight_ref[orbital : orbital + 1, :], (LANES, nvir))
        wcol[orbital] = wrow[...].T[0:nvir, :]
    acc[...] = jnp.zeros_like(acc)

    def virt_end(n, on):
        for copy in on:
            copy.wait_recv()
        return send(vq.at[n], vq.at[n], col=c_sib)

    def couple(n, orbital):
        left = jnp.concatenate([vq[n, 0], vq[n, 1], vq[n, 2], vq[n, 3]], axis=1)
        acc[orbital] += jnp.dot(left, hs[n, orbital], preferred_element_type=F32)

    share_a = virt_end(c_down, on_a)
    share_b = virt_end(c_up, on_b)
    slabs_end(0)
    couple(c, 0)
    share_virt.wait_recv()
    couple(c_sib, 0)
    couple(c_down, 0)
    couple(c_up, 0)
    share_c = virt_end(c_far, on_c)
    slabs_sib_on(1)
    share_a.wait_recv()
    couple(other(c_down), 0)
    share_b.wait_recv()
    couple(other(c_up), 0)
    couple(c_far, 0)
    share_c.wait_recv()
    couple(other(c_far), 0)

    def panel(n, orbital, **target):
        return send(rp.at[n, orbital], rp.at[n, orbital], **target)

    y_up, y_down, z_up, z_down = {}, {}, {}, {}
    share = {}

    def whole(n):
        return send(rp.at[n], rp.at[n], col=c_sib)

    def panels_out(o):
        rp[c, o] = acc[o].astype(BF)
        y_up[1, o] = send(rp.at[c, o], qp.at[1, o], row=r_up)
        y_down[1, o] = send(rp.at[c, o], qp.at[2, o], row=r_down)
        z_up[o] = panel(c, o, col=c_up)
        z_down[o] = panel(c, o, col=c_down)
        qp[0, o] = rp[c, o]

    def y_step(step, o):
        slot = 2 * step - 1
        y_up[step, o].wait_recv()
        y_up[step + 1, o] = send(qp.at[slot, o], qp.at[slot + 2, o], row=r_up)
        y_down[step, o].wait_recv()
        if step == 2 and o == 1:
            return
        y_down[step + 1, o] = send(qp.at[slot + 1, o], qp.at[slot + 3, o], row=r_down)

    def weigh(n, o):
        product = wcol[o] * rp[n, o].astype(F32)
        wl[o, n] = product.astype(BF).T

    panels_out(0)
    slabs_end(1)

    @pl.loop(0, RING)
    def _(n):
        couple(n, 1)

    panels_out(1)
    first_stage = len(links.copies)
    y_step(1, 1)
    z_down[0].wait_recv()
    z_down["far"] = panel(c_up, 0, col=c_down)
    share["own"] = whole(c)
    y_step(1, 0)
    z_up[1].wait_recv()
    z_up["far"] = panel(c_down, 1, col=c_up)
    z_up[0].wait_recv()
    weigh(c, 1)
    z_down[1].wait_recv()
    weigh(c_up, 0)
    weigh(c_down, 0)
    links.retire(24)
    links.retire(40)
    share["down"] = whole(c_down)
    share["own"].wait_recv()
    weigh(c_sib, 0)
    weigh(c, 0)
    y_step(2, 1)
    y_step(2, 0)
    weigh(c_sib, 1)
    z_down["far"].wait_recv()
    weigh(c_down, 1)
    share["down"].wait_recv()
    share["up"] = whole(c_up)
    weigh(c_down_sib, 1)
    weigh(c_far, 0)
    z_up["far"].wait_recv()
    share["far"] = whole(c_far)
    weigh(c_down_sib, 0)
    weigh(c_far, 1)
    weigh(c_up, 1)
    y_up[3, 1].wait_recv()
    y_up[4, 1] = send(qp.at[5, 1], qp.at[7, 1], row=r_up)
    y_down[3, 0].wait_recv()
    y_down[4, 0] = send(qp.at[6, 0], qp.at[7, 0], row=r_down)
    share["up"].wait_recv()
    weigh(c_up_sib, 0)
    share["far"].wait_recv()
    weigh(c_far_sib, 0)
    weigh(c_up_sib, 1)
    weigh(c_far_sib, 1)

    low, high = slice(0, 64), slice(64, 128)
    targets = {"far": d_far, "up": d_up, "down": d_down, "own": d}

    def terms_of(name, slots):
        terms = 0.0
        for o in range(2):
            rows = wl[o, pl.ds(2 * (targets[name] // 2), 2)].reshape(256, 432)
            columns = jnp.concatenate([qp[slot, o] for slot in slots], axis=1)
            terms += jnp.dot(rows, columns, preferred_element_type=F32)
        return terms.reshape(2, 128, LANES * len(slots))

    class RingSum:
        def __init__(self, raw, land, keep, own):
            self.raw, self.land, self.keep, self.own, self.copies = raw, land, keep, own, {}

        def send(self, at, value, **target):
            self.raw[at] = value.astype(BF)
            self.copies[at] = send(self.raw.at[at], self.land.at[at], **target)

        def give(self, name, block):
            if name == "far":
                self.send(0, block[:, high], depth=d_up)
                self.send(1, block[:, low], depth=d_down)
            elif name == "up":
                self.send(2, block[:, low], depth=d_up)
                self.keep[0] = block[:, high]
            elif name == "down":
                self.send(3, block[:, high], depth=d_down)
                self.keep[1] = block[:, low]
            else:
                self.own[...] = block

        def pass_on(self, at):
            self.copies[at].wait_recv()
            self.send(at + 4, self.keep[at] + self.land[at].astype(F32), depth=(d_up, d_down)[at])

        def end(self):
            for at in (2, 3, 4, 5):
                self.copies[at].wait_recv()
            land = self.land
            self.own[:, low] = self.own[:, low] + land[2].astype(F32) + land[5].astype(F32)
            self.own[:, high] = self.own[:, high] + land[3].astype(F32) + land[4].astype(F32)

    plane = lax.rem(d, 2)
    slots_a, slots_b = (0, 2, 4), (5, 7)
    ring_a = RingSum(a_raw, a_land, a_keep, a_own)
    ring_b = RingSum(b_raw, b_land, b_keep, b_own)
    b_pair = {}
    def gram_b(at, name):
        b_terms[at] = terms_of(name, slots_b)
        b_give[at] = b_terms[at, 1 - plane].astype(BF)
        b_pair[name] = send(b_give.at[at], b_take.at[at], depth=d_sib)

    def pair_b(at, name):
        b_pair[name].wait_recv()
        ring_b.give(name, (b_terms[at, plane] + b_take[at].astype(F32))[None])

    rows_of = {0: r, 2: r_up, 4: lax.rem(r + 2, RING), 5: lax.rem(r + 5, RING), 7: lax.rem(r + 4, RING)}
    mine = tile_sems.at[c]

    def tiles_out(slots, total):
        for at, slot in enumerate(slots):
            red[slot] = total[:, LANES * at : LANES * at + LANES]
        for slot in slots:
            to = rows_of[slot]
            if slot in (2, 4, 5):
                links.plan(red.at[slot], tile_land.at[c], recv_sem=mine, row=to, col=r).start()
        for slot in slots:
            to = rows_of[slot]
            copy = links.plan(red.at[slot], tile_land.at[c], recv_sem=mine, col=to)
            straight[slot] = to, copy
            pl.when(to != c)(copy.start)

    straight = {}

    ring_a.give("far", terms_of("far", slots_a))
    ring_a.give("down", terms_of("down", slots_a))
    ring_a.give("own", terms_of("own", slots_a))
    y_up[3, 0].wait_recv()
    y_up[4, 1].wait_recv()
    y_down[4, 0].wait_recv()
    gram_b(1, "up")
    ring_a.give("up", terms_of("up", slots_a))
    gram_b(0, "far")
    ring_a.pass_on(1)
    ring_a.pass_on(0)
    gram_b(2, "down")
    gram_b(3, "own")
    pair_b(0, "far")
    pair_b(2, "down")
    pair_b(1, "up")
    ring_a.end()
    a_sib[...] = a_own[1 - plane].astype(BF)
    last = send(a_sib, a_last, depth=d_sib)
    ring_b.pass_on(1)
    ring_b.pass_on(0)
    links.retire(first_stage)
    pair_b(3, "own")
    ring_b.end()
    tiles_out(slots_b, b_own[0].astype(BF))
    last.wait_recv()
    tiles_out(slots_a, (a_own[plane] + a_last[...].astype(F32)).astype(BF))

    before = len(links.copies) - 8
    links.retire(before)
    for slot, (to, _) in straight.items():

        @pl.when(to == c)
        def _(slot=slot):
            tile_land[c] = red[slot]

    def columns_of(place):
        pair_at = lax.rem(c // 2 + place, 4)
        return [(2 * place + core, 2 * pair_at + core) for core in range(2)]

    def tiles_in(places):
        for place in places:
            for at, n in columns_of(place):

                @pl.when(jnp.logical_or(turned, c != n))
                def _(n=n):
                    pltpu.make_async_remote_copy(
                        src_ref=red.at[0],
                        dst_ref=tile_land.at[n],
                        send_sem=send_sems.at[before],
                        recv_sem=tile_sems.at[n],
                        device_id=links.place(col=c_sib),
                        device_id_type=MESH,
                    ).wait_recv()

                @pl.when(turned)
                def _(at=at, n=n):
                    parts[d, at] = tile_land[n].T

                @pl.when(jnp.logical_not(turned))
                def _(at=at, n=n):
                    parts[d, at] = tile_land[n]

    def pass_on(n, begin, size, **target):
        piece = parts.at[n, pl.ds(begin, size)]
        return send(piece, piece, **target)

    def settle(n):
        targets_of = [pair for place in range(4) for pair in columns_of(place)]

        @pl.when(turned)
        def _():
            for at, m in targets_of:
                out_ref[m, :, pl.ds(pl.multiple_of(LANES * n, LANES), LANES)] = parts[n, at]

        @pl.when(jnp.logical_not(turned))
        def _():
            for at, m in targets_of:
                out_ref[n, :, pl.ds(pl.multiple_of(LANES * m, LANES), LANES)] = parts[n, at]

    first_gather = len(links.copies)
    tiles_in((0, 1))
    pair = pass_on(d, 0, 4, depth=d_sib)
    a_up = pass_on(d, 0, 4, depth=d_up)
    a_down = pass_on(d, 0, 4, depth=d_down)
    tiles_in((3, 2))
    b_up = pass_on(d, 4, 4, depth=d_up)
    b_down = pass_on(d, 4, 4, depth=d_down)
    b_pairs = [pass_on(d, 4, 4, depth=d_sib)]
    for slot, (to, copy) in straight.items():
        pl.when(to != c)(copy.wait_send)
    for at in range(before, first_gather):
        if all(links.copies[at] is not copy for _, copy in straight.values()):
            links.copies[at].wait_send()
    links.retired = first_gather
    settle(d)
    pair.wait_recv()
    a_up2 = pass_on(d_sib, 0, 4, depth=d_up)
    a_down2 = pass_on(d_sib, 0, 4, depth=d_down)
    b_up.wait_recv()
    b_up2 = pass_on(d_down, 6, 2, depth=d_up)
    b_pairs.append(pass_on(d_down, 4, 4, depth=d_sib))
    b_down.wait_recv()
    b_down2 = pass_on(d_up, 4, 2, depth=d_down)
    b_pairs.append(pass_on(d_up, 4, 4, depth=d_sib))
    a_up.wait_recv()
    a_up3 = pass_on(d_down, 2, 2, depth=d_up)
    a_down.wait_recv()
    a_down3 = pass_on(d_up, 0, 2, depth=d_down)
    settle(d_up)
    settle(d_down)
    b_up2.wait_recv()
    b_pairs.append(pass_on(d_far, 6, 2, depth=d_sib))
    b_down2.wait_recv()
    b_pairs.append(pass_on(d_far, 4, 2, depth=d_sib))
    a_up2.wait_recv()
    a_up4 = pass_on(other(d_down), 2, 2, depth=d_up)
    a_down2.wait_recv()
    a_down4 = pass_on(other(d_up), 0, 2, depth=d_down)
    links.retire(len(links.copies) - 6)
    b_pairs[0].wait_recv()
    settle(d_sib)
    a_up3.wait_recv()
    a_down3.wait_recv()
    settle(d_far)
    b_pairs[1].wait_recv()
    settle(other(d_down))
    b_pairs[2].wait_recv()
    settle(other(d_up))
    for copy in (a_up4, a_down4, *b_pairs[3:]):
        copy.wait_recv()
    settle(other(d_far))
    links.retire()


def on_device(half_slabs, virtuals, occupied_energy, virtual_energy, frequency):
    vmem = pl.BlockSpec(memory_space=pltpu.VMEM)
    excitation = virtual_energy[None, :] - occupied_energy[:, None]
    weight = 4.0 * excitation / (excitation * excitation + frequency[0] * frequency[0])
    copies = 128
    gram = pl.pallas_call(
        gather_kernel,
        out_shape=jax.ShapeDtypeStruct((RING, 128, 1024), BF),
        in_specs=[vmem] * 3,
        out_specs=vmem,
        scratch_shapes=[
            pltpu.VMEM((RING, 4, 432, LANES), BF),
            pltpu.VMEM((RING, 2, 512, LANES), BF),
            pltpu.VMEM((2, 432, LANES), F32),
            pltpu.VMEM((RING, 2, 432, LANES), BF),
            pltpu.VMEM((RING, 2, 432, LANES), BF),
            pltpu.VMEM((LANES, 512), F32),
            pltpu.VMEM((2, 432, LANES), F32),
            pltpu.VMEM((2, RING, 128, 432), BF),
            pltpu.VMEM((6, 2, 64, 384), BF),
            pltpu.VMEM((6, 2, 64, 384), BF),
            pltpu.VMEM((2, 2, 64, 384), F32),
            pltpu.VMEM((2, 128, 384), F32),
            pltpu.VMEM((128, 384), BF),
            pltpu.VMEM((128, 384), BF),
            pltpu.VMEM((4, 2, 128, 256), F32),
            pltpu.VMEM((6, 1, 64, 256), BF),
            pltpu.VMEM((6, 1, 64, 256), BF),
            pltpu.VMEM((2, 1, 64, 256), F32),
            pltpu.VMEM((1, 128, 256), F32),
            pltpu.VMEM((4, 128, 256), BF),
            pltpu.VMEM((4, 128, 256), BF),
            pltpu.VMEM((RING, 128, LANES), BF),
            pltpu.VMEM((RING, 128, LANES), BF),
            pltpu.VMEM((RING, RING, 128, LANES), BF),
            pltpu.SemaphoreType.DMA((copies,)),
            pltpu.SemaphoreType.DMA((copies,)),
            pltpu.SemaphoreType.DMA((RING,)),
        ],
        compiler_params=pltpu.CompilerParams(
            collective_id=0, has_side_effects=True, vmem_limit_bytes=48 * 2**20
        ),
        cost_estimate=pl.CostEstimate(flops=2_700_000_000, bytes_accessed=3_000_000, transcendentals=0),
    )(half_slabs, virtuals.T, weight)
    return gram.reshape(1024, 1024).astype(F32)


def solution(mesh):
    placed = (P(None, "depth", ("row", "col")), P("col", "depth"), P(), P("depth"), P())
    return jax.shard_map(
        on_device, mesh=mesh, in_specs=placed, out_specs=P("row", "col"), check_vma=False
    )
```
